128 devices in a mesh: pipe: 2 (over core), expert: 16 (over x, y), tensor: 4 (over z).
Axes of the slice: x: 4, y: 4, z: 4, core: 2. Of those that a mesh axis runs over, the one named last changes fastest.
Arguments:
- block_input: bfloat16 [2, 2048, 768], P(None, 'expert'), may hold values from -6 to 6
- cotangent: bfloat16 [2, 2048, 768], P(None, 'expert'), may hold values from -6 to 6
- routes: int32 [2, 2, 2048, 2], P('pipe', None, 'expert'), may hold values from 0 to 31, all different within a row; in each aligned block of 128 rows (0 to 127, 128 to 255, ..., all dimensions but the last counted through in order) at most 8 rows name the same one
- offset_bucket: int32 [128], replicated, may hold values from 0 to 31
- norm1_gain: float32 [2, 768], P('pipe'), may hold values from 0.5 to 1.5
- qkv_weight: bfloat16 [2, 3, 768, 768], P('pipe', None, None, 'tensor'), may hold values from -0.21875 to 0.21875
- out_weight: bfloat16 [2, 768, 768], P('pipe', 'tensor'), may hold values from -0.875 to 0.875
- bias_table: float32 [2, 12, 32], P('pipe', 'tensor'), may hold values from -4 to 4
- norm2_gain: float32 [2, 768], P('pipe'), may hold values from 0.5 to 1.5
- router_weight: float32 [2, 768, 32], P('pipe'), may hold values from -0.3125 to 0.3125
- up_weight: bfloat16 [2, 32, 768, 3072], P('pipe', 'expert', None, 'tensor'), may hold values from -0.21875 to 0.21875
- down_weight: bfloat16 [2, 32, 3072, 768], P('pipe', 'expert', 'tensor'), may hold values from -0.109375 to 0.109375
Outputs:
- section_ends: float32 [2, 2, 2048, 768], P('pipe', None, 'expert')
- grad_norm1: float32 [2, 768], P('pipe')
- grad_qkv: float32 [2, 3, 768, 768], P('pipe', None, None, 'tensor')
- grad_out: float32 [2, 768, 768], P('pipe', 'tensor')
- grad_bias: float32 [2, 12, 32], P('pipe', 'tensor')
- grad_norm2: float32 [2, 768], P('pipe')
- grad_router: float32 [2, 768, 32], P('pipe')
- grad_up: float32 [2, 32, 768, 3072], P('pipe', 'expert', None, 'tensor')
- grad_down: float32 [2, 32, 3072, 768], P('pipe', 'expert', 'tensor')
The draws below stay inside these ranges and needn't reach their ends.
Inputs may be any that keep to these rules, and one draw needn't show every extreme that they name: For each layer, micro-batch and sequence of 128 tokens, no expert is named by more than 8 routes, a bound that some block reaches. A token's two experts differ.
All inputs are finite; a program needn't handle non-finite values.
Results may differ from the reference program's by a relative error of at most 0.035.
Values may be sent and summed in bfloat16 or wider, within the bound.
A program may use at most 128 MiB of HBM per device.

```python
import math
import jax
import jax.numpy as jnp
import numpy as np
from jax import lax

D = 768
HEADS = 12
HD = 64
FF = 3072
NB = 32
TOP = 2
MB = 2
TOK_DEV = 128
EXPERTS = 32
TOKENS = 2048
CAP = 8
N_EXPERT = 16


def touch_ends(values, rng, least, high):
    extent = values.shape
    spot = [jax.random.randint(jax.random.fold_in(rng, axis), (), 0, extent[axis]) for axis in range(len(extent))]
    values = values.at[tuple(spot)].set(least)
    longest = extent.index(max(extent))
    spot[longest] = (spot[longest] + 1) % extent[longest]
    return values.at[tuple(spot)].set(high)


def block_scale(own_key, dims, shards, least, largest):
    def one(position, shards_of):
        draws = jax.random.uniform(jax.random.fold_in(jax.random.fold_in(own_key, 6), position), (shards_of,), jnp.float32, least / len(shards), largest / len(shards))
        return jnp.repeat(jnp.exp(draws), dims[position] // shards_of).reshape((-1,) + (1,) * (len(dims) - position - 1))

    factor_of = one(*shards[0])
    for cut in shards[1:]:
        factor_of = factor_of * one(*cut)
    return factor_of


def shared_out(stream_key, own, number, rows, count, top, reach, lean):
    sequence = jax.random.permutation(stream_key, count)
    crowded, common = shares(count, rows * top, reach, lean, True), shares(count, rows * top, reach, lean, False)
    places = jnp.arange(count)

    def named(tallies, turn):
        used = int((tallies > 0).sum())
        fixed = max(1, used // 4)
        shifted = fixed + (places - fixed + turn * (used - fixed)) % max(1, count - fixed)
        return jnp.zeros((count,), jnp.int32).at[sequence[jnp.where(places < fixed, places, shifted)]].set(jnp.asarray(tallies, jnp.int32))

    tallies = jnp.where(number % 4 == 0, named(crowded, number // 4), named(common, number - number // 4 - 1))
    mixed = jax.random.permutation(jax.random.fold_in(own, 3), count)
    giver, receiver = mixed[0:count // 2 * 2:2], mixed[1:count // 2 * 2:2]
    slack = jnp.minimum(tallies[giver] - 1, reach - tallies[receiver]) // 2
    slack = jnp.where((giver == sequence[0]) | (receiver == sequence[0]) | (tallies[receiver] == 0), 0, jnp.maximum(slack, 0))
    shifted = jax.random.randint(jax.random.fold_in(own, 4), (count // 2,), 0, 1 << 20) % (slack + 1)
    tallies = tallies.at[giver].add(-shifted).at[receiver].add(shifted)
    labels = jnp.searchsorted(jnp.cumsum(tallies), jnp.arange(rows * top), side="right").astype(jnp.int32)
    table = labels.reshape(top, rows).T
    table = table[jax.random.permutation(jax.random.fold_in(own, 1), rows)]
    turn = jax.random.randint(jax.random.fold_in(own, 2), (rows, 1), 0, top)
    return jnp.take_along_axis(table, (jnp.arange(top)[None, :] + turn) % top, axis=1)


def shares(amount, total, most, lean, full):
    weights = [(1 << 20) // math.isqrt(rank ** lean) + 1 for rank in range(1, amount + 1)]
    largest = most if full else min(most, max(-(-total // amount), total * weights[0] // sum(weights)))
    least = 1 if total - largest >= amount - 1 else 0
    counts, spare = [largest] + [least] * (amount - 1), total - largest - least * (amount - 1)
    while spare > 0:
        candidates = [i for i in range(1, amount) if counts[i] < largest] or [i for i in range(1, amount) if counts[i] < most]
        mass, remaining = sum([weights[i] for i in candidates]), spare
        for i in candidates:
            more = min(most - counts[i], max(1, remaining * weights[i] // mass), spare)
            counts[i] = counts[i] + more
            spare = spare - more
    return np.array(counts)


def bell_draw(rng, shape, spread, bound, cuts=(), kind=jnp.bfloat16):
    drawn = spread * jax.random.normal(rng, shape, jnp.float32)
    if cuts:
        drawn = drawn * block_scale(rng, shape, cuts, -0.22, 0.18)
    return jnp.clip(drawn, -bound, bound).astype(kind)


def setup_inputs(seed: int = 0) -> dict:
    key_list = jax.random.split(jax.random.key(seed), 13)
    block_input = bell_draw(key_list[0], (MB, TOKENS, D), 1.0, 6.0, ((1, 16),))
    cotangent = bell_draw(key_list[1], (MB, TOKENS, D), 1.0, 6.0, ((1, 16),))
    routes_keys = jax.random.split(jax.random.fold_in(key_list[2], 1), 2 * MB * TOKENS // TOK_DEV)
    routes_turns = jax.random.permutation(jax.random.fold_in(key_list[2], 3), 2 * MB * TOKENS // TOK_DEV)
    routes = jax.vmap(lambda own, number: shared_out(jax.random.fold_in(key_list[2], 2), own, number, TOK_DEV, EXPERTS, TOP, CAP, 0))(routes_keys, routes_turns).reshape((2, MB, TOKENS, TOP))
    offset_bucket = touch_ends(jax.random.randint(key_list[3], (TOK_DEV,), 0, NB), jax.random.fold_in(key_list[3], 1), 0, NB - 1).astype(jnp.int32)
    norm1_gain = jnp.clip(1.0 + 0.1 * jax.random.normal(key_list[4], (2, D), jnp.float32), 0.5, 1.5)
    qkv_weight = bell_draw(key_list[5], (2, 3, D, HEADS * HD), D ** -0.5, 0.21875, ((0, 2), (3, 4)))
    out_weight = bell_draw(key_list[6], (2, HEADS * HD, D), (HEADS * HD // 16) ** -0.5, 0.875, ((0, 2), (1, 4)))
    bias_table = bell_draw(key_list[7], (2, HEADS, NB), 1.0, 4.0, ((0, 2), (1, 4)), jnp.float32)
    norm2_gain = jnp.clip(1.0 + 0.1 * jax.random.normal(key_list[8], (2, D), jnp.float32), 0.5, 1.5)
    router_weight = bell_draw(key_list[9], (2, D, EXPERTS), (D // 2) ** -0.5, 0.3125, ((0, 2),), jnp.float32)
    up_weight = bell_draw(key_list[10], (2, EXPERTS, D, FF), D ** -0.5, 0.21875, ((0, 2), (1, 16), (3, 4)))
    down_weight = bell_draw(key_list[11], (2, EXPERTS, FF, D), FF ** -0.5, 0.109375, ((0, 2), (1, 16), (2, 4)))
    return {"block_input": block_input, "cotangent": cotangent, "routes": routes, "offset_bucket": offset_bucket, "norm1_gain": norm1_gain, "qkv_weight": qkv_weight, "out_weight": out_weight, "bias_table": bias_table, "norm2_gain": norm2_gain, "router_weight": router_weight, "up_weight": up_weight, "down_weight": down_weight}


EPS = 1e-06
MASKED = -1e+30

@jax.custom_vjp
def low(v):
    return lax.optimization_barrier(v.astype(jnp.bfloat16)).astype(jnp.float32)

@jax.custom_vjp
def low_back(v):
    return v

def low_keep(v):
    return (low(v), None)

def low_pass(kept, grad):
    return (grad,)

def back_keep(v):
    return (v, None)

def back_low(kept, grad):
    return (low(grad),)
low.defvjp(low_keep, low_pass)
low_back.defvjp(back_keep, back_low)

def rms_norm(values, gain_vec):
    return values * lax.rsqrt(lax.optimization_barrier(jnp.mean(values * values, -1, keepdims=True)) + EPS) * gain_vec

def gelu_tanh(values):
    return jax.nn.gelu(values, approximate=True)

def slot_rows(route_now, expert_total, capacity):
    flat_ids = route_now.reshape(-1).astype(jnp.int32)
    one_hot = (flat_ids[:, None] == jnp.arange(expert_total, dtype=jnp.int32)[None, :]).astype(jnp.int32)
    before = jnp.cumsum(one_hot, 0) - one_hot
    return (flat_ids * capacity + lax.optimization_barrier(jnp.sum(before * one_hot, 1))).astype(jnp.int32)

def route_table(route_now, expert_total):
    return (route_now[:, :, None] == jnp.arange(expert_total, dtype=jnp.int32)[None, None, :]).astype(jnp.float32)

def gate_of(normed, router, route_hot):
    logits = jnp.dot(normed, router, precision=lax.Precision.HIGHEST)
    expert_probs = jax.nn.softmax(logits, -1)
    chosen = lax.optimization_barrier(jnp.sum(expert_probs[:, None, :] * route_hot, -1))
    return chosen / lax.optimization_barrier(jnp.sum(chosen, -1, keepdims=True))

def layer(h_in, route_now, params, offset_bucket):
    gain_one, w_qkv, w_out, bias_rows, gain_two, router, w_up, w_down = params
    token_count = h_in.shape[0]
    n_one = low(rms_norm(h_in, gain_one))
    qkv_rows = low(low_back(jnp.einsum('td,cdf->ctf', n_one, w_qkv, precision=lax.Precision.HIGHEST)))
    head_parts = qkv_rows.reshape(3, N_EXPERT, TOK_DEV, HEADS, HD).transpose(1, 0, 3, 2, 4)
    positions = jnp.arange(TOK_DEV, dtype=jnp.int32)
    offsets = jnp.clip(positions[:, None] - positions[None, :], 0, TOK_DEV - 1).astype(jnp.int32)
    causal = positions[:, None] >= positions[None, :]
    rel_bias = bias_rows[:, offset_bucket[offsets]]

    def one_sequence(seq_parts):
        raw_scores = jnp.einsum('hqd,hkd->hqk', seq_parts[0], seq_parts[1], precision=lax.Precision.HIGHEST) * HD ** (-0.5) + rel_bias
        scores = jnp.where(causal[None], low_back(raw_scores), MASKED)
        attn_probs = low(jax.nn.softmax(scores, -1))
        return jnp.einsum('hqk,hkd->hqd', attn_probs, seq_parts[2], precision=lax.Precision.HIGHEST)
    mixed_heads = lax.map(jax.checkpoint(one_sequence), head_parts)
    mixed_heads = low(low_back(mixed_heads.transpose(0, 2, 1, 3).reshape(token_count, HEADS * HD)))
    h_mid = h_in + low_back(jnp.dot(mixed_heads, w_out, precision=lax.Precision.HIGHEST))
    n_two = low(rms_norm(h_mid, gain_two))
    route_hot = route_table(route_now, EXPERTS)
    gate_values = gate_of(n_two, router, route_hot)
    slot_dest = jax.vmap(lambda block_routes: slot_rows(block_routes, EXPERTS, CAP))(route_now.reshape(N_EXPERT, TOK_DEV, TOP))
    buffers = jax.vmap(lambda row_values, slot_index: jnp.zeros((EXPERTS * CAP, D), jnp.float32).at[slot_index].set(jnp.repeat(row_values, TOP, 0)))(n_two.reshape(N_EXPERT, TOK_DEV, D), slot_dest)
    buffers = low_back(buffers.reshape(N_EXPERT, EXPERTS, CAP, D))
    lifted = low_back(jnp.einsum('secd,edf->secf', buffers, w_up, precision=lax.Precision.HIGHEST))
    hidden = low(gelu_tanh(lifted))
    outputs = low(low_back(jnp.einsum('secf,efd->secd', hidden, w_down, precision=lax.Precision.HIGHEST)))
    picked = jax.vmap(lambda row_values, slot_index: row_values[slot_index])(outputs.reshape(N_EXPERT, EXPERTS * CAP, D), slot_dest).reshape(token_count, TOP, D)
    return h_mid + lax.optimization_barrier(jnp.sum(gate_values[:, :, None] * picked, 1))

def reference(block_input, cotangent, routes, offset_bucket, norm1_gain, qkv_weight, out_weight, bias_table, norm2_gain, router_weight, up_weight, down_weight):
    params = (norm1_gain, qkv_weight.astype(jnp.float32), out_weight.astype(jnp.float32), bias_table, norm2_gain, router_weight, up_weight.astype(jnp.float32), down_weight.astype(jnp.float32))

    def forward(inputs, weights):
        first_layer = [stacked[0] for stacked in weights]
        second_layer = [stacked[1] for stacked in weights]
        results = []
        for micro_index in range(MB):
            middle = low_back(low(layer(inputs[micro_index], routes[0, micro_index], first_layer, offset_bucket)))
            results.append(layer(middle, routes[1, micro_index], second_layer, offset_bucket))
        return jnp.stack(results)
    outputs, pull_back = jax.vjp(forward, block_input.astype(jnp.float32), params)
    grad_inputs, grads = pull_back(cotangent.astype(jnp.float32))
    section_ends = jnp.stack([grad_inputs, outputs])
    return (section_ends, grads[0], grads[1], grads[2], grads[3], grads[4], grads[5], grads[6], grads[7])
```

```python
import functools

import jax
import jax.numpy as jnp
from jax import lax
from jax.experimental import pallas as pl
from jax.experimental.pallas import tpu as pltpu
from jax.sharding import PartitionSpec as P

EPS = 1e-06
MASKED = -1e30
MESH = pl.DeviceIdType.MESH
F32 = jnp.float32
BF16 = jnp.bfloat16
LANES = 128
CAP = 8
TANH_A = 0.7978845608
TANH_B = 0.044715


def dot(a, b, left, right):
    return lax.dot_general(a, b, (((left,), (right,)), ((), ())), preferred_element_type=F32)


def nn(a, b):
    return dot(a, b, 1, 0)


def nt(a, b):
    return dot(a, b, 1, 1)


def tn(a, b):
    return dot(a, b, 0, 0)


def lanes_of(shape, dim):
    return lax.broadcasted_iota(jnp.int32, shape, dim)


def kernel(
    dims,
    x_in, cot_in, routes_in, hot_in, gain_in, rel_in, router_in, qkv_in, out_in, up_in, down_in,
    sec_out, own_out, recv_out, attn_out, small_out,
    xin, cot, hot, routes, gain, rel, router, w_qkv, w_out, w_up, w_down,
    hs, n_one, qkv, probs_s, mixed_s, h_mid_s, n_two, comb, eprobs, x_s, u_s, y_s, x_dy, x_du, x_hid, g_s, fin, dqkv,
    send_a, recv_a, red_a, red_g, grads, chunk, chunk_in, small, small_in, shard, shard_small, pair, pair_small,
    total, total_small,
    sem_in, sem_w, sem_ws, sa_send, sa_recv, rd_send, rd_recv, gr_send, gr_recv, gr_loc,
    ck_send, ck_recv, sm_send, sm_recv, pr_send, pr_recv, ag_send, ag_recv, ag_loc, sec_send, sec_recv, sec_loc,
):
    ne, nz, seq, width, local, heads, ff, hd = dims
    p = lax.axis_index("pipe")
    x = lax.axis_index("expert")
    z = lax.axis_index("tensor")
    other = 1 - p
    slots = ne * 2 * CAP
    hw = heads * hd
    rows = width // ne

    barrier = pltpu.get_barrier_semaphore()

    def hello_e(r, _):
        pl.semaphore_signal(barrier, inc=1, device_id={"expert": lax.rem(x + r, ne)}, device_id_type=MESH)
        return 0

    def hello_z(r, _):
        pl.semaphore_signal(barrier, inc=1, device_id={"tensor": lax.rem(z + r, nz)}, device_id_type=MESH)
        return 0

    lax.fori_loop(1, ne, hello_e, 0)
    lax.fori_loop(1, nz, hello_z, 0)
    pl.semaphore_signal(barrier, inc=1, device_id={"pipe": other}, device_id_type=MESH)

    ins = [
        pltpu.make_async_copy(x_in.at[p], xin, sem_in.at[0]),
        pltpu.make_async_copy(cot_in.at[p], cot, sem_in.at[1]),
        pltpu.make_async_copy(hot_in, hot, sem_in.at[2]),
    ]
    for copy in ins:
        copy.start()
    weights = [
        (gain_in, gain), (qkv_in, w_qkv), (rel_in, rel), (out_in, w_out), (router_in, router), (routes_in, routes),
        (up_in, w_up), (down_in, w_down),
    ]
    for k, (src, dst) in enumerate(weights):
        pltpu.make_async_copy(src.at[p] if k == 5 else src, dst.at[p], sem_w.at[k, p]).start()
    pl.semaphore_wait(barrier, ne - 1 + nz - 1 + 1)
    outgoing = []
    for k, (src, dst) in enumerate(weights):
        copy = pltpu.make_async_remote_copy(
            src_ref=src.at[other] if k == 5 else src, dst_ref=dst.at[p], send_sem=sem_ws.at[k], recv_sem=sem_w.at[k, p],
            device_id={"pipe": other}, device_id_type=MESH)
        copy.start()
        outgoing.append(copy)

    def await_weight(k, l):
        dst = weights[k][1]
        pltpu.make_async_copy(dst.at[l], dst.at[l], sem_w.at[k, l]).wait()

    def exchange(kind, l):
        def one(r, _):
            pltpu.make_async_remote_copy(
                src_ref=send_a.at[l, kind, r], dst_ref=recv_a.at[l, kind, r],
                send_sem=sa_send.at[l, kind], recv_sem=sa_recv.at[l, kind],
                device_id={"expert": lax.rem(x + r if kind % 2 == 0 else x + ne - r, ne)}, device_id_type=MESH).start()
            return 0
        lax.fori_loop(1, ne, one, 0)
        recv_a[l, kind, 0] = send_a[l, kind, 0]

    def arrived(kind, l):
        part = send_a.at[l, kind, pl.ds(1, ne - 1)]
        pltpu.make_async_copy(part, part, sa_send.at[l, kind]).wait()
        part = recv_a.at[l, kind, pl.ds(1, ne - 1)]
        pltpu.make_async_copy(part, part, sa_recv.at[l, kind]).wait()
        return recv_a[l, kind]

    def reduce_start(buf, at, sem):
        def one(r, _):
            pltpu.make_async_remote_copy(
                src_ref=buf.at[(*at, 0)], dst_ref=buf.at[(*at, r)], send_sem=rd_send.at[sem], recv_sem=rd_recv.at[sem],
                device_id={"tensor": lax.rem(z + r, nz)}, device_id_type=MESH).start()
            return 0
        lax.fori_loop(1, nz, one, 0)

    def reduce_end(buf, at, sem):
        part = buf.at[(*at, pl.ds(1, nz - 1))]
        pltpu.make_async_copy(part, part, rd_send.at[sem]).wait()
        pltpu.make_async_copy(part, part, rd_recv.at[sem]).wait()
        acc = None
        for a in range(nz):
            term = buf[(*at, lax.rem(z + nz - a, nz))].astype(F32)
            acc = term if acc is None else acc + term
        return acc

    def split(blocks):
        wide = blocks.astype(F32)
        return [wide[:, e * CAP:(e + 1) * CAP].reshape(ne * CAP, width).astype(BF16) for e in range(local)]

    def join(parts):
        return jnp.concatenate([part.reshape(ne, CAP, width) for part in parts], axis=1).astype(BF16)

    def head_mask(h):
        at = lanes_of((1, hw), 1)
        return ((at >= h * hd) & (at < (h + 1) * hd)).astype(BF16)

    def scale_of(h):
        return lax.rsqrt(jnp.mean(h * h, -1, keepdims=True) + EPS)

    def chosen_of(l):
        ids = routes[l]
        at = lanes_of((seq, LANES), 1)
        return [(at == ids[:, k:k + 1]).astype(F32) for k in range(2)]

    def forward(l, _):
        h_in = hs[l]
        await_weight(0, l)
        n1 = (h_in * scale_of(h_in) * gain[l, 0:1]).astype(BF16)
        n_one[l] = n1
        await_weight(1, l)
        for c in range(3):
            qkv[l, c] = nn(n1, w_qkv[l, c]).astype(BF16)
        q, k, v = qkv[l, 0], qkv[l, 1], qkv[l, 2]
        await_weight(2, l)
        causal = lanes_of((seq, seq), 0) >= lanes_of((seq, seq), 1)
        mixed = jnp.zeros((seq, hw), F32)
        for h in range(heads):
            mask = head_mask(h)
            bias = pltpu.roll(jnp.broadcast_to(rel[l, h:h + 1], (seq, seq)), 0, 1, stride=1, stride_axis=0)
            s = nt(q * mask, k) * (hd ** -0.5) + bias
            s = jnp.where(causal, s, MASKED)
            e = jnp.exp(s - jnp.max(s, -1, keepdims=True))
            prob = e / jnp.sum(e, -1, keepdims=True)
            probs_s[l, h] = prob
            mixed = mixed + nn(prob.astype(BF16), v * mask)
        mixed = mixed.astype(BF16)
        mixed_s[l] = mixed
        await_weight(3, l)
        red_a[l, 0, 0] = nn(mixed, w_out[l]).astype(BF16)
        reduce_start(red_a, (l, 0), l)

        await_weight(5, l)
        ids = routes[l]
        hot_e = chosen_of(l)
        row_at, col_at = lanes_of((seq, seq), 0), lanes_of((seq, seq), 1)
        earlier = (row_at > col_at).astype(BF16)
        count = nn(earlier, (hot_e[0] + hot_e[1]).astype(BF16))
        for kk in range(2):
            before = count if kk == 0 else count + hot_e[0]
            c = jnp.sum(before * hot_e[kk], -1, keepdims=True).astype(jnp.int32)
            e = ids[:, kk:kk + 1]
            place = (((e >> 1) - x + ne) & (ne - 1)) * (2 * CAP) + (e & 1) * CAP + c
            comb[l, kk * seq:(kk + 1) * seq] = (lanes_of((seq, slots), 1) == place).astype(F32).astype(BF16)
        both = comb[l, 0:seq] + comb[l, seq:2 * seq]
        await_weight(4, l)

        h_mid = h_in + reduce_end(red_a, (l, 0), l)
        h_mid_s[l] = h_mid
        n2 = (h_mid * scale_of(h_mid) * gain[l, 1:2]).astype(BF16)
        n_two[l] = n2
        send_a[l, 0] = tn(both, n2).astype(BF16).reshape(ne, 2 * CAP, width)
        exchange(0, l)
        wide = nn(n2, router[l])
        logits = wide[:, :LANES] + wide[:, LANES:]
        logits = jnp.where(lanes_of((seq, LANES), 1) < ne * local, logits, MASKED)
        e = jnp.exp(logits - jnp.max(logits, -1, keepdims=True))
        ep = e / jnp.sum(e, -1, keepdims=True)
        eprobs[l] = ep
        picked = [jnp.sum(ep * hot_e[kk], -1, keepdims=True) for kk in range(2)]
        inv = picked[0] + picked[1]
        gates = [picked[kk] / inv for kk in range(2)]
        await_weight(6, l)
        await_weight(7, l)
        parts = split(arrived(0, l))
        for e in range(local):
            x_s[l, e] = parts[e]

        def expert(e, _):
            u = nn(x_s[l, e], w_up[l, e])
            u_s[l, e] = u
            t = jnp.tanh(TANH_A * (u + TANH_B * u * u * u))
            y_s[e] = nn((0.5 * u * (1.0 + t)).astype(BF16), w_down[l, e])
            return 0
        lax.fori_loop(0, local, expert, 0)
        send_a[l, 1] = join([y_s[e] for e in range(local)])
        exchange(1, l)
        back = arrived(1, l).reshape(slots, width)
        got = gates[0] * nn(comb[l, 0:seq], back) + gates[1] * nn(comb[l, seq:2 * seq], back)
        red_a[l, 1, 0] = got.astype(BF16)
        reduce_start(red_a, (l, 1), 2 + l)
        out = h_mid + reduce_end(red_a, (l, 1), 2 + l)
        hs[l + 1] = jnp.where(l == 0, out.astype(BF16).astype(F32), out)
        return 0

    for copy in ins:
        copy.wait()
    hs[0] = xin[...].astype(F32)
    lax.fori_loop(0, 2, forward, 0)

    def deliver(src, owner):
        @pl.when(p == owner)
        def _():
            pltpu.make_async_copy(src, sec_out.at[p], sec_loc).start()

        @pl.when(p != owner)
        def _():
            pltpu.make_async_remote_copy(
                src_ref=src, dst_ref=sec_out.at[p], send_sem=sec_send, recv_sem=sec_recv,
                device_id={"pipe": other}, device_id_type=MESH).start()

    deliver(hs.at[2], 1)
    g_s[...] = cot[...].astype(F32)

    def backward(i, _):
        l = 1 - i
        g = g_s[...]
        hot_e = chosen_of(l)
        ep = eprobs[l]
        picked = [jnp.sum(ep * hot_e[kk], -1, keepdims=True) for kk in range(2)]
        inv = picked[0] + picked[1]
        gates = [picked[kk] / inv for kk in range(2)]
        dy = jnp.concatenate([(gates[kk] * g).astype(BF16) for kk in range(2)], axis=0)
        send_a[l, 2] = tn(comb[l], dy).astype(BF16).reshape(ne, 2 * CAP, width)
        exchange(2, l)
        back = recv_a[l, 1].reshape(slots, width)
        at = lanes_of((seq, LANES), 1)
        gg = jnp.zeros((seq, LANES), F32)
        for kk in range(2):
            part = jnp.sum(g * nn(comb[l, kk * seq:(kk + 1) * seq], back), -1, keepdims=True)
            high = part.astype(BF16).astype(F32)
            gg = gg + jnp.where(at == kk, high, 0.0) + jnp.where(at == 2 + kk, part - high, 0.0)
        red_g[l, 0, :, width:] = gg.astype(BF16)
        parts = split(arrived(2, l))
        for e in range(local):
            x_dy[e] = parts[e]

        def expert(e, _):
            dy_e = x_dy[e]
            dh = nt(dy_e, w_down[l, e])
            u = u_s[l, e]
            t = jnp.tanh(TANH_A * (u + TANH_B * u * u * u))
            slope = 0.5 * (1.0 + t) + (0.5 * TANH_A) * u * (1.0 - t * t) * (1.0 + (3.0 * TANH_B) * u * u)
            du = (dh * slope).astype(BF16)
            x_du[e] = du
            x_hid[e] = (0.5 * u * (1.0 + t)).astype(BF16)
            y_s[e] = nt(du, w_up[l, e])
            return 0
        lax.fori_loop(0, local, expert, 0)
        send_a[l, 3] = join([y_s[e] for e in range(local)])
        exchange(3, l)

        def expert_grads(e, _):
            grads[l, 0, e] = tn(x_s[l, e], x_du[e]).astype(BF16)
            grads[l, 1, e] = tn(x_hid[e], x_dy[e]).astype(BF16)
            return 0
        lax.fori_loop(0, local, expert_grads, 0)

        @pl.when(p == l)
        def _():
            pltpu.make_async_copy(grads.at[l], own_out, gr_loc).start()

        @pl.when(p != l)
        def _():
            pltpu.make_async_remote_copy(
                src_ref=grads.at[l], dst_ref=recv_out, send_sem=gr_send, recv_sem=gr_recv,
                device_id={"pipe": other}, device_id_type=MESH).start()

        both = comb[l, 0:seq] + comb[l, seq:2 * seq]
        red_g[l, 0, :, :width] = nn(both, arrived(3, l).reshape(slots, width)).astype(BF16)
        reduce_start(red_g, (l,), 4 + l)
        h_mid = h_mid_s[l]
        scale = scale_of(h_mid)
        gain_two = gain[l, 1:2]
        summed = reduce_end(red_g, (l,), 4 + l)
        dn2 = summed[:, :width]
        tail = summed[:, width:]
        gg = [jnp.sum(jnp.where((at == kk) | (at == 2 + kk), tail, 0.0), -1, keepdims=True) for kk in range(2)]
        centre = gg[0] * gates[0] + gg[1] * gates[1]
        dprob = hot_e[0] * ((gg[0] - centre) / inv) + hot_e[1] * ((gg[1] - centre) / inv)
        dlog = (ep * (dprob - jnp.sum(ep * dprob, -1, keepdims=True))).astype(BF16)
        dn2 = dn2 + nt(jnp.concatenate([dlog, dlog], axis=1), router[l])
        small_g = tn(n_two[l], dlog)
        e33 = (at == 33).astype(F32).astype(BF16)
        small_g = small_g + tn((dn2 * h_mid * scale).astype(BF16), e33)
        dg = dn2 * gain_two
        dmid = g + scale * dg - h_mid * (scale * scale * scale) * jnp.mean(h_mid * dg, -1, keepdims=True)
        da = dmid.astype(BF16)
        chunk[l, :, 3] = tn(da, mixed_s[l]).astype(BF16).reshape(ne, rows, hw)
        dmixed = nt(da, w_out[l]).astype(BF16)
        q, k, v = qkv[l, 0], qkv[l, 1], qkv[l, 2]
        dq = jnp.zeros((seq, hw), F32)
        dk = jnp.zeros((seq, hw), F32)
        dv = jnp.zeros((seq, hw), F32)
        causal = lanes_of((seq, seq), 0) >= lanes_of((seq, seq), 1)
        row_at = lanes_of((seq, seq), 0)
        top = lanes_of((8, LANES), 0)
        bias_g = jnp.zeros((8, LANES), F32)
        for h in range(heads):
            mask = head_mask(h)
            prob = probs_s[l, h]
            dm = dmixed * mask
            dp = nt(dm, v)
            dv = dv + tn(prob.astype(BF16), dm)
            ds = jnp.where(causal, prob * (dp - jnp.sum(prob * dp, -1, keepdims=True)), 0.0).astype(BF16)
            dq = dq + nn(ds, k * mask)
            dk = dk + tn(ds, q * mask)
            turned = ds.astype(F32)
            bit = 1
            while bit < seq:
                turned = jnp.where((row_at & bit) != 0, pltpu.roll(turned, seq - bit, 1), turned)
                bit *= 2
            bias_g = bias_g + jnp.where(top == h, jnp.sum(turned, 0, keepdims=True), 0.0)
        dqkv[0] = (dq * (hd ** -0.5)).astype(BF16)
        dqkv[1] = (dk * (hd ** -0.5)).astype(BF16)
        dqkv[2] = dv.astype(BF16)
        dn1 = nt(dqkv[0], w_qkv[l, 0]) + nt(dqkv[1], w_qkv[l, 1]) + nt(dqkv[2], w_qkv[l, 2])
        red_a[l, 2, 0] = dn1.astype(BF16)
        reduce_start(red_a, (l, 2), 6 + l)
        n1 = n_one[l]
        for c in range(3):
            chunk[l, :, c] = tn(n1, dqkv[c]).astype(BF16).reshape(ne, rows, hw)

        def scatter(r, _):
            to = lax.rem(x + r, ne)
            pltpu.make_async_remote_copy(
                src_ref=chunk.at[l, to], dst_ref=chunk_in.at[l, r], send_sem=ck_send.at[l], recv_sem=ck_recv.at[l],
                device_id={"expert": to}, device_id_type=MESH).start()
            return 0
        lax.fori_loop(1, ne, scatter, 0)
        chunk_in[l, 0] = chunk[l, x]
        bias_high = bias_g.astype(BF16)
        bias_low = (bias_g - bias_high.astype(F32)).astype(BF16)
        bias_g = nn(bias_high, hot[...]) + nn(bias_low, hot[...])
        h_in = hs[l]
        scale_one = scale_of(h_in)
        dn1 = reduce_end(red_a, (l, 2), 6 + l)
        e32 = (at == 32).astype(F32).astype(BF16)
        small_g = small_g + tn((dn1 * h_in * scale_one).astype(BF16), e32)
        small_g = jnp.concatenate([small_g[:8] + bias_g, small_g[8:]], axis=0)
        small[l] = small_g.astype(BF16).reshape(ne, rows, LANES)

        def scatter_small(r, _):
            to = lax.rem(x + r, ne)
            pltpu.make_async_remote_copy(
                src_ref=small.at[l, to], dst_ref=small_in.at[l, r], send_sem=sm_send.at[l], recv_sem=sm_recv.at[l],
                device_id={"expert": to}, device_id_type=MESH).start()
            return 0
        lax.fori_loop(1, ne, scatter_small, 0)
        small_in[l, 0] = small[l, x]
        dg = dn1 * gain[l, 0:1]
        dh = dmid + scale_one * dg - h_in * (scale_one * scale_one * scale_one) * jnp.mean(h_in * dg, -1, keepdims=True)
        fin[...] = dh
        g_s[...] = dh.astype(BF16).astype(F32)
        return 0

    lax.fori_loop(0, 2, backward, 0)
    deliver(fin, 0)

    def settle(i, _):
        l = 1 - i
        for src, dst, send, recv, out, to, k in (
            (chunk, chunk_in, ck_send, ck_recv, shard, pair, 0),
            (small, small_in, sm_send, sm_recv, shard_small, pair_small, 1),
        ):
            part = src.at[l, pl.ds(1, ne - 1)]
            pltpu.make_async_copy(part, part, send.at[l]).wait()
            part = dst.at[l, pl.ds(1, ne - 1)]
            pltpu.make_async_copy(part, part, recv.at[l]).wait()
            acc = dst[l, 0].astype(F32)
            for r in range(1, ne):
                acc = acc + dst[l, r].astype(F32)
            out[l] = acc.astype(BF16)

            @pl.when(p != l)
            def _():
                pltpu.make_async_remote_copy(
                    src_ref=out.at[l], dst_ref=to, send_sem=pr_send.at[k], recv_sem=pr_recv.at[k],
                    device_id={"pipe": other}, device_id_type=MESH).start()
        return 0

    lax.fori_loop(0, 2, settle, 0)
    finals = ((shard, pair, total, attn_out, 0), (shard_small, pair_small, total_small, small_out, 1))
    for src, to, whole, dst, k in finals:
        pltpu.make_async_copy(to, to, pr_send.at[k]).wait()
        pltpu.make_async_copy(to, to, pr_recv.at[k]).wait()
        whole[...] = (src[p].astype(F32) + to[...].astype(F32)).astype(BF16)
        pltpu.make_async_copy(whole, dst.at[x], ag_loc.at[k]).start()

        def spread(r, _, whole=whole, dst=dst, k=k):
            pltpu.make_async_remote_copy(
                src_ref=whole, dst_ref=dst.at[x], send_sem=ag_send.at[k], recv_sem=ag_recv.at[k],
                device_id={"expert": lax.rem(x + r, ne)}, device_id_type=MESH).start()
            return 0
        lax.fori_loop(1, ne, spread, 0)

    for copy in outgoing:
        copy.wait_send()
    for sem in (gr_loc, gr_send, gr_recv):
        pltpu.make_async_copy(grads.at[0], grads.at[0], sem).wait()
    for sem in (sec_loc, sec_send, sec_recv):
        pltpu.make_async_copy(fin, fin, sem).wait()
    for src, to, whole, dst, k in finals:
        pltpu.make_async_copy(whole, whole, ag_loc.at[k]).wait()
        part = dst.at[pl.ds(0, ne - 1)]
        pltpu.make_async_copy(part, part, ag_send.at[k]).wait()
        pltpu.make_async_copy(part, part, ag_recv.at[k]).wait()


def body(
    block_input, cotangent, routes, offset_bucket, norm1_gain, qkv_weight, out_weight, bias_table, norm2_gain,
    router_weight, up_weight, down_weight,
):
    ne = lax.axis_size("expert")
    nz = lax.axis_size("tensor")
    micro, seq, width = block_input.shape
    heads, buckets = bias_table.shape[1:]
    local, _, ff = up_weight.shape[1:]
    hw = qkv_weight.shape[3]
    hd = hw // heads
    experts = router_weight.shape[2]
    rows = width // ne
    slots = ne * local * CAP

    routes_in = jnp.pad(routes[0], ((0, 0), (0, 0), (0, LANES - routes.shape[3])))
    back = jnp.roll(offset_bucket[::-1], 1)
    hot = (back[:, None] == jnp.arange(buckets, dtype=jnp.int32)[None, :]).astype(F32)
    hot_in = jnp.pad(hot, ((0, 0), (64, LANES - 64 - buckets))).astype(BF16)
    rel = jnp.sum(hot[None] * bias_table[0][:, None, :], -1)
    rel_in = jnp.pad(rel, ((0, 8 - heads), (0, 0)))
    gain_in = jnp.pad(jnp.concatenate([norm1_gain, norm2_gain], 0), ((0, 6), (0, 0)))
    high = lax.reduce_precision(router_weight[0], 8, 7)
    wide = ((0, 0), (0, LANES - experts))
    router_in = jnp.concatenate([jnp.pad(high, wide), jnp.pad(router_weight[0] - high, wide)], 1).astype(BF16)

    any_space = pl.BlockSpec(memory_space=pl.ANY)
    vm = pltpu.VMEM
    dma = pltpu.SemaphoreType.DMA
    sds = jax.ShapeDtypeStruct
    sec, own, recv, attn, small = pl.pallas_call(
        functools.partial(kernel, (ne, nz, seq, width, local, heads, ff, hd)),
        out_shape=[
            sds((micro, seq, width), F32), sds((2, local, width, ff), BF16), sds((2, local, width, ff), BF16),
            sds((ne, 4, rows, hw), BF16), sds((ne, rows, LANES), BF16),
        ],
        in_specs=[any_space] * 11,
        out_specs=[any_space] * 5,
        scratch_shapes=[
            vm((seq, width), BF16), vm((seq, width), BF16), vm((seq, LANES), BF16), vm((2, seq, LANES), jnp.int32),
            vm((2, 8, width), F32), vm((2, 8, LANES), F32), vm((2, width, 2 * LANES), BF16), vm((2, 3, width, hw), BF16),
            vm((2, hw, width), BF16), vm((2, local, width, ff), BF16), vm((2, local, ff, width), BF16),
            vm((3, seq, width), F32), vm((2, seq, width), BF16), vm((2, 3, seq, hw), BF16),
            vm((2, heads, seq, seq), F32), vm((2, seq, hw), BF16), vm((2, seq, width), F32), vm((2, seq, width), BF16),
            vm((2, 2 * seq, slots), BF16), vm((2, seq, LANES), F32), vm((2, local, ne * CAP, width), BF16),
            vm((2, local, ne * CAP, ff), F32), vm((local, ne * CAP, width), F32),
            vm((local, ne * CAP, width), BF16), vm((local, ne * CAP, ff), BF16), vm((local, ne * CAP, ff), BF16),
            vm((seq, width), F32), vm((seq, width), F32), vm((3, seq, hw), BF16),
            vm((2, 4, ne, 2 * CAP, width), BF16), vm((2, 4, ne, 2 * CAP, width), BF16),
            vm((2, 3, nz, seq, width), BF16), vm((2, nz, seq, width + LANES), BF16),
            vm((2, 2, local, width, ff), BF16), vm((2, ne, 4, rows, hw), BF16), vm((2, ne, 4, rows, hw), BF16),
            vm((2, ne, rows, LANES), BF16), vm((2, ne, rows, LANES), BF16),
            vm((2, 4, rows, hw), BF16), vm((2, rows, LANES), BF16), vm((4, rows, hw), BF16), vm((rows, LANES), BF16),
            vm((4, rows, hw), BF16), vm((rows, LANES), BF16),
            dma((3,)), dma((8, 2)), dma((8,)), dma((2, 4)), dma((2, 4)), dma((8,)), dma((8,)), dma, dma, dma,
            dma((2,)), dma((2,)), dma((2,)), dma((2,)), dma((2,)), dma((2,)), dma((2,)), dma((2,)), dma((2,)),
            dma, dma, dma,
        ],
        compiler_params=pltpu.CompilerParams(
            collective_id=0, has_side_effects=True, vmem_limit_bytes=60 * 1024 * 1024),
        cost_estimate=pl.CostEstimate(flops=20_000_000_000, bytes_accessed=40_000_000, transcendentals=2_000_000),
    )(
        block_input, cotangent, routes_in, hot_in, gain_in, rel_in, router_in, qkv_weight[0], out_weight[0],
        up_weight[0], down_weight[0],
    )
    both = own.astype(F32) + recv.astype(F32)
    attn = attn.transpose(1, 0, 2, 3).reshape(4, width, hw).astype(F32)
    small = small.reshape(width, LANES).astype(F32)
    return (
        sec[None], small[:, 32][None], attn[None, :3], attn[3].T[None], small[None, :heads, 64:64 + buckets],
        small[:, 33][None], small[None, :, :experts], both[None, 0], both[None, 1],
    )


def solution(mesh):
    in_specs = (
        P(None, "expert", None), P(None, "expert", None), P("pipe", None, "expert", None), P(), P("pipe", None),
        P("pipe", None, None, "tensor"), P("pipe", "tensor", None), P("pipe", "tensor", None), P("pipe", None),
        P("pipe", None, None), P("pipe", "expert", None, "tensor"), P("pipe", "expert", "tensor", None),
    )
    out_specs = (
        P("pipe", None, "expert", None), P("pipe", None), P("pipe", None, None, "tensor"), P("pipe", "tensor", None),
        P("pipe", "tensor", None), P("pipe", None), P("pipe", None, None), P("pipe", "expert", None, "tensor"),
        P("pipe", "expert", "tensor", None),
    )
    return jax.shard_map(body, mesh=mesh, in_specs=in_specs, out_specs=out_specs, check_vma=False)
```

```python
import functools

import jax
import jax.numpy as jnp
from jax import lax
from jax.experimental import pallas as pl
from jax.experimental.pallas import tpu as pltpu
from jax.sharding import PartitionSpec as P

EPS = 1e-06
MASKED = -1e30
MESH = pl.DeviceIdType.MESH
F32 = jnp.float32
BF16 = jnp.bfloat16
LANES = 128
CAP = 8
PARTS = 3
SMALL = 64
TANH_A = 0.7978845608
TANH_B = 0.044715


def dot(a, b, left, right):
    return lax.dot_general(a, b, (((left,), (right,)), ((), ())), preferred_element_type=F32)


def nn(a, b):
    return dot(a, b, 1, 0)


def nt(a, b):
    return dot(a, b, 1, 1)


def tn(a, b):
    return dot(a, b, 0, 0)


def lanes_of(shape, dim):
    return lax.broadcasted_iota(jnp.int32, shape, dim)


def kernel(
    dims,
    x_in, cot_in, routes_in, bucket_in, one_in, two_in, bias_in, router_in, qkv_in, out_in, up_in, down_in,
    sec_out, own_up, own_down, recv_up, recv_down, attn_out, small_out,
    xin, cot, bucket, hot, routes, gain_one, gain_two, bias_w, router, w_qkv, w_out, w_up, w_down,
    hs, n_one, qkv, probs_s, mixed_s, h_mid_s, n_two, comb, eprobs, x_s, u_s, x_dy, x_du, x_hid, g_s, fin, dqkv,
    send_a, recv_a, send_c, recv_c, red_a, red_c, red_g, g_up, g_down, chunk, chunk_pair, chunk_in, flat, small, small_pair,
    small_in, total, total_small,
    sem_in, sem_w, sem_ws, sa_send, sa_recv, sc_send, sc_recv, rd_send, rd_recv, rc_send, rc_recv, gr_send, gr_recv, gr_loc,
    ck_send, ck_recv, pr_send, pr_recv, ag_send, ag_recv, ag_loc, sec_send, sec_recv, sec_loc,
):
    ne, nz, seq, width, local, heads, ff, hd = dims
    p = lax.axis_index("pipe")
    x = lax.axis_index("expert")
    z = lax.axis_index("tensor")
    other = 1 - p
    slots = ne * 2 * CAP
    hw = heads * hd
    rows = width // ne
    parts_c = PARTS
    part_w = width // parts_c
    fold = width // LANES
    per = hw // rows
    flat_rows = fold * SMALL // ne

    barrier = pltpu.get_barrier_semaphore()

    def hello_e(r, _):
        pl.semaphore_signal(barrier, inc=1, device_id={"expert": lax.rem(x + r, ne)}, device_id_type=MESH)
        return 0

    def hello_z(r, _):
        pl.semaphore_signal(barrier, inc=1, device_id={"tensor": lax.rem(z + r, nz)}, device_id_type=MESH)
        return 0

    lax.fori_loop(1, ne, hello_e, 0)
    lax.fori_loop(1, nz, hello_z, 0)
    pl.semaphore_signal(barrier, inc=1, device_id={"pipe": other}, device_id_type=MESH)

    ins = [
        pltpu.make_async_copy(x_in.at[p], xin, sem_in.at[0]),
        pltpu.make_async_copy(cot_in.at[p], cot, sem_in.at[1]),
        pltpu.make_async_copy(bucket_in, bucket, sem_in.at[2]),
    ]
    for copy in ins:
        copy.start()
    weights = [
        (one_in, gain_one), (qkv_in, w_qkv), (bias_in, bias_w), (out_in, w_out), (routes_in, routes), (router_in, router),
        (two_in, gain_two), (up_in, w_up), (down_in, w_down),
    ]
    for k, (src, dst) in enumerate(weights):
        pltpu.make_async_copy(src.at[p] if k == 4 else src, dst.at[p], sem_w.at[k, p]).start()
    pl.semaphore_wait(barrier, ne - 1 + nz - 1 + 1)
    outgoing = []
    for k, (src, dst) in enumerate(weights):
        copy = pltpu.make_async_remote_copy(
            src_ref=src.at[other] if k == 4 else src, dst_ref=dst.at[p], send_sem=sem_ws.at[k], recv_sem=sem_w.at[k, p],
            device_id={"pipe": other}, device_id_type=MESH)
        copy.start()
        outgoing.append(copy)

    def await_weight(k, l):
        dst = weights[k][1]
        pltpu.make_async_copy(dst.at[l], dst.at[l], sem_w.at[k, l]).wait()

    def send_all(src, dst, send, recv, forth):
        def one(r, _):
            pltpu.make_async_remote_copy(
                src_ref=src.at[r], dst_ref=dst.at[r], send_sem=send, recv_sem=recv,
                device_id={"expert": lax.rem(x + r if forth else x + ne - r, ne)}, device_id_type=MESH).start()
            return 0
        lax.fori_loop(1, ne, one, 0)
        dst[0] = src[0]

    def await_all(src, dst, send, recv):
        part = src.at[pl.ds(1, ne - 1)]
        pltpu.make_async_copy(part, part, send).wait()
        part = dst.at[pl.ds(1, ne - 1)]
        pltpu.make_async_copy(part, part, recv).wait()

    def exchange(kind, l):
        send_all(send_a.at[l, kind], recv_a.at[l, kind], sa_send.at[l, kind], sa_recv.at[l, kind], True)

    def arrived(kind, l):
        await_all(send_a.at[l, kind], recv_a.at[l, kind], sa_send.at[l, kind], sa_recv.at[l, kind])
        return recv_a[l, kind]

    def exchange_back(kind, l, c):
        send_all(send_c.at[l, kind, c], recv_c.at[l, kind, c], sc_send.at[l, kind, c], sc_recv.at[l, kind, c], False)

    def arrived_back(kind, l, c):
        await_all(send_c.at[l, kind, c], recv_c.at[l, kind, c], sc_send.at[l, kind, c], sc_recv.at[l, kind, c])
        return recv_c[l, kind, c].reshape(slots, part_w)

    def reduce_start(buf, send, recv):
        def one(r, _):
            pltpu.make_async_remote_copy(
                src_ref=buf.at[0], dst_ref=buf.at[r], send_sem=send, recv_sem=recv,
                device_id={"tensor": lax.rem(z + r, nz)}, device_id_type=MESH).start()
            return 0
        lax.fori_loop(1, nz, one, 0)

    def reduce_end(buf, send, recv):
        part = buf.at[pl.ds(1, nz - 1)]
        pltpu.make_async_copy(part, part, send).wait()
        pltpu.make_async_copy(part, part, recv).wait()
        acc = None
        for a in range(nz):
            term = buf[lax.rem(z + nz - a, nz)].astype(F32)
            acc = term if acc is None else acc + term
        return acc

    def summed_back(kind, l, weigh):
        for c in range(parts_c):
            red_c[l, kind, c, 0] = weigh(arrived_back(kind, l, c)).astype(BF16)
            reduce_start(red_c.at[l, kind, c], rc_send.at[l, kind, c], rc_recv.at[l, kind, c])
        return lambda: jnp.concatenate(
            [reduce_end(red_c.at[l, kind, c], rc_send.at[l, kind, c], rc_recv.at[l, kind, c]) for c in range(parts_c)], axis=1)

    def split(blocks):
        wide = blocks.astype(F32)
        return [wide[:, e * CAP:(e + 1) * CAP].reshape(ne * CAP, width).astype(BF16) for e in range(local)]

    def join(parts):
        return jnp.concatenate([part.reshape(ne, CAP, part_w) for part in parts], axis=1).astype(BF16)

    def head_mask(h):
        at = lanes_of((1, hw), 1)
        return ((at >= h * hd) & (at < (h + 1) * hd)).astype(BF16)

    def scale_of(h):
        return lax.rsqrt(jnp.mean(h * h, -1, keepdims=True) + EPS)

    def column(row):
        eye = lanes_of((seq, seq), 0) == lanes_of((seq, seq), 1)
        return jnp.sum(jnp.where(eye, row.astype(F32), 0.0), -1, keepdims=True)

    def chosen_of(ids):
        at = lanes_of((seq, ne * local), 1)
        return [(at == e).astype(F32) for e in ids]

    def named(l):
        return [column(routes[l, k:k + 1]).astype(jnp.int32) for k in range(2)]

    def router_of(l):
        r = router[l]
        high = r.astype(BF16)
        return high, (r - high.astype(F32)).astype(BF16)

    def forward(l, _):
        h_in = hs[l]
        await_weight(0, l)
        n1 = (h_in * scale_of(h_in) * gain_one[l]).astype(BF16)
        n_one[l] = n1
        await_weight(1, l)
        for c in range(3):
            qkv[l, c] = nt(n1, w_qkv[l, c]).astype(BF16)
        q, k, v = qkv[l, 0], qkv[l, 1], qkv[l, 2]
        await_weight(2, l)
        causal = lanes_of((seq, seq), 0) >= lanes_of((seq, seq), 1)
        mixed = jnp.zeros((seq, hw), F32)
        for h in range(heads):
            mask = head_mask(h)
            rel = lax.dot_general(
                jnp.broadcast_to(bias_w[l, h], (8, hot.shape[1])), hot[...], (((1,), (1,)), ((), ())),
                precision=lax.Precision.HIGHEST, preferred_element_type=F32)
            bias = pltpu.roll(jnp.broadcast_to(rel[0:1], (seq, seq)), 0, 1, stride=1, stride_axis=0)
            s = nt(q * mask, k) * (hd ** -0.5) + bias
            s = jnp.where(causal, s, MASKED)
            e = jnp.exp(s - jnp.max(s, -1, keepdims=True))
            prob = e / jnp.sum(e, -1, keepdims=True)
            probs_s[l, h] = prob
            mixed = mixed + nn(prob.astype(BF16), v * mask)
        mixed = mixed.astype(BF16)
        mixed_s[l] = mixed
        await_weight(3, l)
        red_a[l, 0, 0] = nn(mixed, w_out[l]).astype(BF16)
        reduce_start(red_a.at[l, 0], rd_send.at[l, 0], rd_recv.at[l, 0])

        await_weight(4, l)
        ids = named(l)
        hot_e = chosen_of(ids)
        row_at, col_at = lanes_of((seq, seq), 0), lanes_of((seq, seq), 1)
        earlier = (row_at > col_at).astype(BF16)
        count = nn(earlier, (hot_e[0] + hot_e[1]).astype(BF16))
        for kk in range(2):
            before = count if kk == 0 else count + hot_e[0]
            c = jnp.sum(before * hot_e[kk], -1, keepdims=True).astype(jnp.int32)
            e = ids[kk]
            place = (((e >> 1) - x + ne) & (ne - 1)) * (2 * CAP) + (e & 1) * CAP + c
            comb[l, kk * seq:(kk + 1) * seq] = (lanes_of((seq, slots), 1) == place).astype(F32).astype(BF16)
        both = comb[l, 0:seq] + comb[l, seq:2 * seq]
        await_weight(5, l)
        await_weight(6, l)

        h_mid = h_in + reduce_end(red_a.at[l, 0], rd_send.at[l, 0], rd_recv.at[l, 0])
        h_mid_s[l] = h_mid
        n2 = (h_mid * scale_of(h_mid) * gain_two[l]).astype(BF16)
        n_two[l] = n2
        send_a[l, 0] = tn(both, n2).astype(BF16).reshape(ne, 2 * CAP, width)
        exchange(0, l)
        high, low = router_of(l)
        logits = nt(n2, high) + nt(n2, low)
        e = jnp.exp(logits - jnp.max(logits, -1, keepdims=True))
        ep = e / jnp.sum(e, -1, keepdims=True)
        eprobs[l] = ep
        picked = [jnp.sum(ep * hot_e[kk], -1, keepdims=True) for kk in range(2)]
        inv = picked[0] + picked[1]
        gates = [picked[kk] / inv for kk in range(2)]
        await_weight(7, l)
        await_weight(8, l)
        parts = split(arrived(0, l))
        for e in range(local):
            x_s[l, e] = parts[e]

        def expert(e, _):
            u = nn(x_s[l, e], w_up[l, e])
            u_s[l, e] = u
            t = jnp.tanh(TANH_A * (u + TANH_B * u * u * u))
            x_hid[e] = (0.5 * u * (1.0 + t)).astype(BF16)
            return 0
        lax.fori_loop(0, local, expert, 0)
        for c in range(parts_c):
            cols = slice(c * part_w, (c + 1) * part_w)
            send_c[l, 0, c] = join([nn(x_hid[e], w_down[l, e, :, cols]) for e in range(local)])
            exchange_back(0, l, c)
        out = summed_back(0, l, lambda back: gates[0] * nn(comb[l, 0:seq], back) + gates[1] * nn(comb[l, seq:2 * seq], back))
        out = h_mid + out()
        hs[l + 1] = jnp.where(l == 0, out.astype(BF16).astype(F32), out)
        return 0

    for copy in ins:
        copy.wait()
    hs[0] = xin[...].astype(F32)
    turn_at, turn_of = lanes_of((seq, seq), 0), lanes_of((seq, seq), 1)
    turned_bucket = jnp.where((turn_at + turn_of == 0) | (turn_at + turn_of == seq), bucket[...].astype(F32), 0.0)
    turned_bucket = jnp.sum(turned_bucket, -1, keepdims=True).astype(jnp.int32)
    hot[...] = (turned_bucket == lanes_of(hot.shape, 1)).astype(F32)
    lax.fori_loop(0, 2, forward, 0)

    def deliver(src, owner):
        @pl.when(p == owner)
        def _():
            pltpu.make_async_copy(src, sec_out.at[p], sec_loc).start()

        @pl.when(p != owner)
        def _():
            pltpu.make_async_remote_copy(
                src_ref=src, dst_ref=sec_out.at[p], send_sem=sec_send, recv_sem=sec_recv,
                device_id={"pipe": other}, device_id_type=MESH).start()

    def merge(k, src, pair, mine, within, dst, send, recv):
        pltpu.make_async_copy(pair, pair, pr_recv.at[k]).wait()
        mine[...] = (src[p].astype(F32) + pair[...].astype(F32)).astype(mine.dtype)

        def scatter(r, _):
            to = lax.rem(x + r, ne)
            pltpu.make_async_remote_copy(
                src_ref=within(mine, to), dst_ref=dst.at[r], send_sem=send, recv_sem=recv,
                device_id={"expert": to}, device_id_type=MESH).start()
            return 0
        lax.fori_loop(1, ne, scatter, 0)

    def merge_attn():
        merge(0, chunk, chunk_pair, chunk_pair, lambda ref, j: ref.at[j], chunk_in, ck_send.at[0], ck_recv.at[0])
        chunk_in[0] = chunk_pair[x]

    def piece(ref, j):
        return ref.at[pl.ds(pl.multiple_of(j * flat_rows, 8), flat_rows)]

    def merge_small():
        merge(1, small, small_pair, small_pair, piece, small_in, ck_send.at[1], ck_recv.at[1])
        small_in[0] = small_pair[pl.ds(pl.multiple_of(x * flat_rows, 8), flat_rows)]

    def spread(k, arrived_at, whole, dst):
        part = arrived_at.at[pl.ds(1, ne - 1)]
        pltpu.make_async_copy(part, part, ck_send.at[k]).wait()
        pltpu.make_async_copy(part, part, ck_recv.at[k]).wait()
        acc = arrived_at[0].astype(F32)
        for r in range(1, ne):
            acc = acc + arrived_at[r].astype(F32)
        whole[...] = acc.astype(whole.dtype)
        pltpu.make_async_copy(whole, dst, ag_loc.at[k]).start()

        def one(r, _):
            pltpu.make_async_remote_copy(
                src_ref=whole, dst_ref=dst, send_sem=ag_send.at[k], recv_sem=ag_recv.at[k],
                device_id={"expert": lax.rem(x + r, ne)}, device_id_type=MESH).start()
            return 0
        lax.fori_loop(1, ne, one, 0)

    def spread_attn():
        spread(0, chunk_in, total, attn_out.at[x])

    def spread_small():
        spread(1, small_in, total_small, piece(small_out, x))

    def to_partner(src, dst, send, recv):
        pltpu.make_async_remote_copy(
            src_ref=src, dst_ref=dst, send_sem=send, recv_sem=recv, device_id={"pipe": other}, device_id_type=MESH).start()

    deliver(hs.at[2], 1)
    g_s[...] = cot[...].astype(F32)

    def backward(i, _):
        l = 1 - i
        g = g_s[...]
        hot_e = chosen_of(named(l))
        ep = eprobs[l]
        picked = [jnp.sum(ep * hot_e[kk], -1, keepdims=True) for kk in range(2)]
        inv = picked[0] + picked[1]
        gates = [picked[kk] / inv for kk in range(2)]
        dy = jnp.concatenate([(gates[kk] * g).astype(BF16) for kk in range(2)], axis=0)
        send_a[l, 1] = tn(comb[l], dy).astype(BF16).reshape(ne, 2 * CAP, width)
        exchange(1, l)

        @pl.when((p == 1) & (l == 0))
        def _():
            merge_attn()
            merge_small()

        at = lanes_of((seq, LANES), 1)
        gg = jnp.zeros((seq, LANES), F32)
        for kk in range(2):
            part = None
            for c in range(parts_c):
                got = nn(comb[l, kk * seq:(kk + 1) * seq], recv_c[l, 0, c].reshape(slots, part_w))
                term = jnp.sum(g[:, c * part_w:(c + 1) * part_w] * got, -1, keepdims=True)
                part = term if part is None else part + term
            high = part.astype(BF16).astype(F32)
            gg = gg + jnp.where(at == kk, high, 0.0) + jnp.where(at == 2 + kk, part - high, 0.0)
        red_g[l, 0] = gg.astype(BF16)
        reduce_start(red_g.at[l], rd_send.at[l, 2], rd_recv.at[l, 2])
        parts = split(arrived(1, l))
        for e in range(local):
            x_dy[e] = parts[e]

        def expert(e, _):
            dy_e = x_dy[e]
            dh = nt(dy_e, w_down[l, e])
            u = u_s[l, e]
            t = jnp.tanh(TANH_A * (u + TANH_B * u * u * u))
            slope = 0.5 * (1.0 + t) + (0.5 * TANH_A) * u * (1.0 - t * t) * (1.0 + (3.0 * TANH_B) * u * u)
            du = (dh * slope).astype(BF16)
            x_du[e] = du
            x_hid[e] = (0.5 * u * (1.0 + t)).astype(BF16)
            return 0
        lax.fori_loop(0, local, expert, 0)
        for c in range(parts_c):
            cols = slice(c * part_w, (c + 1) * part_w)
            send_c[l, 1, c] = join([nt(x_du[e], w_up[l, e, cols]) for e in range(local)])
            exchange_back(1, l, c)

        @pl.when((p == 1) & (l == 0))
        def _():
            spread_attn()
            spread_small()

        def expert_grads(e, _):
            g_up[l, e] = tn(x_s[l, e], x_du[e]).astype(BF16)
            g_down[l, e] = tn(x_hid[e], x_dy[e]).astype(BF16)
            return 0
        lax.fori_loop(0, local, expert_grads, 0)

        both = comb[l, 0:seq] + comb[l, seq:2 * seq]
        dn2 = summed_back(1, l, lambda back: nn(both, back))

        @pl.when(p == l)
        def _():
            pltpu.make_async_copy(g_up.at[l], own_up, gr_loc.at[0]).start()
            pltpu.make_async_copy(g_down.at[l], own_down, gr_loc.at[1]).start()

        @pl.when(p != l)
        def _():
            to_partner(g_up.at[l], recv_up, gr_send.at[0], gr_recv.at[0])
            to_partner(g_down.at[l], recv_down, gr_send.at[1], gr_recv.at[1])

        h_mid = h_mid_s[l]
        scale = scale_of(h_mid)
        tail = reduce_end(red_g.at[l], rd_send.at[l, 2], rd_recv.at[l, 2])
        dn2 = dn2()
        gg = [jnp.sum(jnp.where((at == kk) | (at == 2 + kk), tail, 0.0), -1, keepdims=True) for kk in range(2)]
        centre = gg[0] * gates[0] + gg[1] * gates[1]
        dprob = hot_e[0] * ((gg[0] - centre) / inv) + hot_e[1] * ((gg[1] - centre) / inv)
        dlog = (ep * (dprob - jnp.sum(ep * dprob, -1, keepdims=True))).astype(BF16)
        high, low = router_of(l)
        dn2 = dn2 + nn(dlog, high) + nn(dlog, low)
        flat[...] = jnp.zeros_like(flat)
        flat[0:ne * local] = tn(dlog, n_two[l])
        flat[ne * local + 1:ne * local + 2] = jnp.sum(dn2 * h_mid * scale, 0, keepdims=True)
        dg = dn2 * gain_two[l]
        dmid = g + scale * dg - h_mid * (scale * scale * scale) * jnp.mean(h_mid * dg, -1, keepdims=True)
        da = dmid.astype(BF16)
        chunk[l, 3 * per:4 * per] = tn(mixed_s[l], da).astype(BF16).reshape(per, rows, width)
        dmixed = nt(da, w_out[l]).astype(BF16)
        q, k, v = qkv[l, 0], qkv[l, 1], qkv[l, 2]
        dq = jnp.zeros((seq, hw), F32)
        dk = jnp.zeros((seq, hw), F32)
        dv = jnp.zeros((seq, hw), F32)
        causal = lanes_of((seq, seq), 0) >= lanes_of((seq, seq), 1)
        row_at = lanes_of((seq, seq), 0)
        top = lanes_of((8, LANES), 0)
        bias_g = jnp.zeros((8, LANES), F32)
        for h in range(heads):
            mask = head_mask(h)
            prob = probs_s[l, h]
            dm = dmixed * mask
            dp = nt(dm, v)
            dv = dv + tn(prob.astype(BF16), dm)
            ds = jnp.where(causal, prob * (dp - jnp.sum(prob * dp, -1, keepdims=True)), 0.0).astype(BF16)
            dq = dq + nn(ds, k * mask)
            dk = dk + tn(ds, q * mask)
            turned = ds.astype(F32)
            bit = 1
            while bit < seq:
                turned = jnp.where((row_at & bit) != 0, pltpu.roll(turned, seq - bit, 1), turned)
                bit *= 2
            bias_g = bias_g + jnp.where(top == h, jnp.sum(turned, 0, keepdims=True), 0.0)
        dqkv[0] = (dq * (hd ** -0.5)).astype(BF16)
        dqkv[1] = (dk * (hd ** -0.5)).astype(BF16)
        dqkv[2] = dv.astype(BF16)
        dn1 = nn(dqkv[0], w_qkv[l, 0]) + nn(dqkv[1], w_qkv[l, 1]) + nn(dqkv[2], w_qkv[l, 2])
        red_a[l, 1, 0] = dn1.astype(BF16)
        reduce_start(red_a.at[l, 1], rd_send.at[l, 1], rd_recv.at[l, 1])
        n1 = n_one[l]
        for c in range(3):
            chunk[l, c * per:(c + 1) * per] = tn(dqkv[c], n1).astype(BF16).reshape(per, rows, width)

        @pl.when(p != l)
        def _():
            to_partner(chunk.at[l], chunk_pair, pr_send.at[0], pr_recv.at[0])

        @pl.when((p == 0) & (l == 0))
        def _():
            merge_attn()

        bias_high = bias_g.astype(BF16)
        bias_low = (bias_g - bias_high.astype(F32)).astype(BF16)
        hot_b = hot[...].astype(BF16)
        flat[ne * local + 8:ne * local + 16, 0:hot.shape[1]] = nn(bias_high, hot_b) + nn(bias_low, hot_b)
        h_in = hs[l]
        scale_one = scale_of(h_in)
        dn1 = reduce_end(red_a.at[l, 1], rd_send.at[l, 1], rd_recv.at[l, 1])
        flat[ne * local:ne * local + 1] = jnp.sum(dn1 * h_in * scale_one, 0, keepdims=True)
        for b in range(fold):
            small[l, b * SMALL:(b + 1) * SMALL] = flat[:, b * LANES:(b + 1) * LANES]

        @pl.when(p != l)
        def _():
            to_partner(small.at[l], small_pair, pr_send.at[1], pr_recv.at[1])

        dg = dn1 * gain_one[l]
        dh = dmid + scale_one * dg - h_in * (scale_one * scale_one * scale_one) * jnp.mean(h_in * dg, -1, keepdims=True)
        fin[...] = dh
        g_s[...] = dh.astype(BF16).astype(F32)
        return 0

    lax.fori_loop(0, 2, backward, 0)
    deliver(fin, 0)

    @pl.when(p == 0)
    def _():
        merge_small()
        spread_attn()
        spread_small()

    for copy in outgoing:
        copy.wait_send()
    for k, ref in enumerate((g_up, g_down)):
        for sem in (gr_loc, gr_send, gr_recv):
            pltpu.make_async_copy(ref.at[0], ref.at[0], sem.at[k]).wait()
    for sem in (sec_loc, sec_send, sec_recv):
        pltpu.make_async_copy(fin, fin, sem).wait()
    for k, (pair, whole, arrived_at) in enumerate(((chunk_pair, total, chunk_in), (small_pair, total_small, small_in))):
        pltpu.make_async_copy(pair, pair, pr_send.at[k]).wait()
        pltpu.make_async_copy(whole, whole, ag_loc.at[k]).wait()
        part = arrived_at.at[pl.ds(1, ne - 1)]
        pltpu.make_async_copy(part, part, ag_send.at[k]).wait()
        pltpu.make_async_copy(part, part, ag_recv.at[k]).wait()


def body(
    block_input, cotangent, routes, offset_bucket, norm1_gain, qkv_weight, out_weight, bias_table, norm2_gain,
    router_weight, up_weight, down_weight,
):
    ne = lax.axis_size("expert")
    nz = lax.axis_size("tensor")
    micro, seq, width = block_input.shape
    heads, buckets = bias_table.shape[1:]
    local, _, ff = up_weight.shape[1:]
    hw = qkv_weight.shape[3]
    hd = hw // heads
    experts = router_weight.shape[2]
    rows = width // ne
    parts_c = PARTS
    part_w = width // parts_c
    fold = width // LANES
    per = hw // rows
    flat_rows = fold * SMALL // ne
    slots = ne * local * CAP

    any_space = pl.BlockSpec(memory_space=pl.ANY)
    vm = pltpu.VMEM
    dma = pltpu.SemaphoreType.DMA
    sds = jax.ShapeDtypeStruct
    part_w = width // PARTS
    flat = width // LANES * SMALL
    parts_in = (2, 2, PARTS, ne, 2 * CAP, part_w)
    half = (local, width, ff)
    sec, own_up, own_down, recv_up, recv_down, attn, small = pl.pallas_call(
        functools.partial(kernel, (ne, nz, seq, width, local, heads, ff, hd)),
        out_shape=[
            sds((micro, seq, width), F32), sds(half, BF16), sds(half, BF16), sds(half, BF16), sds(half, BF16),
            sds((ne, rows, width), BF16), sds((flat, LANES), F32),
        ],
        in_specs=[any_space] * 12,
        out_specs=[any_space] * 7,
        scratch_shapes=[
            vm((seq, width), BF16), vm((seq, width), BF16), vm((1, seq), jnp.int32), vm((seq, buckets), F32),
            vm((2, 2, seq), jnp.int32), vm((2, 1, width), F32), vm((2, 1, width), F32), vm((2, heads, 1, buckets), F32),
            vm((2, experts, width), F32), vm((2, 3, hw, width), BF16),
            vm((2, hw, width), BF16), vm((2, local, width, ff), BF16), vm((2, local, ff, width), BF16),
            vm((3, seq, width), F32), vm((2, seq, width), BF16), vm((2, 3, seq, hw), BF16),
            vm((2, heads, seq, seq), F32), vm((2, seq, hw), BF16), vm((2, seq, width), F32), vm((2, seq, width), BF16),
            vm((2, 2 * seq, slots), BF16), vm((2, seq, experts), F32), vm((2, local, ne * CAP, width), BF16),
            vm((2, local, ne * CAP, ff), F32),
            vm((local, ne * CAP, width), BF16), vm((local, ne * CAP, ff), BF16), vm((local, ne * CAP, ff), BF16),
            vm((seq, width), F32), vm((seq, width), F32), vm((3, seq, hw), BF16),
            vm((2, 2, ne, 2 * CAP, width), BF16), vm((2, 2, ne, 2 * CAP, width), BF16), vm(parts_in, BF16), vm(parts_in, BF16),
            vm((2, 2, nz, seq, width), BF16), vm((2, 2, PARTS, nz, seq, part_w), BF16), vm((2, nz, seq, LANES), BF16),
            vm((2, *half), BF16), vm((2, *half), BF16), vm((2, ne, rows, width), BF16), vm((ne, rows, width), BF16),
            vm((ne, rows, width), BF16), vm((SMALL, width), F32), vm((2, flat, LANES), F32), vm((flat, LANES), F32),
            vm((ne, flat // ne, LANES), F32), vm((rows, width), BF16), vm((flat // ne, LANES), F32),
            dma((3,)), dma((9, 2)), dma((9,)), dma((2, 2)), dma((2, 2)), dma((2, 2, PARTS)), dma((2, 2, PARTS)),
            dma((2, 3)), dma((2, 3)), dma((2, 2, PARTS)), dma((2, 2, PARTS)), dma((2,)), dma((2,)), dma((2,)),
            dma((2,)), dma((2,)), dma((2,)), dma((2,)), dma((2,)), dma((2,)), dma((2,)), dma, dma, dma,
        ],
        compiler_params=pltpu.CompilerParams(
            collective_id=0, has_side_effects=True, vmem_limit_bytes=60 * 1024 * 1024),
        cost_estimate=pl.CostEstimate(flops=20_000_000_000, bytes_accessed=40_000_000, transcendentals=2_000_000),
    )(
        block_input, cotangent, routes[0].transpose(0, 2, 1), offset_bucket[None], norm1_gain, norm2_gain,
        bias_table.transpose(1, 0, 2), router_weight[0].T, qkv_weight[0].transpose(0, 2, 1), out_weight[0],
        up_weight[0], down_weight[0],
    )
    grad_up = own_up.astype(F32) + recv_up.astype(F32)
    grad_down = own_down.astype(F32) + recv_down.astype(F32)
    attn = attn.reshape(4, hw, width).astype(F32)
    small = small.reshape(width // LANES, SMALL, LANES).transpose(1, 0, 2).reshape(SMALL, width)
    return (
        sec[None], small[experts][None], attn[None, :3].transpose(0, 1, 3, 2), attn[3][None],
        small[None, experts + 8:experts + 8 + heads, :buckets], small[experts + 1][None], small[:experts].T[None],
        grad_up[None], grad_down[None],
    )


def solution(mesh):
    in_specs = (
        P(None, "expert", None), P(None, "expert", None), P("pipe", None, "expert", None), P(), P("pipe", None),
        P("pipe", None, None, "tensor"), P("pipe", "tensor", None), P("pipe", "tensor", None), P("pipe", None),
        P("pipe", None, None), P("pipe", "expert", None, "tensor"), P("pipe", "expert", "tensor", None),
    )
    out_specs = (
        P("pipe", None, "expert", None), P("pipe", None), P("pipe", None, None, "tensor"), P("pipe", "tensor", None),
        P("pipe", "tensor", None), P("pipe", None), P("pipe", None, None), P("pipe", "expert", None, "tensor"),
        P("pipe", "expert", "tensor", None),
    )
    return jax.shard_map(body, mesh=mesh, in_specs=in_specs, out_specs=out_specs, check_vma=False)
```

```python
import functools

import jax
import jax.numpy as jnp
from jax import lax
from jax.experimental import pallas as pl
from jax.experimental.pallas import tpu as pltpu
from jax.sharding import PartitionSpec as P

EPS = 1e-06
MASKED = -1e30
MESH = pl.DeviceIdType.MESH
F32 = jnp.float32
BF16 = jnp.bfloat16
LANES = 128
CAP = 8
PARTS = 3
SMALL = 64
VMEM_MB = 60
TANH_A = 0.7978845608
TANH_B = 0.044715


def dot(a, b, left, right):
    return lax.dot_general(a, b, (((left,), (right,)), ((), ())), preferred_element_type=F32)


def nn(a, b):
    return dot(a, b, 1, 0)


def nt(a, b):
    return dot(a, b, 1, 1)


def tn(a, b):
    return dot(a, b, 0, 0)


def lanes_of(shape, dim):
    return lax.broadcasted_iota(jnp.int32, shape, dim)


def kernel(
    dims,
    x_in, cot_in, routes_in, bucket_in, one_in, two_in, bias_in, router_in, qkv_in, out_in, up_in, down_in,
    sec_out, own_up, own_down, recv_up, recv_down, attn_out, small_out,
    xin, cot, bucket, hot, routes, gain_one, gain_two, bias_w, router, w_qkv, w_out, w_up, w_down,
    hs, n_one, qkv, probs_s, mixed_s, h_mid_s, n_two, comb, eprobs, x_s, u_s, x_dy, x_du, hid_s, g_s, fin, dqkv,
    send_a, recv_a, send_g, recv_g, send_c, recv_c, red_a, red_c, red_g, g_up, g_down, chunk, chunk_pair, chunk_in, flat, small, small_pair,
    small_in, total, total_small,
    sem_in, sem_w, sem_ws, sa_send, sa_recv, sg_send, sg_recv, sc_send, sc_recv, rd_send, rd_recv, rc_send, rc_recv, gr_send, gr_recv, gr_loc,
    ck_send, ck_recv, pr_send, pr_recv, ag_send, ag_recv, ag_loc, sec_send, sec_recv, sec_loc,
):
    ne, nz, seq, width, local, heads, ff, hd = dims
    p = lax.axis_index("pipe")
    x = lax.axis_index("expert")
    z = lax.axis_index("tensor")
    other = 1 - p
    slots = ne * 2 * CAP
    hw = heads * hd
    rows = width // ne
    parts_c = PARTS
    part_w = width // parts_c
    fold = width // LANES
    per = hw // rows
    flat_rows = fold * SMALL // ne

    barrier = pltpu.get_barrier_semaphore()

    def hello_e(r, _):
        pl.semaphore_signal(barrier, inc=1, device_id={"expert": lax.rem(x + r, ne)}, device_id_type=MESH)
        return 0

    def hello_z(r, _):
        pl.semaphore_signal(barrier, inc=1, device_id={"tensor": lax.rem(z + r, nz)}, device_id_type=MESH)
        return 0

    lax.fori_loop(1, ne, hello_e, 0)
    lax.fori_loop(1, nz, hello_z, 0)
    pl.semaphore_signal(barrier, inc=1, device_id={"pipe": other}, device_id_type=MESH)

    ins = [
        pltpu.make_async_copy(x_in.at[p], xin, sem_in.at[0]),
        pltpu.make_async_copy(cot_in.at[p], cot, sem_in.at[1]),
        pltpu.make_async_copy(bucket_in, bucket, sem_in.at[2]),
    ]
    for copy in ins:
        copy.start()
    weights = [
        (one_in, gain_one), (qkv_in, w_qkv), (bias_in, bias_w), (out_in, w_out), (routes_in, routes), (router_in, router),
        (two_in, gain_two), (up_in, w_up), (down_in, w_down),
    ]
    def load(k):
        src, dst = weights[k]
        pltpu.make_async_copy(src.at[p] if k == 4 else src, dst.at[p], sem_w.at[k, p]).start()

    def lend(k):
        src, dst = weights[k]
        return pltpu.make_async_remote_copy(
            src_ref=src.at[other] if k == 4 else src, dst_ref=dst.at[p], send_sem=sem_ws.at[k], recv_sem=sem_w.at[k, p],
            device_id={"pipe": other}, device_id_type=MESH)

    load(4)

    @pl.when(p == 0)
    def _():
        for k in (0, 1, 2, 3, 5, 6):
            load(k)
    pl.semaphore_wait(barrier, ne - 1 + nz - 1 + 1)
    lend(4).start()

    @pl.when(p == 0)
    def _():
        for k in (0, 1, 2, 3, 5, 6, 7, 8):
            lend(k).start()
        for k in (7, 8):
            load(k)

    def await_weight(k, l):
        dst = weights[k][1]
        pltpu.make_async_copy(dst.at[l], dst.at[l], sem_w.at[k, l]).wait()

    def send_all(src, dst, send, recv, forth):
        def one(r, _):
            pltpu.make_async_remote_copy(
                src_ref=src.at[r], dst_ref=dst.at[r], send_sem=send, recv_sem=recv,
                device_id={"expert": lax.rem(x + r if forth else x + ne - r, ne)}, device_id_type=MESH).start()
            return 0
        lax.fori_loop(1, ne, one, 0)
        dst[0] = src[0]

    def await_all(src, dst, send, recv):
        part = src.at[pl.ds(1, ne - 1)]
        pltpu.make_async_copy(part, part, send).wait()
        part = dst.at[pl.ds(1, ne - 1)]
        pltpu.make_async_copy(part, part, recv).wait()

    def exchange(kind, l):
        send_all(send_a.at[kind], recv_a.at[l, kind], sa_send.at[l, kind], sa_recv.at[l, kind], True)

    def arrived(kind, l):
        await_all(send_a.at[kind], recv_a.at[l, kind], sa_send.at[l, kind], sa_recv.at[l, kind])
        return recv_a[l, kind]

    def exchange_back(kind, l, c):
        send_all(send_c.at[c], recv_c.at[l, kind, c], sc_send.at[l, kind, c], sc_recv.at[l, kind, c], False)

    def arrived_back(kind, l, c):
        await_all(send_c.at[c], recv_c.at[l, kind, c], sc_send.at[l, kind, c], sc_recv.at[l, kind, c])
        return recv_c[l, kind, c].reshape(slots, part_w)

    def reduce_start(buf, send, recv):
        def one(r, _):
            pltpu.make_async_remote_copy(
                src_ref=buf.at[0], dst_ref=buf.at[r], send_sem=send, recv_sem=recv,
                device_id={"tensor": lax.rem(z + r, nz)}, device_id_type=MESH).start()
            return 0
        lax.fori_loop(1, nz, one, 0)

    def reduce_end(buf, send, recv):
        part = buf.at[pl.ds(1, nz - 1)]
        pltpu.make_async_copy(part, part, send).wait()
        pltpu.make_async_copy(part, part, recv).wait()
        acc = None
        for a in range(nz):
            term = buf[lax.rem(z + nz - a, nz)].astype(F32)
            acc = term if acc is None else acc + term
        return acc

    def summed_back(kind, l, weigh):
        for c in range(parts_c):
            red_c[l, kind, c, 0] = weigh(arrived_back(kind, l, c)).astype(BF16)
            reduce_start(red_c.at[l, kind, c], rc_send.at[l, kind, c], rc_recv.at[l, kind, c])
        return lambda: jnp.concatenate(
            [reduce_end(red_c.at[l, kind, c], rc_send.at[l, kind, c], rc_recv.at[l, kind, c]) for c in range(parts_c)], axis=1)

    def split(blocks):
        wide = blocks.astype(F32)
        return [wide[:, e * CAP:(e + 1) * CAP].reshape(ne * CAP, width).astype(BF16) for e in range(local)]

    def join(parts):
        return jnp.concatenate([part.reshape(ne, CAP, part_w) for part in parts], axis=1).astype(BF16)

    def head_mask(h):
        at = lanes_of((1, hw), 1)
        return ((at >= h * hd) & (at < (h + 1) * hd)).astype(BF16)

    def scale_of(h):
        return lax.rsqrt(jnp.mean(h * h, -1, keepdims=True) + EPS)

    def column(row):
        eye = lanes_of((seq, seq), 0) == lanes_of((seq, seq), 1)
        return jnp.sum(jnp.where(eye, row.astype(F32), 0.0), -1, keepdims=True)

    def chosen_of(ids):
        at = lanes_of((seq, ne * local), 1)
        return [(at == e).astype(F32) for e in ids]

    def named(l):
        return [column(routes[l, k:k + 1]).astype(jnp.int32) for k in range(2)]

    def router_of(l):
        r = router[l]
        high = r.astype(BF16)
        return high, (r - high.astype(F32)).astype(BF16)

    def place(l):
        ids = named(l)
        hot_e = chosen_of(ids)
        row_at, col_at = lanes_of((seq, seq), 0), lanes_of((seq, seq), 1)
        earlier = (row_at > col_at).astype(BF16)
        count = nn(earlier, (hot_e[0] + hot_e[1]).astype(BF16))
        for kk in range(2):
            before = count if kk == 0 else count + hot_e[0]
            c = jnp.sum(before * hot_e[kk], -1, keepdims=True).astype(jnp.int32)
            e = ids[kk]
            at = (((e >> 1) - x + ne) & (ne - 1)) * (2 * CAP) + (e & 1) * CAP + c
            comb[l, kk * seq:(kk + 1) * seq] = (lanes_of((seq, slots), 1) == at).astype(F32).astype(BF16)

    def forward(l, _):
        h_in = hs[l]
        await_weight(0, l)
        n1 = (h_in * scale_of(h_in) * gain_one[l]).astype(BF16)
        n_one[l] = n1
        await_weight(1, l)
        for c in range(3):
            qkv[l, c] = nt(n1, w_qkv[l, c]).astype(BF16)
        q, k, v = qkv[l, 0], qkv[l, 1], qkv[l, 2]
        await_weight(2, l)
        causal = lanes_of((seq, seq), 0) >= lanes_of((seq, seq), 1)
        mixed = jnp.zeros((seq, hw), F32)
        for h in range(heads):
            mask = head_mask(h)
            rel = lax.dot_general(
                jnp.broadcast_to(bias_w[l, h], (8, hot.shape[1])), hot[...], (((1,), (1,)), ((), ())),
                precision=lax.Precision.HIGHEST, preferred_element_type=F32)
            bias = pltpu.roll(jnp.broadcast_to(rel[0:1], (seq, seq)), 0, 1, stride=1, stride_axis=0)
            s = nt(q * mask, k) * (hd ** -0.5) + bias
            s = jnp.where(causal, s, MASKED)
            e = jnp.exp(s - jnp.max(s, -1, keepdims=True))
            prob = e / jnp.sum(e, -1, keepdims=True)
            probs_s[l, h] = prob
            mixed = mixed + nn(prob.astype(BF16), v * mask)
        mixed = mixed.astype(BF16)
        mixed_s[l] = mixed
        await_weight(3, l)
        red_a[l, 0, 0] = nn(mixed, w_out[l]).astype(BF16)
        reduce_start(red_a.at[l, 0], rd_send.at[l, 0], rd_recv.at[l, 0])

        @pl.when(l == 0)
        def _():
            @pl.when(p == 1)
            def _():
                for k in (0, 1, 2, 3, 5, 6, 7, 8):
                    lend(k).start()
                    load(k)
            for layer in range(2):
                await_weight(4, layer)
                place(layer)
            send_a[1] = tn(comb[1, 0:seq] + comb[1, seq:2 * seq], cot[...]).astype(BF16).reshape(ne, 2 * CAP, width)
            exchange(1, 1)

        hot_e = chosen_of(named(l))
        both = comb[l, 0:seq] + comb[l, seq:2 * seq]
        await_weight(5, l)
        await_weight(6, l)

        h_mid = h_in + reduce_end(red_a.at[l, 0], rd_send.at[l, 0], rd_recv.at[l, 0])
        h_mid_s[l] = h_mid
        n2 = (h_mid * scale_of(h_mid) * gain_two[l]).astype(BF16)
        n_two[l] = n2
        send_a[0] = tn(both, n2).astype(BF16).reshape(ne, 2 * CAP, width)
        exchange(0, l)
        high, low = router_of(l)
        logits = nt(n2, high) + nt(n2, low)
        e = jnp.exp(logits - jnp.max(logits, -1, keepdims=True))
        ep = e / jnp.sum(e, -1, keepdims=True)
        eprobs[l] = ep
        picked = [jnp.sum(ep * hot_e[kk], -1, keepdims=True) for kk in range(2)]
        inv = picked[0] + picked[1]
        gates = [picked[kk] / inv for kk in range(2)]

        @pl.when(l == 1)
        def _():
            at = lanes_of((seq, LANES), 1)
            sent = []
            for kk in range(2):
                top = gates[kk].astype(BF16).astype(F32)
                sent.append(jnp.where(at == 0, top, jnp.where(at == 1, gates[kk] - top, 0.0)).astype(BF16))
            send_g[...] = tn(comb[l], jnp.concatenate(sent, axis=0)).astype(BF16).reshape(ne, 2 * CAP, LANES)
            send_all(send_g, recv_g, sg_send, sg_recv, True)

        await_weight(7, l)
        await_weight(8, l)
        parts = split(arrived(0, l))
        for e in range(local):
            x_s[l, e] = parts[e]

        def expert(e, _):
            u = nn(x_s[l, e], w_up[l, e])
            u_s[l, e] = u
            t = jnp.tanh(TANH_A * (u + TANH_B * u * u * u))
            hid_s[l, e] = (0.5 * u * (1.0 + t)).astype(BF16)
            return 0
        lax.fori_loop(0, local, expert, 0)
        for c in range(parts_c):
            cols = slice(c * part_w, (c + 1) * part_w)
            send_c[c] = join([nn(hid_s[l, e], w_down[l, e, :, cols]) for e in range(local)])
            exchange_back(0, l, c)

        def slopes(e, _):
            u = u_s[l, e]
            t = jnp.tanh(TANH_A * (u + TANH_B * u * u * u))
            u_s[l, e] = 0.5 * (1.0 + t) + (0.5 * TANH_A) * u * (1.0 - t * t) * (1.0 + (3.0 * TANH_B) * u * u)
            return 0
        lax.fori_loop(0, local, slopes, 0)
        out = summed_back(0, l, lambda back: gates[0] * nn(comb[l, 0:seq], back) + gates[1] * nn(comb[l, seq:2 * seq], back))
        out = h_mid + out()
        hs[l + 1] = jnp.where(l == 0, out.astype(BF16).astype(F32), out)
        return 0

    for copy in ins:
        copy.wait()
    hs[0] = xin[...].astype(F32)
    turn_at, turn_of = lanes_of((seq, seq), 0), lanes_of((seq, seq), 1)
    turned_bucket = jnp.where((turn_at + turn_of == 0) | (turn_at + turn_of == seq), bucket[...].astype(F32), 0.0)
    turned_bucket = jnp.sum(turned_bucket, -1, keepdims=True).astype(jnp.int32)
    hot[...] = (turned_bucket == lanes_of(hot.shape, 1)).astype(F32)
    lax.fori_loop(0, 2, forward, 0)

    def deliver(src, owner):
        @pl.when(p == owner)
        def _():
            pltpu.make_async_copy(src, sec_out.at[p], sec_loc).start()

        @pl.when(p != owner)
        def _():
            pltpu.make_async_remote_copy(
                src_ref=src, dst_ref=sec_out.at[p], send_sem=sec_send, recv_sem=sec_recv,
                device_id={"pipe": other}, device_id_type=MESH).start()

    def merge(k, src, pair, mine, within, dst, send, recv):
        pltpu.make_async_copy(pair, pair, pr_recv.at[k]).wait()
        mine[...] = (src[p].astype(F32) + pair[...].astype(F32)).astype(mine.dtype)

        def scatter(r, _):
            to = lax.rem(x + r, ne)
            pltpu.make_async_remote_copy(
                src_ref=within(mine, to), dst_ref=dst.at[r], send_sem=send, recv_sem=recv,
                device_id={"expert": to}, device_id_type=MESH).start()
            return 0
        lax.fori_loop(1, ne, scatter, 0)

    def merge_attn():
        merge(0, chunk, chunk_pair, chunk_pair, lambda ref, j: ref.at[j], chunk_in, ck_send.at[0], ck_recv.at[0])
        chunk_in[0] = chunk_pair[x]

    def piece(ref, j):
        return ref.at[pl.ds(pl.multiple_of(j * flat_rows, 8), flat_rows)]

    def merge_small():
        merge(1, small, small_pair, small_pair, piece, small_in, ck_send.at[1], ck_recv.at[1])
        small_in[0] = small_pair[pl.ds(pl.multiple_of(x * flat_rows, 8), flat_rows)]

    def spread(k, arrived_at, whole, dst):
        part = arrived_at.at[pl.ds(1, ne - 1)]
        pltpu.make_async_copy(part, part, ck_send.at[k]).wait()
        pltpu.make_async_copy(part, part, ck_recv.at[k]).wait()
        acc = arrived_at[0].astype(F32)
        for r in range(1, ne):
            acc = acc + arrived_at[r].astype(F32)
        whole[...] = acc.astype(whole.dtype)
        pltpu.make_async_copy(whole, dst, ag_loc.at[k]).start()

        def one(r, _):
            pltpu.make_async_remote_copy(
                src_ref=whole, dst_ref=dst, send_sem=ag_send.at[k], recv_sem=ag_recv.at[k],
                device_id={"expert": lax.rem(x + r, ne)}, device_id_type=MESH).start()
            return 0
        lax.fori_loop(1, ne, one, 0)

    def spread_attn():
        spread(0, chunk_in, total, attn_out.at[x])

    def spread_small():
        spread(1, small_in, total_small, piece(small_out, x))

    def to_partner(src, dst, send, recv):
        pltpu.make_async_remote_copy(
            src_ref=src, dst_ref=dst, send_sem=send, recv_sem=recv, device_id={"pipe": other}, device_id_type=MESH).start()

    part = send_a.at[1, pl.ds(1, ne - 1)]
    pltpu.make_async_copy(part, part, sa_send.at[1, 1]).wait()
    deliver(hs.at[2], 1)
    g_s[...] = cot[...].astype(F32)

    def backward(i, _):
        l = 1 - i
        g = g_s[...]
        hot_e = chosen_of(named(l))
        ep = eprobs[l]
        picked = [jnp.sum(ep * hot_e[kk], -1, keepdims=True) for kk in range(2)]
        inv = picked[0] + picked[1]
        gates = [picked[kk] / inv for kk in range(2)]
        at = lanes_of((seq, LANES), 1)

        @pl.when(l == 0)
        def _():
            dy = jnp.concatenate([(gates[kk] * g).astype(BF16) for kk in range(2)], axis=0)
            send_a[1] = tn(comb[l], dy).astype(BF16).reshape(ne, 2 * CAP, width)
            exchange(1, l)

            @pl.when(p == 1)
            def _():
                merge_attn()
                merge_small()
            parts = split(arrived(1, l))
            for e in range(local):
                x_dy[e] = parts[e]

        @pl.when(l == 1)
        def _():
            await_all(send_g, recv_g, sg_send, sg_recv)
            weigh = jnp.sum(recv_g[...].astype(F32), -1, keepdims=True)
            part = recv_a.at[l, 1, pl.ds(1, ne - 1)]
            pltpu.make_async_copy(part, part, sa_recv.at[l, 1]).wait()
            wide = recv_a[l, 1].astype(F32) * weigh
            for e in range(local):
                x_dy[e] = wide[:, e * CAP:(e + 1) * CAP].reshape(ne * CAP, width).astype(BF16)

        def expert(e, _):
            dy_e = x_dy[e]
            dh = nt(dy_e, w_down[l, e])
            x_du[e] = (dh * u_s[l, e]).astype(BF16)
            return 0
        lax.fori_loop(0, local, expert, 0)
        for c in range(parts_c):
            cols = slice(c * part_w, (c + 1) * part_w)
            send_c[c] = join([nt(x_du[e], w_up[l, e, cols]) for e in range(local)])
            exchange_back(1, l, c)

        @pl.when((p == 1) & (l == 0))
        def _():
            spread_attn()
            spread_small()

        gg = jnp.zeros((seq, LANES), F32)
        for kk in range(2):
            part = None
            for c in range(parts_c):
                got = nn(comb[l, kk * seq:(kk + 1) * seq], recv_c[l, 0, c].reshape(slots, part_w))
                term = jnp.sum(g[:, c * part_w:(c + 1) * part_w] * got, -1, keepdims=True)
                part = term if part is None else part + term
            high = part.astype(BF16).astype(F32)
            gg = gg + jnp.where(at == kk, high, 0.0) + jnp.where(at == 2 + kk, part - high, 0.0)
        red_g[l, 0] = gg.astype(BF16)
        reduce_start(red_g.at[l], rd_send.at[l, 2], rd_recv.at[l, 2])

        def expert_grads(e, _):
            g_up[l, e] = tn(x_s[l, e], x_du[e]).astype(BF16)
            g_down[l, e] = tn(hid_s[l, e], x_dy[e]).astype(BF16)
            return 0
        lax.fori_loop(0, local, expert_grads, 0)

        both = comb[l, 0:seq] + comb[l, seq:2 * seq]
        dn2 = summed_back(1, l, lambda back: nn(both, back))

        @pl.when(p == l)
        def _():
            pltpu.make_async_copy(g_up.at[l], own_up, gr_loc.at[0]).start()
            pltpu.make_async_copy(g_down.at[l], own_down, gr_loc.at[1]).start()

        @pl.when(p != l)
        def _():
            to_partner(g_up.at[l], recv_up, gr_send.at[0], gr_recv.at[0])
            to_partner(g_down.at[l], recv_down, gr_send.at[1], gr_recv.at[1])

        h_mid = h_mid_s[l]
        scale = scale_of(h_mid)
        tail = reduce_end(red_g.at[l], rd_send.at[l, 2], rd_recv.at[l, 2])
        dn2 = dn2()
        gg = [jnp.sum(jnp.where((at == kk) | (at == 2 + kk), tail, 0.0), -1, keepdims=True) for kk in range(2)]
        centre = gg[0] * gates[0] + gg[1] * gates[1]
        dprob = hot_e[0] * ((gg[0] - centre) / inv) + hot_e[1] * ((gg[1] - centre) / inv)
        dlog = (ep * (dprob - jnp.sum(ep * dprob, -1, keepdims=True))).astype(BF16)
        high, low = router_of(l)
        dn2 = dn2 + nn(dlog, high) + nn(dlog, low)
        flat[...] = jnp.zeros_like(flat)
        flat[0:ne * local] = tn(dlog, n_two[l])
        flat[ne * local + 1:ne * local + 2] = jnp.sum(dn2 * h_mid * scale, 0, keepdims=True)
        dg = dn2 * gain_two[l]
        dmid = g + scale * dg - h_mid * (scale * scale * scale) * jnp.mean(h_mid * dg, -1, keepdims=True)
        da = dmid.astype(BF16)
        dmixed = nt(da, w_out[l]).astype(BF16)
        q, k, v = qkv[l, 0], qkv[l, 1], qkv[l, 2]
        dq = jnp.zeros((seq, hw), F32)
        dk = jnp.zeros((seq, hw), F32)
        dv = jnp.zeros((seq, hw), F32)
        causal = lanes_of((seq, seq), 0) >= lanes_of((seq, seq), 1)
        row_at = lanes_of((seq, seq), 0)
        top = lanes_of((8, LANES), 0)
        bias_g = jnp.zeros((8, LANES), F32)
        for h in range(heads):
            mask = head_mask(h)
            prob = probs_s[l, h]
            dm = dmixed * mask
            dp = nt(dm, v)
            dv = dv + tn(prob.astype(BF16), dm)
            ds = jnp.where(causal, prob * (dp - jnp.sum(prob * dp, -1, keepdims=True)), 0.0).astype(BF16)
            dq = dq + nn(ds, k * mask)
            dk = dk + tn(ds, q * mask)
            turned = ds.astype(F32)
            bit = 1
            while bit < seq:
                turned = jnp.where((row_at & bit) != 0, pltpu.roll(turned, seq - bit, 1), turned)
                bit *= 2
            bias_g = bias_g + jnp.where(top == h, jnp.sum(turned, 0, keepdims=True), 0.0)
        dqkv[0] = (dq * (hd ** -0.5)).astype(BF16)
        dqkv[1] = (dk * (hd ** -0.5)).astype(BF16)
        dqkv[2] = dv.astype(BF16)
        dn1 = nn(dqkv[0], w_qkv[l, 0]) + nn(dqkv[1], w_qkv[l, 1]) + nn(dqkv[2], w_qkv[l, 2])
        red_a[l, 1, 0] = dn1.astype(BF16)
        reduce_start(red_a.at[l, 1], rd_send.at[l, 1], rd_recv.at[l, 1])
        n1 = n_one[l]
        chunk[l, 3 * per:4 * per] = tn(mixed_s[l], da).astype(BF16).reshape(per, rows, width)
        for c in range(3):
            chunk[l, c * per:(c + 1) * per] = tn(dqkv[c], n1).astype(BF16).reshape(per, rows, width)

        @pl.when(p != l)
        def _():
            to_partner(chunk.at[l], chunk_pair, pr_send.at[0], pr_recv.at[0])

        @pl.when((p == 0) & (l == 0))
        def _():
            merge_attn()

        bias_high = bias_g.astype(BF16)
        bias_low = (bias_g - bias_high.astype(F32)).astype(BF16)
        hot_b = hot[...].astype(BF16)
        flat[ne * local + 8:ne * local + 16, 0:hot.shape[1]] = nn(bias_high, hot_b) + nn(bias_low, hot_b)
        h_in = hs[l]
        scale_one = scale_of(h_in)
        dn1 = reduce_end(red_a.at[l, 1], rd_send.at[l, 1], rd_recv.at[l, 1])
        flat[ne * local:ne * local + 1] = jnp.sum(dn1 * h_in * scale_one, 0, keepdims=True)
        for b in range(fold):
            small[l, b * SMALL:(b + 1) * SMALL] = flat[:, b * LANES:(b + 1) * LANES]

        @pl.when(p != l)
        def _():
            to_partner(small.at[l], small_pair, pr_send.at[1], pr_recv.at[1])

        dg = dn1 * gain_one[l]
        dh = dmid + scale_one * dg - h_in * (scale_one * scale_one * scale_one) * jnp.mean(h_in * dg, -1, keepdims=True)
        fin[...] = dh
        g_s[...] = dh.astype(BF16).astype(F32)
        return 0

    lax.fori_loop(0, 2, backward, 0)
    deliver(fin, 0)

    @pl.when(p == 0)
    def _():
        merge_small()
        spread_attn()
        spread_small()

    for k in range(len(weights)):
        lend(k).wait_send()
    for k, ref in enumerate((g_up, g_down)):
        for sem in (gr_loc, gr_send, gr_recv):
            pltpu.make_async_copy(ref.at[0], ref.at[0], sem.at[k]).wait()
    for sem in (sec_loc, sec_send, sec_recv):
        pltpu.make_async_copy(fin, fin, sem).wait()
    for k, (pair, whole, arrived_at) in enumerate(((chunk_pair, total, chunk_in), (small_pair, total_small, small_in))):
        pltpu.make_async_copy(pair, pair, pr_send.at[k]).wait()
        pltpu.make_async_copy(whole, whole, ag_loc.at[k]).wait()
        part = arrived_at.at[pl.ds(1, ne - 1)]
        pltpu.make_async_copy(part, part, ag_send.at[k]).wait()
        pltpu.make_async_copy(part, part, ag_recv.at[k]).wait()


def body(
    block_input, cotangent, routes, offset_bucket, norm1_gain, qkv_weight, out_weight, bias_table, norm2_gain,
    router_weight, up_weight, down_weight,
):
    ne = lax.axis_size("expert")
    nz = lax.axis_size("tensor")
    micro, seq, width = block_input.shape
    heads, buckets = bias_table.shape[1:]
    local, _, ff = up_weight.shape[1:]
    hw = qkv_weight.shape[3]
    hd = hw // heads
    experts = router_weight.shape[2]
    rows = width // ne
    parts_c = PARTS
    part_w = width // parts_c
    fold = width // LANES
    per = hw // rows
    flat_rows = fold * SMALL // ne
    slots = ne * local * CAP

    any_space = pl.BlockSpec(memory_space=pl.ANY)
    hbm = pl.BlockSpec(memory_space=pltpu.HBM)
    vm = pltpu.VMEM
    dma = pltpu.SemaphoreType.DMA
    sds = jax.ShapeDtypeStruct
    part_w = width // PARTS
    flat = width // LANES * SMALL
    parts_in = (2, 2, PARTS, ne, 2 * CAP, part_w)
    half = (local, width, ff)
    sec, own_up, own_down, recv_up, recv_down, attn, small = pl.pallas_call(
        functools.partial(kernel, (ne, nz, seq, width, local, heads, ff, hd)),
        out_shape=[
            sds((micro, seq, width), F32), sds(half, BF16), sds(half, BF16), sds(half, BF16), sds(half, BF16),
            sds((ne, rows, width), BF16), sds((flat, LANES), F32),
        ],
        in_specs=[hbm] * 12,
        out_specs=[any_space] * 7,
        scratch_shapes=[
            vm((seq, width), BF16), vm((seq, width), BF16), vm((1, seq), jnp.int32), vm((seq, buckets), F32),
            vm((2, 2, seq), jnp.int32), vm((2, 1, width), F32), vm((2, 1, width), F32), vm((2, heads, 1, buckets), F32),
            vm((2, experts, width), F32), vm((2, 3, hw, width), BF16),
            vm((2, hw, width), BF16), vm((2, local, width, ff), BF16), vm((2, local, ff, width), BF16),
            vm((3, seq, width), F32), vm((2, seq, width), BF16), vm((2, 3, seq, hw), BF16),
            vm((2, heads, seq, seq), F32), vm((2, seq, hw), BF16), vm((2, seq, width), F32), vm((2, seq, width), BF16),
            vm((2, 2 * seq, slots), BF16), vm((2, seq, experts), F32), vm((2, local, ne * CAP, width), BF16),
            vm((2, local, ne * CAP, ff), F32),
            vm((local, ne * CAP, width), BF16), vm((local, ne * CAP, ff), BF16), vm((2, local, ne * CAP, ff), BF16),
            vm((seq, width), F32), vm((seq, width), F32), vm((3, seq, hw), BF16),
            vm((2, ne, 2 * CAP, width), BF16), vm((2, 2, ne, 2 * CAP, width), BF16), vm((ne, 2 * CAP, LANES), BF16),
            vm((ne, 2 * CAP, LANES), BF16), vm(parts_in[2:], BF16), vm(parts_in, BF16),
            vm((2, 2, nz, seq, width), BF16), vm((2, 2, PARTS, nz, seq, part_w), BF16), vm((2, nz, seq, LANES), BF16),
            vm((2, *half), BF16), vm((2, *half), BF16), vm((2, ne, rows, width), BF16), vm((ne, rows, width), BF16),
            vm((ne, rows, width), BF16), vm((SMALL, width), F32), vm((2, flat, LANES), F32), vm((flat, LANES), F32),
            vm((ne, flat // ne, LANES), F32), vm((rows, width), BF16), vm((flat // ne, LANES), F32),
            dma((3,)), dma((9, 2)), dma((9,)), dma((2, 2)), dma((2, 2)), dma, dma, dma((2, 2, PARTS)), dma((2, 2, PARTS)),
            dma((2, 3)), dma((2, 3)), dma((2, 2, PARTS)), dma((2, 2, PARTS)), dma((2,)), dma((2,)), dma((2,)),
            dma((2,)), dma((2,)), dma((2,)), dma((2,)), dma((2,)), dma((2,)), dma((2,)), dma, dma, dma,
        ],
        compiler_params=pltpu.CompilerParams(
            collective_id=0, has_side_effects=True, vmem_limit_bytes=VMEM_MB * 1024 * 1024),
        cost_estimate=pl.CostEstimate(flops=20_000_000_000, bytes_accessed=40_000_000, transcendentals=2_000_000),
    )(
        block_input, cotangent, routes[0].transpose(0, 2, 1), offset_bucket[None], norm1_gain, norm2_gain,
        bias_table.transpose(1, 0, 2), router_weight[0].T, qkv_weight[0].transpose(0, 2, 1), out_weight[0],
        up_weight[0], down_weight[0],
    )
    grad_up = own_up.astype(F32) + recv_up.astype(F32)
    grad_down = own_down.astype(F32) + recv_down.astype(F32)
    attn = attn.reshape(4, hw, width).astype(F32)
    small = small.reshape(width // LANES, SMALL, LANES).transpose(1, 0, 2).reshape(SMALL, width)
    return (
        sec[None], small[experts][None], attn[None, :3].transpose(0, 1, 3, 2), attn[3][None],
        small[None, experts + 8:experts + 8 + heads, :buckets], small[experts + 1][None], small[:experts].T[None],
        grad_up[None], grad_down[None],
    )


def solution(mesh):
    in_specs = (
        P(None, "expert", None), P(None, "expert", None), P("pipe", None, "expert", None), P(), P("pipe", None),
        P("pipe", None, None, "tensor"), P("pipe", "tensor", None), P("pipe", "tensor", None), P("pipe", None),
        P("pipe", None, None), P("pipe", "expert", None, "tensor"), P("pipe", "expert", "tensor", None),
    )
    out_specs = (
        P("pipe", None, "expert", None), P("pipe", None), P("pipe", None, None, "tensor"), P("pipe", "tensor", None),
        P("pipe", "tensor", None), P("pipe", None), P("pipe", None, None), P("pipe", "expert", None, "tensor"),
        P("pipe", "expert", "tensor", None),
    )
    return jax.shard_map(body, mesh=mesh, in_specs=in_specs, out_specs=out_specs, check_vma=False)
```

```python
import functools

import jax
import jax.numpy as jnp
from jax import lax
from jax.experimental import pallas as pl
from jax.experimental.pallas import tpu as pltpu
from jax.sharding import PartitionSpec as P

EPS = 1e-06
MASKED = -1e30
MESH = pl.DeviceIdType.MESH
F32 = jnp.float32
BF16 = jnp.bfloat16
LANES = 128
CAP = 8
PARTS = 3
SMALL = 64
VMEM_MB = 60
TANH_A = 0.7978845608
TANH_B = 0.044715


def dot(a, b, left, right):
    return lax.dot_general(a, b, (((left,), (right,)), ((), ())), preferred_element_type=F32)


def nn(a, b):
    return dot(a, b, 1, 0)


def nt(a, b):
    return dot(a, b, 1, 1)


def tn(a, b):
    return dot(a, b, 0, 0)


def lanes_of(shape, dim):
    return lax.broadcasted_iota(jnp.int32, shape, dim)


def kernel(
    dims,
    x_in, cot_in, routes_in, bucket_in, one_in, two_in, bias_in, router_in, qkv_in, out_in, up_in, down_in,
    sec_out, own_up, own_down, recv_up, recv_down, attn_out, small_out,
    xin, cot, bucket, hot, routes, gain_one, gain_two, bias_w, router, w_qkv, w_full, w_up, w_down,
    hs, n_one, qkv, probs_s, mixed_s, h_mid_s, n_two, comb, eprobs, x_s, u_s, x_dy, x_du, hid_s, g_s, fin, dqkv,
    send_a, recv_a, send_g, recv_g, send_c, recv_c, mix, red_a, red_c, red_g, g_up, g_down, chunk, chunk_pair, chunk_in, flat, small, small_pair,
    small_in, total, total_small,
    sem_in, sem_w, sem_ws, wo_send, wo_recv, mx_send, mx_recv, sa_send, sa_recv, sg_send, sg_recv, sc_send, sc_recv, rd_send, rd_recv, rc_send, rc_recv, gr_send, gr_recv, gr_loc,
    ck_send, ck_recv, pr_send, pr_recv, ag_send, ag_recv, ag_loc, sec_send, sec_recv, sec_loc,
):
    ne, nz, seq, width, local, heads, ff, hd = dims
    p = lax.axis_index("pipe")
    x = lax.axis_index("expert")
    z = lax.axis_index("tensor")
    other = 1 - p
    slots = ne * 2 * CAP
    hw = heads * hd
    rows = width // ne
    parts_c = PARTS
    part_w = width // parts_c
    fold = width // LANES
    per = hw // rows
    flat_rows = fold * SMALL // ne

    barrier = pltpu.get_barrier_semaphore()

    def hello_e(r, _):
        pl.semaphore_signal(barrier, inc=1, device_id={"expert": lax.rem(x + r, ne)}, device_id_type=MESH)
        return 0

    def hello_z(r, _):
        pl.semaphore_signal(barrier, inc=1, device_id={"tensor": lax.rem(z + r, nz)}, device_id_type=MESH)
        return 0

    lax.fori_loop(1, ne, hello_e, 0)
    lax.fori_loop(1, nz, hello_z, 0)
    pl.semaphore_signal(barrier, inc=1, device_id={"pipe": other}, device_id_type=MESH)

    ins = [
        pltpu.make_async_copy(x_in.at[p], xin, sem_in.at[0]),
        pltpu.make_async_copy(cot_in.at[p], cot, sem_in.at[1]),
        pltpu.make_async_copy(bucket_in, bucket, sem_in.at[2]),
    ]
    for copy in ins:
        copy.start()
    weights = [
        (one_in, gain_one), (qkv_in, w_qkv), (bias_in, bias_w), (w_full, w_full), (routes_in, routes), (router_in, router),
        (two_in, gain_two), (up_in, w_up), (down_in, w_down),
    ]
    def load(k):
        src, dst = weights[k]
        pltpu.make_async_copy(src.at[p] if k == 4 else src, dst.at[p], sem_w.at[k, p]).start()

    def lend(k):
        src, dst = weights[k]
        return pltpu.make_async_remote_copy(
            src_ref=src.at[other] if k == 4 else src.at[p] if k == 3 else src, dst_ref=dst.at[p], send_sem=sem_ws.at[k], recv_sem=sem_w.at[k, p],
            device_id={"pipe": other}, device_id_type=MESH)

    def gather_start():
        pltpu.make_async_copy(out_in, w_full.at[p, z], sem_in.at[3]).start()

        def one(r, _):
            pltpu.make_async_remote_copy(
                src_ref=out_in, dst_ref=w_full.at[p, z], send_sem=wo_send, recv_sem=wo_recv,
                device_id={"tensor": lax.rem(z + r, nz)}, device_id_type=MESH).start()
            return 0
        lax.fori_loop(1, nz, one, 0)

    def gather_end():
        pltpu.make_async_copy(out_in, w_full.at[p, z], sem_in.at[3]).wait()
        part = w_full.at[p, pl.ds(1, nz - 1)]
        pltpu.make_async_copy(part, part, wo_send).wait()
        pltpu.make_async_copy(part, part, wo_recv).wait()
        lend(3).start()

    load(4)

    @pl.when(p == 0)
    def _():
        for k in (0, 1, 2, 5, 6):
            load(k)
    pl.semaphore_wait(barrier, ne - 1 + nz - 1 + 1)
    lend(4).start()

    @pl.when(p == 0)
    def _():
        gather_start()
        for k in (0, 1, 2, 5, 6, 7, 8):
            lend(k).start()
        for k in (7, 8):
            load(k)

    def await_weight(k, l):
        dst = weights[k][1]
        pltpu.make_async_copy(dst.at[l], dst.at[l], sem_w.at[k, l]).wait()

    def send_all(src, dst, send, recv, forth):
        def one(r, _):
            pltpu.make_async_remote_copy(
                src_ref=src.at[r], dst_ref=dst.at[r], send_sem=send, recv_sem=recv,
                device_id={"expert": lax.rem(x + r if forth else x + ne - r, ne)}, device_id_type=MESH).start()
            return 0
        lax.fori_loop(1, ne, one, 0)
        dst[0] = src[0]

    def await_all(src, dst, send, recv):
        part = src.at[pl.ds(1, ne - 1)]
        pltpu.make_async_copy(part, part, send).wait()
        part = dst.at[pl.ds(1, ne - 1)]
        pltpu.make_async_copy(part, part, recv).wait()

    def exchange(kind, l):
        send_all(send_a.at[kind], recv_a.at[l, kind], sa_send.at[l, kind], sa_recv.at[l, kind], True)

    def arrived(kind, l):
        await_all(send_a.at[kind], recv_a.at[l, kind], sa_send.at[l, kind], sa_recv.at[l, kind])
        return recv_a[l, kind]

    def exchange_back(kind, l, c):
        send_all(send_c.at[c], recv_c.at[l, kind, c], sc_send.at[l, kind, c], sc_recv.at[l, kind, c], False)

    def arrived_back(kind, l, c):
        await_all(send_c.at[c], recv_c.at[l, kind, c], sc_send.at[l, kind, c], sc_recv.at[l, kind, c])
        return recv_c[l, kind, c].reshape(slots, part_w)

    def reduce_start(buf, send, recv):
        def one(r, _):
            pltpu.make_async_remote_copy(
                src_ref=buf.at[0], dst_ref=buf.at[r], send_sem=send, recv_sem=recv,
                device_id={"tensor": lax.rem(z + r, nz)}, device_id_type=MESH).start()
            return 0
        lax.fori_loop(1, nz, one, 0)

    def reduce_end(buf, send, recv):
        part = buf.at[pl.ds(1, nz - 1)]
        pltpu.make_async_copy(part, part, send).wait()
        pltpu.make_async_copy(part, part, recv).wait()
        acc = None
        for a in range(nz):
            term = buf[lax.rem(z + nz - a, nz)].astype(F32)
            acc = term if acc is None else acc + term
        return acc

    def summed_back(kind, l, weigh):
        for c in range(parts_c):
            red_c[l, kind, c, 0] = weigh(arrived_back(kind, l, c)).astype(BF16)
            reduce_start(red_c.at[l, kind, c], rc_send.at[l, kind, c], rc_recv.at[l, kind, c])
        return lambda: jnp.concatenate(
            [reduce_end(red_c.at[l, kind, c], rc_send.at[l, kind, c], rc_recv.at[l, kind, c]) for c in range(parts_c)], axis=1)

    def split(blocks):
        wide = blocks.astype(F32)
        return [wide[:, e * CAP:(e + 1) * CAP].reshape(ne * CAP, width).astype(BF16) for e in range(local)]

    def join(parts):
        return jnp.concatenate([part.reshape(ne, CAP, part_w) for part in parts], axis=1).astype(BF16)

    def head_mask(h):
        at = lanes_of((1, hw), 1)
        return ((at >= h * hd) & (at < (h + 1) * hd)).astype(BF16)

    def scale_of(h):
        return lax.rsqrt(jnp.mean(h * h, -1, keepdims=True) + EPS)

    def column(row):
        eye = lanes_of((seq, seq), 0) == lanes_of((seq, seq), 1)
        return jnp.sum(jnp.where(eye, row.astype(F32), 0.0), -1, keepdims=True)

    def chosen_of(ids):
        at = lanes_of((seq, ne * local), 1)
        return [(at == e).astype(F32) for e in ids]

    def named(l):
        return [column(routes[l, k:k + 1]).astype(jnp.int32) for k in range(2)]

    def router_of(l):
        r = router[l]
        high = r.astype(BF16)
        return high, (r - high.astype(F32)).astype(BF16)

    def place(l):
        ids = named(l)
        hot_e = chosen_of(ids)
        row_at, col_at = lanes_of((seq, seq), 0), lanes_of((seq, seq), 1)
        earlier = (row_at > col_at).astype(BF16)
        count = nn(earlier, (hot_e[0] + hot_e[1]).astype(BF16))
        for kk in range(2):
            before = count if kk == 0 else count + hot_e[0]
            c = jnp.sum(before * hot_e[kk], -1, keepdims=True).astype(jnp.int32)
            e = ids[kk]
            at = (((e >> 1) - x + ne) & (ne - 1)) * (2 * CAP) + (e & 1) * CAP + c
            comb[l, kk * seq:(kk + 1) * seq] = (lanes_of((seq, slots), 1) == at).astype(F32).astype(BF16)

    def forward(l, _):
        h_in = hs[l]
        await_weight(0, l)
        n1 = (h_in * scale_of(h_in) * gain_one[l]).astype(BF16)
        n_one[l] = n1
        await_weight(1, l)
        for c in range(3):
            qkv[l, c] = nt(n1, w_qkv[l, c]).astype(BF16)
        q, k, v = qkv[l, 0], qkv[l, 1], qkv[l, 2]
        await_weight(2, l)
        causal = lanes_of((seq, seq), 0) >= lanes_of((seq, seq), 1)
        mixed = jnp.zeros((seq, hw), F32)
        for h in range(heads):
            mask = head_mask(h)
            rel = lax.dot_general(
                jnp.broadcast_to(bias_w[l, h], (8, hot.shape[1])), hot[...], (((1,), (1,)), ((), ())),
                precision=lax.Precision.HIGHEST, preferred_element_type=F32)
            bias = pltpu.roll(jnp.broadcast_to(rel[0:1], (seq, seq)), 0, 1, stride=1, stride_axis=0)
            s = nt(q * mask, k) * (hd ** -0.5) + bias
            s = jnp.where(causal, s, MASKED)
            e = jnp.exp(s - jnp.max(s, -1, keepdims=True))
            prob = e / jnp.sum(e, -1, keepdims=True)
            probs_s[l, h] = prob
            mixed = mixed + nn(prob.astype(BF16), v * mask)
        mixed = mixed.astype(BF16)
        mixed_s[l] = mixed
        mix[l, 0] = mixed
        reduce_start(mix.at[l], mx_send.at[l], mx_recv.at[l])

        @pl.when(l == 0)
        def _():
            @pl.when(p == 1)
            def _():
                gather_start()
                for k in (0, 1, 2, 5, 6, 7, 8):
                    lend(k).start()
                    load(k)
            for layer in range(2):
                await_weight(4, layer)
                place(layer)
            send_a[1] = tn(comb[1, 0:seq] + comb[1, seq:2 * seq], cot[...]).astype(BF16).reshape(ne, 2 * CAP, width)
            exchange(1, 1)

        hot_e = chosen_of(named(l))
        both = comb[l, 0:seq] + comb[l, seq:2 * seq]
        await_weight(5, l)
        await_weight(6, l)

        @pl.when((p == 0) & (l == 0))
        def _():
            gather_end()

        @pl.when(l != p)
        def _():
            await_weight(3, l)

        part = mix.at[l, pl.ds(1, nz - 1)]
        pltpu.make_async_copy(part, part, mx_send.at[l]).wait()
        pltpu.make_async_copy(part, part, mx_recv.at[l]).wait()
        attn = None
        for a in range(nz):
            term = nn(mix[l, lax.rem(z + nz - a, nz)], w_full[l, a])
            attn = term if attn is None else attn + term
        h_mid = h_in + attn
        h_mid_s[l] = h_mid
        n2 = (h_mid * scale_of(h_mid) * gain_two[l]).astype(BF16)
        n_two[l] = n2
        send_a[0] = tn(both, n2).astype(BF16).reshape(ne, 2 * CAP, width)
        exchange(0, l)
        high, low = router_of(l)
        logits = nt(n2, high) + nt(n2, low)
        e = jnp.exp(logits - jnp.max(logits, -1, keepdims=True))
        ep = e / jnp.sum(e, -1, keepdims=True)
        eprobs[l] = ep
        picked = [jnp.sum(ep * hot_e[kk], -1, keepdims=True) for kk in range(2)]
        inv = picked[0] + picked[1]
        gates = [picked[kk] / inv for kk in range(2)]

        @pl.when(l == 1)
        def _():
            at = lanes_of((seq, LANES), 1)
            sent = []
            for kk in range(2):
                top = gates[kk].astype(BF16).astype(F32)
                sent.append(jnp.where(at == 0, top, jnp.where(at == 1, gates[kk] - top, 0.0)).astype(BF16))
            send_g[...] = tn(comb[l], jnp.concatenate(sent, axis=0)).astype(BF16).reshape(ne, 2 * CAP, LANES)
            send_all(send_g, recv_g, sg_send, sg_recv, True)

        await_weight(7, l)
        await_weight(8, l)
        parts = split(arrived(0, l))
        for e in range(local):
            x_s[l, e] = parts[e]

        def expert(e, _):
            u = nn(x_s[l, e], w_up[l, e])
            u_s[l, e] = u
            t = jnp.tanh(TANH_A * (u + TANH_B * u * u * u))
            hid_s[l, e] = (0.5 * u * (1.0 + t)).astype(BF16)
            return 0
        lax.fori_loop(0, local, expert, 0)
        for c in range(parts_c):
            cols = slice(c * part_w, (c + 1) * part_w)
            send_c[c] = join([nn(hid_s[l, e], w_down[l, e, :, cols]) for e in range(local)])
            exchange_back(0, l, c)

        @pl.when((p == 1) & (l == 0))
        def _():
            gather_end()

        def slopes(e, _):
            u = u_s[l, e]
            t = jnp.tanh(TANH_A * (u + TANH_B * u * u * u))
            u_s[l, e] = 0.5 * (1.0 + t) + (0.5 * TANH_A) * u * (1.0 - t * t) * (1.0 + (3.0 * TANH_B) * u * u)
            return 0
        lax.fori_loop(0, local, slopes, 0)
        out = summed_back(0, l, lambda back: gates[0] * nn(comb[l, 0:seq], back) + gates[1] * nn(comb[l, seq:2 * seq], back))
        out = h_mid + out()
        hs[l + 1] = jnp.where(l == 0, out.astype(BF16).astype(F32), out)
        return 0

    for copy in ins:
        copy.wait()
    hs[0] = xin[...].astype(F32)
    turn_at, turn_of = lanes_of((seq, seq), 0), lanes_of((seq, seq), 1)
    turned_bucket = jnp.where((turn_at + turn_of == 0) | (turn_at + turn_of == seq), bucket[...].astype(F32), 0.0)
    turned_bucket = jnp.sum(turned_bucket, -1, keepdims=True).astype(jnp.int32)
    hot[...] = (turned_bucket == lanes_of(hot.shape, 1)).astype(F32)
    lax.fori_loop(0, 2, forward, 0)

    def deliver(src, owner):
        @pl.when(p == owner)
        def _():
            pltpu.make_async_copy(src, sec_out.at[p], sec_loc).start()

        @pl.when(p != owner)
        def _():
            pltpu.make_async_remote_copy(
                src_ref=src, dst_ref=sec_out.at[p], send_sem=sec_send, recv_sem=sec_recv,
                device_id={"pipe": other}, device_id_type=MESH).start()

    def piece(ref, j):
        return ref.at[pl.ds(pl.multiple_of(j * flat_rows, 8), flat_rows)]

    def merge_attn():
        pltpu.make_async_copy(chunk_pair, chunk_pair, pr_recv.at[0]).wait()
        for c in range(parts_c):
            chunk_pair[c] = (chunk[p, c].astype(F32) + chunk_pair[c].astype(F32)).astype(BF16)

            def scatter(r, _, c=c):
                to = lax.rem(x + r, ne)
                pltpu.make_async_remote_copy(
                    src_ref=chunk_pair.at[c, to], dst_ref=chunk_in.at[c, r], send_sem=ck_send.at[c], recv_sem=ck_recv.at[c],
                    device_id={"expert": to}, device_id_type=MESH).start()
                return 0
            lax.fori_loop(1, ne, scatter, 0)
            chunk_in[c, 0] = chunk_pair[c, x]

    def merge_small():
        pltpu.make_async_copy(small_pair, small_pair, pr_recv.at[1]).wait()
        small_pair[...] = small[p] + small_pair[...]

        def scatter(r, _):
            to = lax.rem(x + r, ne)
            pltpu.make_async_remote_copy(
                src_ref=piece(small_pair, to), dst_ref=small_in.at[r], send_sem=ck_send.at[parts_c], recv_sem=ck_recv.at[parts_c],
                device_id={"expert": to}, device_id_type=MESH).start()
            return 0
        lax.fori_loop(1, ne, scatter, 0)
        small_in[0] = small_pair[pl.ds(pl.multiple_of(x * flat_rows, 8), flat_rows)]

    def spread(k, arrived_at, whole, dst):
        part = arrived_at.at[pl.ds(1, ne - 1)]
        pltpu.make_async_copy(part, part, ck_send.at[k]).wait()
        pltpu.make_async_copy(part, part, ck_recv.at[k]).wait()
        acc = arrived_at[0].astype(F32)
        for r in range(1, ne):
            acc = acc + arrived_at[r].astype(F32)
        whole[...] = acc.astype(whole.dtype)
        pltpu.make_async_copy(whole, dst, ag_loc.at[k]).start()

        def one(r, _):
            pltpu.make_async_remote_copy(
                src_ref=whole, dst_ref=dst, send_sem=ag_send.at[k], recv_sem=ag_recv.at[k],
                device_id={"expert": lax.rem(x + r, ne)}, device_id_type=MESH).start()
            return 0
        lax.fori_loop(1, ne, one, 0)

    def spread_attn():
        for c in range(parts_c):
            spread(c, chunk_in.at[c], total.at[c], attn_out.at[x, :, pl.ds(c * part_w, part_w)])

    def spread_small():
        spread(parts_c, small_in, total_small, piece(small_out, x))

    def to_partner(src, dst, send, recv):
        pltpu.make_async_remote_copy(
            src_ref=src, dst_ref=dst, send_sem=send, recv_sem=recv, device_id={"pipe": other}, device_id_type=MESH).start()

    part = send_a.at[1, pl.ds(1, ne - 1)]
    pltpu.make_async_copy(part, part, sa_send.at[1, 1]).wait()
    deliver(hs.at[2], 1)
    g_s[...] = cot[...].astype(F32)

    def keep_grad(l, k, value):
        value = value.astype(BF16)
        for c in range(parts_c):
            chunk[l, c, k * per:(k + 1) * per] = value[:, c * part_w:(c + 1) * part_w].reshape(per, rows, part_w)

    def backward(i, _):
        l = 1 - i
        g = g_s[...]
        hot_e = chosen_of(named(l))
        ep = eprobs[l]
        picked = [jnp.sum(ep * hot_e[kk], -1, keepdims=True) for kk in range(2)]
        inv = picked[0] + picked[1]
        gates = [picked[kk] / inv for kk in range(2)]
        at = lanes_of((seq, LANES), 1)

        @pl.when(l == 0)
        def _():
            dy = jnp.concatenate([(gates[kk] * g).astype(BF16) for kk in range(2)], axis=0)
            send_a[1] = tn(comb[l], dy).astype(BF16).reshape(ne, 2 * CAP, width)
            exchange(1, l)

            @pl.when(p == 1)
            def _():
                merge_attn()
                merge_small()
            parts = split(arrived(1, l))
            for e in range(local):
                x_dy[e] = parts[e]

        @pl.when(l == 1)
        def _():
            await_all(send_g, recv_g, sg_send, sg_recv)
            weigh = jnp.sum(recv_g[...].astype(F32), -1, keepdims=True)
            part = recv_a.at[l, 1, pl.ds(1, ne - 1)]
            pltpu.make_async_copy(part, part, sa_recv.at[l, 1]).wait()
            wide = recv_a[l, 1].astype(F32) * weigh
            for e in range(local):
                x_dy[e] = wide[:, e * CAP:(e + 1) * CAP].reshape(ne * CAP, width).astype(BF16)

        def expert(e, _):
            dy_e = x_dy[e]
            dh = nt(dy_e, w_down[l, e])
            x_du[e] = (dh * u_s[l, e]).astype(BF16)
            return 0
        lax.fori_loop(0, local, expert, 0)
        for c in range(parts_c):
            cols = slice(c * part_w, (c + 1) * part_w)
            send_c[c] = join([nt(x_du[e], w_up[l, e, cols]) for e in range(local)])
            exchange_back(1, l, c)

        @pl.when((p == 1) & (l == 0))
        def _():
            spread_attn()
            spread_small()

        gg = jnp.zeros((seq, LANES), F32)
        for kk in range(2):
            part = None
            for c in range(parts_c):
                got = nn(comb[l, kk * seq:(kk + 1) * seq], recv_c[l, 0, c].reshape(slots, part_w))
                term = jnp.sum(g[:, c * part_w:(c + 1) * part_w] * got, -1, keepdims=True)
                part = term if part is None else part + term
            high = part.astype(BF16).astype(F32)
            gg = gg + jnp.where(at == kk, high, 0.0) + jnp.where(at == 2 + kk, part - high, 0.0)
        red_g[l, 0] = gg.astype(BF16)
        reduce_start(red_g.at[l], rd_send.at[l, 1], rd_recv.at[l, 1])

        def expert_grads(e, _):
            g_up[l, e] = tn(x_s[l, e], x_du[e]).astype(BF16)
            g_down[l, e] = tn(hid_s[l, e], x_dy[e]).astype(BF16)
            return 0
        lax.fori_loop(0, local, expert_grads, 0)

        both = comb[l, 0:seq] + comb[l, seq:2 * seq]
        dn2 = summed_back(1, l, lambda back: nn(both, back))

        @pl.when(p == l)
        def _():
            pltpu.make_async_copy(g_up.at[l], own_up, gr_loc.at[0]).start()
            pltpu.make_async_copy(g_down.at[l], own_down, gr_loc.at[1]).start()

        @pl.when(p != l)
        def _():
            to_partner(g_up.at[l], recv_up, gr_send.at[0], gr_recv.at[0])
            to_partner(g_down.at[l], recv_down, gr_send.at[1], gr_recv.at[1])

        h_mid = h_mid_s[l]
        scale = scale_of(h_mid)
        tail = reduce_end(red_g.at[l], rd_send.at[l, 1], rd_recv.at[l, 1])
        dn2 = dn2()
        gg = [jnp.sum(jnp.where((at == kk) | (at == 2 + kk), tail, 0.0), -1, keepdims=True) for kk in range(2)]
        centre = gg[0] * gates[0] + gg[1] * gates[1]
        dprob = hot_e[0] * ((gg[0] - centre) / inv) + hot_e[1] * ((gg[1] - centre) / inv)
        dlog = (ep * (dprob - jnp.sum(ep * dprob, -1, keepdims=True))).astype(BF16)
        high, low = router_of(l)
        dn2 = dn2 + nn(dlog, high) + nn(dlog, low)
        flat[...] = jnp.zeros_like(flat)
        flat[0:ne * local] = tn(dlog, n_two[l])
        flat[ne * local + 1:ne * local + 2] = jnp.sum(dn2 * h_mid * scale, 0, keepdims=True)
        dg = dn2 * gain_two[l]
        dmid = g + scale * dg - h_mid * (scale * scale * scale) * jnp.mean(h_mid * dg, -1, keepdims=True)
        da = dmid.astype(BF16)
        dmixed = nt(da, w_full[l, z]).astype(BF16)
        q, k, v = qkv[l, 0], qkv[l, 1], qkv[l, 2]
        dq = jnp.zeros((seq, hw), F32)
        dk = jnp.zeros((seq, hw), F32)
        dv = jnp.zeros((seq, hw), F32)
        causal = lanes_of((seq, seq), 0) >= lanes_of((seq, seq), 1)
        row_at = lanes_of((seq, seq), 0)
        top = lanes_of((8, LANES), 0)
        bias_g = jnp.zeros((8, LANES), F32)
        for h in range(heads):
            mask = head_mask(h)
            prob = probs_s[l, h]
            dm = dmixed * mask
            dp = nt(dm, v)
            dv = dv + tn(prob.astype(BF16), dm)
            ds = jnp.where(causal, prob * (dp - jnp.sum(prob * dp, -1, keepdims=True)), 0.0).astype(BF16)
            dq = dq + nn(ds, k * mask)
            dk = dk + tn(ds, q * mask)
            turned = ds.astype(F32)
            bit = 1
            while bit < seq:
                turned = jnp.where((row_at & bit) != 0, pltpu.roll(turned, seq - bit, 1), turned)
                bit *= 2
            bias_g = bias_g + jnp.where(top == h, jnp.sum(turned, 0, keepdims=True), 0.0)
        dqkv[0] = (dq * (hd ** -0.5)).astype(BF16)
        dqkv[1] = (dk * (hd ** -0.5)).astype(BF16)
        dqkv[2] = dv.astype(BF16)
        dn1 = nn(dqkv[0], w_qkv[l, 0]) + nn(dqkv[1], w_qkv[l, 1]) + nn(dqkv[2], w_qkv[l, 2])
        red_a[l, 0] = dn1.astype(BF16)
        reduce_start(red_a.at[l], rd_send.at[l, 0], rd_recv.at[l, 0])
        n1 = n_one[l]
        keep_grad(l, 3, tn(mixed_s[l], da))
        for c in range(3):
            keep_grad(l, c, tn(dqkv[c], n1))

        @pl.when(p != l)
        def _():
            to_partner(chunk.at[l], chunk_pair, pr_send.at[0], pr_recv.at[0])

        @pl.when((p == 0) & (l == 0))
        def _():
            merge_attn()

        bias_high = bias_g.astype(BF16)
        bias_low = (bias_g - bias_high.astype(F32)).astype(BF16)
        hot_b = hot[...].astype(BF16)
        flat[ne * local + 8:ne * local + 16, 0:hot.shape[1]] = nn(bias_high, hot_b) + nn(bias_low, hot_b)
        h_in = hs[l]
        scale_one = scale_of(h_in)
        dn1 = reduce_end(red_a.at[l], rd_send.at[l, 0], rd_recv.at[l, 0])
        flat[ne * local:ne * local + 1] = jnp.sum(dn1 * h_in * scale_one, 0, keepdims=True)
        for b in range(fold):
            small[l, b * SMALL:(b + 1) * SMALL] = flat[:, b * LANES:(b + 1) * LANES]

        @pl.when(p != l)
        def _():
            to_partner(small.at[l], small_pair, pr_send.at[1], pr_recv.at[1])

        dg = dn1 * gain_one[l]
        dh = dmid + scale_one * dg - h_in * (scale_one * scale_one * scale_one) * jnp.mean(h_in * dg, -1, keepdims=True)
        fin[...] = dh
        g_s[...] = dh.astype(BF16).astype(F32)
        return 0

    lax.fori_loop(0, 2, backward, 0)
    deliver(fin, 0)

    @pl.when(p == 0)
    def _():
        merge_small()
        spread_attn()
        spread_small()

    for k in range(len(weights)):
        lend(k).wait_send()
    for k, ref in enumerate((g_up, g_down)):
        for sem in (gr_loc, gr_send, gr_recv):
            pltpu.make_async_copy(ref.at[0], ref.at[0], sem.at[k]).wait()
    for sem in (sec_loc, sec_send, sec_recv):
        pltpu.make_async_copy(fin, fin, sem).wait()
    for k, pair in enumerate((chunk_pair, small_pair)):
        pltpu.make_async_copy(pair, pair, pr_send.at[k]).wait()
    for k in range(parts_c + 1):
        whole, arrived_at = (total.at[k], chunk_in.at[k]) if k < parts_c else (total_small, small_in)
        pltpu.make_async_copy(whole, whole, ag_loc.at[k]).wait()
        part = arrived_at.at[pl.ds(1, ne - 1)]
        pltpu.make_async_copy(part, part, ag_send.at[k]).wait()
        pltpu.make_async_copy(part, part, ag_recv.at[k]).wait()


def body(
    block_input, cotangent, routes, offset_bucket, norm1_gain, qkv_weight, out_weight, bias_table, norm2_gain,
    router_weight, up_weight, down_weight,
):
    ne = lax.axis_size("expert")
    nz = lax.axis_size("tensor")
    micro, seq, width = block_input.shape
    heads, buckets = bias_table.shape[1:]
    local, _, ff = up_weight.shape[1:]
    hw = qkv_weight.shape[3]
    hd = hw // heads
    experts = router_weight.shape[2]
    rows = width // ne
    parts_c = PARTS
    part_w = width // parts_c
    fold = width // LANES
    per = hw // rows
    flat_rows = fold * SMALL // ne
    slots = ne * local * CAP

    any_space = pl.BlockSpec(memory_space=pl.ANY)
    hbm = pl.BlockSpec(memory_space=pltpu.HBM)
    vm = pltpu.VMEM
    dma = pltpu.SemaphoreType.DMA
    sds = jax.ShapeDtypeStruct
    part_w = width // PARTS
    flat = width // LANES * SMALL
    parts_in = (2, 2, PARTS, ne, 2 * CAP, part_w)
    half = (local, width, ff)
    cut = (PARTS, ne, rows, part_w)
    sec, own_up, own_down, recv_up, recv_down, attn, small = pl.pallas_call(
        functools.partial(kernel, (ne, nz, seq, width, local, heads, ff, hd)),
        out_shape=[
            sds((micro, seq, width), F32), sds(half, BF16), sds(half, BF16), sds(half, BF16), sds(half, BF16),
            sds((ne, rows, width), BF16), sds((flat, LANES), F32),
        ],
        in_specs=[hbm] * 12,
        out_specs=[any_space] * 7,
        scratch_shapes=[
            vm((seq, width), BF16), vm((seq, width), BF16), vm((1, seq), jnp.int32), vm((seq, buckets), F32),
            vm((2, 2, seq), jnp.int32), vm((2, 1, width), F32), vm((2, 1, width), F32), vm((2, heads, 1, buckets), F32),
            vm((2, experts, width), F32), vm((2, 3, hw, width), BF16),
            vm((2, nz, hw, width), BF16), vm((2, local, width, ff), BF16), vm((2, local, ff, width), BF16),
            vm((3, seq, width), F32), vm((2, seq, width), BF16), vm((2, 3, seq, hw), BF16),
            vm((2, heads, seq, seq), F32), vm((2, seq, hw), BF16), vm((2, seq, width), F32), vm((2, seq, width), BF16),
            vm((2, 2 * seq, slots), BF16), vm((2, seq, experts), F32), vm((2, local, ne * CAP, width), BF16),
            vm((2, local, ne * CAP, ff), F32),
            vm((local, ne * CAP, width), BF16), vm((local, ne * CAP, ff), BF16), vm((2, local, ne * CAP, ff), BF16),
            vm((seq, width), F32), vm((seq, width), F32), vm((3, seq, hw), BF16),
            vm((2, ne, 2 * CAP, width), BF16), vm((2, 2, ne, 2 * CAP, width), BF16), vm((ne, 2 * CAP, LANES), BF16),
            vm((ne, 2 * CAP, LANES), BF16), vm(parts_in[2:], BF16), vm(parts_in, BF16),
            vm((2, nz, seq, hw), BF16), vm((2, nz, seq, width), BF16), vm((2, 2, PARTS, nz, seq, part_w), BF16), vm((2, nz, seq, LANES), BF16),
            vm((2, *half), BF16), vm((2, *half), BF16), vm((2, *cut), BF16), vm(cut, BF16),
            vm(cut, BF16), vm((SMALL, width), F32), vm((2, flat, LANES), F32), vm((flat, LANES), F32),
            vm((ne, flat // ne, LANES), F32), vm((PARTS, rows, part_w), BF16), vm((flat // ne, LANES), F32),
            dma((4,)), dma((9, 2)), dma((9,)), dma, dma, dma((2,)), dma((2,)), dma((2, 2)), dma((2, 2)), dma, dma, dma((2, 2, PARTS)), dma((2, 2, PARTS)),
            dma((2, 2)), dma((2, 2)), dma((2, 2, PARTS)), dma((2, 2, PARTS)), dma((2,)), dma((2,)), dma((2,)),
            dma((PARTS + 1,)), dma((PARTS + 1,)), dma((2,)), dma((2,)), dma((PARTS + 1,)), dma((PARTS + 1,)), dma((PARTS + 1,)),
            dma, dma, dma,
        ],
        compiler_params=pltpu.CompilerParams(
            collective_id=0, has_side_effects=True, vmem_limit_bytes=VMEM_MB * 1024 * 1024),
        cost_estimate=pl.CostEstimate(flops=20_000_000_000, bytes_accessed=40_000_000, transcendentals=2_000_000),
    )(
        block_input, cotangent, routes[0].transpose(0, 2, 1), offset_bucket[None], norm1_gain, norm2_gain,
        bias_table.transpose(1, 0, 2), router_weight[0].T, qkv_weight[0].transpose(0, 2, 1), out_weight[0],
        up_weight[0], down_weight[0],
    )
    grad_up = own_up.astype(F32) + recv_up.astype(F32)
    grad_down = own_down.astype(F32) + recv_down.astype(F32)
    attn = attn.reshape(4, hw, width).astype(F32)
    small = small.reshape(width // LANES, SMALL, LANES).transpose(1, 0, 2).reshape(SMALL, width)
    return (
        sec[None], small[experts][None], attn[None, :3].transpose(0, 1, 3, 2), attn[3][None],
        small[None, experts + 8:experts + 8 + heads, :buckets], small[experts + 1][None], small[:experts].T[None],
        grad_up[None], grad_down[None],
    )


def solution(mesh):
    in_specs = (
        P(None, "expert", None), P(None, "expert", None), P("pipe", None, "expert", None), P(), P("pipe", None),
        P("pipe", None, None, "tensor"), P("pipe", "tensor", None), P("pipe", "tensor", None), P("pipe", None),
        P("pipe", None, None), P("pipe", "expert", None, "tensor"), P("pipe", "expert", "tensor", None),
    )
    out_specs = (
        P("pipe", None, "expert", None), P("pipe", None), P("pipe", None, None, "tensor"), P("pipe", "tensor", None),
        P("pipe", "tensor", None), P("pipe", None), P("pipe", None, None), P("pipe", "expert", None, "tensor"),
        P("pipe", "expert", "tensor", None),
    )
    return jax.shard_map(body, mesh=mesh, in_specs=in_specs, out_specs=out_specs, check_vma=False)
```

```python
import functools

import jax
import jax.numpy as jnp
from jax import lax
from jax.experimental import pallas as pl
from jax.experimental.pallas import tpu as pltpu
from jax.sharding import PartitionSpec as P

EPS = 1e-06
MASKED = -1e30
MESH = pl.DeviceIdType.MESH
F32 = jnp.float32
BF16 = jnp.bfloat16
LANES = 128
CAP = 8
PARTS = 3
SMALL = 64
VMEM_MB = 60
TANH_A = 0.7978845608
TANH_B = 0.044715


def dot(a, b, left, right):
    return lax.dot_general(a, b, (((left,), (right,)), ((), ())), preferred_element_type=F32)


def nn(a, b):
    return dot(a, b, 1, 0)


def nt(a, b):
    return dot(a, b, 1, 1)


def tn(a, b):
    return dot(a, b, 0, 0)


def lanes_of(shape, dim):
    return lax.broadcasted_iota(jnp.int32, shape, dim)


def kernel(
    dims,
    x_in, cot_in, routes_in, bucket_in, one_in, two_in, bias_in, router_in, qkv_in, out_in, up_in, down_in,
    sec_out, own_up, own_down, recv_up, recv_down, attn_out, small_out,
    xin, cot, bucket, hot, routes, gain_one, gain_two, bias_w, router, w_qkv, w_full, w_up, w_down,
    hs, n_one, qkv, probs_s, mixed_s, h_mid_s, n_two, comb, eprobs, x_s, u_s, x_dy, x_du, hid_s, g_s, fin, dqkv,
    send_a, recv_a, send_g, recv_g, send_c, recv_c, mix, red_a, red_c, red_g, g_up, g_down, chunk, chunk_pair, chunk_in, flat, small, small_pair,
    small_in, total, total_small,
    sem_in, sem_w, sem_ws, wo_send, wo_recv, mx_send, mx_recv, sa_send, sa_recv, sg_send, sg_recv, sc_send, sc_recv, rd_send, rd_recv, rc_send, rc_recv, gr_send, gr_recv, gr_loc,
    ck_send, ck_recv, pr_send, pr_recv, ag_send, ag_recv, ag_loc, sec_send, sec_recv, sec_loc,
):
    ne, nz, seq, width, local, heads, ff, hd = dims
    p = lax.axis_index("pipe")
    x = lax.axis_index("expert")
    z = lax.axis_index("tensor")
    other = 1 - p
    slots = ne * 2 * CAP
    hw = heads * hd
    rows = width // ne
    parts_c = PARTS
    part_w = width // parts_c
    fold = width // LANES
    per = hw // rows
    flat_rows = fold * SMALL // ne

    barrier = pltpu.get_barrier_semaphore()

    def hello_e(r, _):
        pl.semaphore_signal(barrier, inc=1, device_id={"expert": lax.rem(x + r, ne)}, device_id_type=MESH)
        return 0

    def hello_z(r, _):
        pl.semaphore_signal(barrier, inc=1, device_id={"tensor": lax.rem(z + r, nz)}, device_id_type=MESH)
        return 0

    lax.fori_loop(1, ne, hello_e, 0)
    lax.fori_loop(1, nz, hello_z, 0)
    pl.semaphore_signal(barrier, inc=1, device_id={"pipe": other}, device_id_type=MESH)

    ins = [
        pltpu.make_async_copy(x_in.at[p], xin, sem_in.at[0]),
        pltpu.make_async_copy(cot_in.at[p], cot, sem_in.at[1]),
        pltpu.make_async_copy(bucket_in, bucket, sem_in.at[2]),
    ]
    for copy in ins:
        copy.start()
    weights = [
        (one_in, gain_one), (qkv_in, w_qkv), (bias_in, bias_w), (w_full, w_full), (routes_in, routes), (router_in, router),
        (two_in, gain_two), (up_in, w_up), (down_in, w_down),
    ]
    def load(k):
        src, dst = weights[k]
        pltpu.make_async_copy(src.at[p] if k == 4 else src, dst.at[p], sem_w.at[k, p]).start()

    def lend(k):
        src, dst = weights[k]
        return pltpu.make_async_remote_copy(
            src_ref=src.at[other] if k == 4 else src.at[p] if k == 3 else src, dst_ref=dst.at[p], send_sem=sem_ws.at[k], recv_sem=sem_w.at[k, p],
            device_id={"pipe": other}, device_id_type=MESH)

    def gather_start():
        pltpu.make_async_copy(out_in, w_full.at[p, z], sem_in.at[3]).start()

        def one(r, _):
            pltpu.make_async_remote_copy(
                src_ref=out_in, dst_ref=w_full.at[p, z], send_sem=wo_send, recv_sem=wo_recv,
                device_id={"tensor": lax.rem(z + r, nz)}, device_id_type=MESH).start()
            return 0
        lax.fori_loop(1, nz, one, 0)

    def gather_end():
        pltpu.make_async_copy(out_in, w_full.at[p, z], sem_in.at[3]).wait()
        part = w_full.at[p, pl.ds(1, nz - 1)]
        pltpu.make_async_copy(part, part, wo_send).wait()
        pltpu.make_async_copy(part, part, wo_recv).wait()
        lend(3).start()

    load(4)

    @pl.when(p == 0)
    def _():
        for k in (0, 1, 2, 5, 6):
            load(k)
    pl.semaphore_wait(barrier, ne - 1 + nz - 1 + 1)
    lend(4).start()

    @pl.when(p == 0)
    def _():
        gather_start()
        for k in (0, 1, 2, 5, 6, 7, 8):
            lend(k).start()
        for k in (7, 8):
            load(k)

    def await_weight(k, l):
        dst = weights[k][1]
        pltpu.make_async_copy(dst.at[l], dst.at[l], sem_w.at[k, l]).wait()

    def send_all(src, dst, send, recv, forth):
        def one(r, _):
            pltpu.make_async_remote_copy(
                src_ref=src.at[r], dst_ref=dst.at[r], send_sem=send, recv_sem=recv,
                device_id={"expert": lax.rem(x + r if forth else x + ne - r, ne)}, device_id_type=MESH).start()
            return 0
        lax.fori_loop(1, ne, one, 0)
        dst[0] = src[0]

    def await_all(src, dst, send, recv):
        part = src.at[pl.ds(1, ne - 1)]
        pltpu.make_async_copy(part, part, send).wait()
        part = dst.at[pl.ds(1, ne - 1)]
        pltpu.make_async_copy(part, part, recv).wait()

    def exchange(kind, l):
        send_all(send_a.at[kind], recv_a.at[l, kind], sa_send.at[l, kind], sa_recv.at[l, kind], True)

    def arrived(kind, l):
        await_all(send_a.at[kind], recv_a.at[l, kind], sa_send.at[l, kind], sa_recv.at[l, kind])
        return recv_a[l, kind]

    def exchange_back(kind, l, c):
        send_all(send_c.at[c], recv_c.at[l, kind, c], sc_send.at[l, kind, c], sc_recv.at[l, kind, c], False)

    def arrived_back(kind, l, c):
        await_all(send_c.at[c], recv_c.at[l, kind, c], sc_send.at[l, kind, c], sc_recv.at[l, kind, c])
        return recv_c[l, kind, c].reshape(slots, part_w)

    def reduce_start(buf, send, recv):
        def one(r, _):
            pltpu.make_async_remote_copy(
                src_ref=buf.at[0], dst_ref=buf.at[r], send_sem=send, recv_sem=recv,
                device_id={"tensor": lax.rem(z + r, nz)}, device_id_type=MESH).start()
            return 0
        lax.fori_loop(1, nz, one, 0)

    def reduce_end(buf, send, recv):
        part = buf.at[pl.ds(1, nz - 1)]
        pltpu.make_async_copy(part, part, send).wait()
        pltpu.make_async_copy(part, part, recv).wait()
        acc = None
        for a in range(nz):
            term = buf[lax.rem(z + nz - a, nz)].astype(F32)
            acc = term if acc is None else acc + term
        return acc

    def summed_back(kind, l, weigh):
        for c in range(parts_c):
            red_c[l, kind, c, 0] = weigh(arrived_back(kind, l, c)).astype(BF16)
            reduce_start(red_c.at[l, kind, c], rc_send.at[l, kind, c], rc_recv.at[l, kind, c])
        return lambda: jnp.concatenate(
            [reduce_end(red_c.at[l, kind, c], rc_send.at[l, kind, c], rc_recv.at[l, kind, c]) for c in range(parts_c)], axis=1)

    def split(blocks):
        wide = blocks.astype(F32)
        return [wide[:, e * CAP:(e + 1) * CAP].reshape(ne * CAP, width).astype(BF16) for e in range(local)]

    def join(parts):
        return jnp.concatenate([part.reshape(ne, CAP, part_w) for part in parts], axis=1).astype(BF16)

    def head_mask(h):
        at = lanes_of((1, hw), 1)
        return ((at >= h * hd) & (at < (h + 1) * hd)).astype(BF16)

    def scale_of(h):
        return lax.rsqrt(jnp.mean(h * h, -1, keepdims=True) + EPS)

    def column(row):
        eye = lanes_of((seq, seq), 0) == lanes_of((seq, seq), 1)
        return jnp.sum(jnp.where(eye, row.astype(F32), 0.0), -1, keepdims=True)

    def chosen_of(ids):
        at = lanes_of((seq, ne * local), 1)
        return [(at == e).astype(F32) for e in ids]

    def named(l):
        return [column(routes[l, k:k + 1]).astype(jnp.int32) for k in range(2)]

    def router_of(l):
        r = router[l]
        high = r.astype(BF16)
        return high, (r - high.astype(F32)).astype(BF16)

    def place(l):
        ids = named(l)
        hot_e = chosen_of(ids)
        row_at, col_at = lanes_of((seq, seq), 0), lanes_of((seq, seq), 1)
        earlier = (row_at > col_at).astype(BF16)
        count = nn(earlier, (hot_e[0] + hot_e[1]).astype(BF16))
        for kk in range(2):
            before = count if kk == 0 else count + hot_e[0]
            c = jnp.sum(before * hot_e[kk], -1, keepdims=True).astype(jnp.int32)
            e = ids[kk]
            at = (((e >> 1) - x + ne) & (ne - 1)) * (2 * CAP) + (e & 1) * CAP + c
            comb[l, kk * seq:(kk + 1) * seq] = (lanes_of((seq, slots), 1) == at).astype(F32).astype(BF16)

    def forward(l, _):
        h_in = hs[l]
        await_weight(0, l)
        n1 = (h_in * scale_of(h_in) * gain_one[l]).astype(BF16)
        n_one[l] = n1
        await_weight(1, l)
        for c in range(3):
            qkv[l, c] = nt(n1, w_qkv[l, c]).astype(BF16)
        q, k, v = qkv[l, 0], qkv[l, 1], qkv[l, 2]
        await_weight(2, l)
        causal = lanes_of((seq, seq), 0) >= lanes_of((seq, seq), 1)
        mixed = jnp.zeros((seq, hw), F32)
        for h in range(heads):
            mask = head_mask(h)
            rel = lax.dot_general(
                jnp.broadcast_to(bias_w[l, h], (8, hot.shape[1])), hot[...], (((1,), (1,)), ((), ())),
                precision=lax.Precision.HIGHEST, preferred_element_type=F32)
            bias = pltpu.roll(jnp.broadcast_to(rel[0:1], (seq, seq)), 0, 1, stride=1, stride_axis=0)
            s = nt(q * mask, k) * (hd ** -0.5) + bias
            s = jnp.where(causal, s, MASKED)
            e = jnp.exp(s - jnp.max(s, -1, keepdims=True))
            prob = e / jnp.sum(e, -1, keepdims=True)
            probs_s[l, h] = prob
            mixed = mixed + nn(prob.astype(BF16), v * mask)
        mixed = mixed.astype(BF16)
        mixed_s[l] = mixed
        mix[l, 0] = mixed
        reduce_start(mix.at[l], mx_send.at[l], mx_recv.at[l])

        @pl.when(l == 0)
        def _():
            @pl.when(p == 1)
            def _():
                gather_start()
                for k in (0, 1, 2, 5, 6, 7, 8):
                    lend(k).start()
                    load(k)
            for layer in range(2):
                await_weight(4, layer)
                place(layer)
            send_a[1] = tn(comb[1, 0:seq] + comb[1, seq:2 * seq], cot[...]).astype(BF16).reshape(ne, 2 * CAP, width)
            exchange(1, 1)

        hot_e = chosen_of(named(l))
        both = comb[l, 0:seq] + comb[l, seq:2 * seq]
        await_weight(5, l)
        await_weight(6, l)

        @pl.when((p == 0) & (l == 0))
        def _():
            gather_end()

        @pl.when(l != p)
        def _():
            await_weight(3, l)

        part = mix.at[l, pl.ds(1, nz - 1)]
        pltpu.make_async_copy(part, part, mx_send.at[l]).wait()
        pltpu.make_async_copy(part, part, mx_recv.at[l]).wait()
        attn = None
        for a in range(nz):
            term = nn(mix[l, lax.rem(z + nz - a, nz)], w_full[l, a])
            attn = term if attn is None else attn + term
        h_mid = h_in + attn
        h_mid_s[l] = h_mid
        n2 = (h_mid * scale_of(h_mid) * gain_two[l]).astype(BF16)
        n_two[l] = n2
        send_a[0] = tn(both, n2).astype(BF16).reshape(ne, 2 * CAP, width)
        exchange(0, l)
        high, low = router_of(l)
        logits = nt(n2, high) + nt(n2, low)
        e = jnp.exp(logits - jnp.max(logits, -1, keepdims=True))
        ep = e / jnp.sum(e, -1, keepdims=True)
        eprobs[l] = ep
        picked = [jnp.sum(ep * hot_e[kk], -1, keepdims=True) for kk in range(2)]
        inv = picked[0] + picked[1]
        gates = [picked[kk] / inv for kk in range(2)]

        @pl.when(l == 1)
        def _():
            at = lanes_of((seq, LANES), 1)
            sent = []
            for kk in range(2):
                top = gates[kk].astype(BF16).astype(F32)
                sent.append(jnp.where(at == 0, top, jnp.where(at == 1, gates[kk] - top, 0.0)).astype(BF16))
            send_g[...] = tn(comb[l], jnp.concatenate(sent, axis=0)).astype(BF16).reshape(ne, 2 * CAP, LANES)
            send_all(send_g, recv_g, sg_send, sg_recv, True)

        await_weight(7, l)
        await_weight(8, l)
        parts = split(arrived(0, l))
        for e in range(local):
            x_s[l, e] = parts[e]

        def expert(e, _):
            u = nn(x_s[l, e], w_up[l, e])
            u_s[l, e] = u
            t = jnp.tanh(TANH_A * (u + TANH_B * u * u * u))
            hid_s[l, e] = (0.5 * u * (1.0 + t)).astype(BF16)
            return 0
        lax.fori_loop(0, local, expert, 0)
        for c in range(parts_c):
            cols = slice(c * part_w, (c + 1) * part_w)
            send_c[c] = join([nn(hid_s[l, e], w_down[l, e, :, cols]) for e in range(local)])
            exchange_back(0, l, c)

        @pl.when((p == 1) & (l == 0))
        def _():
            gather_end()

        def slopes(e, _):
            u = u_s[l, e]
            t = jnp.tanh(TANH_A * (u + TANH_B * u * u * u))
            u_s[l, e] = 0.5 * (1.0 + t) + (0.5 * TANH_A) * u * (1.0 - t * t) * (1.0 + (3.0 * TANH_B) * u * u)
            return 0
        lax.fori_loop(0, local, slopes, 0)
        out = summed_back(0, l, lambda back: gates[0] * nn(comb[l, 0:seq], back) + gates[1] * nn(comb[l, seq:2 * seq], back))
        out = h_mid + out()
        hs[l + 1] = jnp.where(l == 0, out.astype(BF16).astype(F32), out)
        return 0

    for copy in ins:
        copy.wait()
    hs[0] = xin[...].astype(F32)
    turn_at, turn_of = lanes_of((seq, seq), 0), lanes_of((seq, seq), 1)
    turned_bucket = jnp.where((turn_at + turn_of == 0) | (turn_at + turn_of == seq), bucket[...].astype(F32), 0.0)
    turned_bucket = jnp.sum(turned_bucket, -1, keepdims=True).astype(jnp.int32)
    hot[...] = (turned_bucket == lanes_of(hot.shape, 1)).astype(F32)
    lax.fori_loop(0, 2, forward, 0)

    def deliver(src, owner):
        @pl.when(p == owner)
        def _():
            pltpu.make_async_copy(src, sec_out.at[p], sec_loc).start()

        @pl.when(p != owner)
        def _():
            pltpu.make_async_remote_copy(
                src_ref=src, dst_ref=sec_out.at[p], send_sem=sec_send, recv_sem=sec_recv,
                device_id={"pipe": other}, device_id_type=MESH).start()

    def piece(ref, j):
        return ref.at[pl.ds(pl.multiple_of(j * flat_rows, 8), flat_rows)]

    def merge_attn():
        pltpu.make_async_copy(chunk_pair, chunk_pair, pr_recv.at[0]).wait()
        for c in range(parts_c):
            chunk_pair[c] = (chunk[p, c].astype(F32) + chunk_pair[c].astype(F32)).astype(BF16)

            def scatter(r, _, c=c):
                to = lax.rem(x + r, ne)
                pltpu.make_async_remote_copy(
                    src_ref=chunk_pair.at[c, to], dst_ref=chunk_in.at[c, r], send_sem=ck_send.at[c], recv_sem=ck_recv.at[c],
                    device_id={"expert": to}, device_id_type=MESH).start()
                return 0
            lax.fori_loop(1, ne, scatter, 0)
            chunk_in[c, 0] = chunk_pair[c, x]

    def merge_small():
        pltpu.make_async_copy(small_pair, small_pair, pr_recv.at[1]).wait()
        small_pair[...] = small[p] + small_pair[...]

        def scatter(r, _):
            to = lax.rem(x + r, ne)
            pltpu.make_async_remote_copy(
                src_ref=piece(small_pair, to), dst_ref=small_in.at[r], send_sem=ck_send.at[parts_c], recv_sem=ck_recv.at[parts_c],
                device_id={"expert": to}, device_id_type=MESH).start()
            return 0
        lax.fori_loop(1, ne, scatter, 0)
        small_in[0] = small_pair[pl.ds(pl.multiple_of(x * flat_rows, 8), flat_rows)]

    def spread(k, arrived_at, whole, dst):
        part = arrived_at.at[pl.ds(1, ne - 1)]
        pltpu.make_async_copy(part, part, ck_send.at[k]).wait()
        pltpu.make_async_copy(part, part, ck_recv.at[k]).wait()
        acc = arrived_at[0].astype(F32)
        for r in range(1, ne):
            acc = acc + arrived_at[r].astype(F32)
        whole[...] = acc.astype(whole.dtype)
        pltpu.make_async_copy(whole, dst, ag_loc.at[k]).start()

        def one(r, _):
            pltpu.make_async_remote_copy(
                src_ref=whole, dst_ref=dst, send_sem=ag_send.at[k], recv_sem=ag_recv.at[k],
                device_id={"expert": lax.rem(x + r, ne)}, device_id_type=MESH).start()
            return 0
        lax.fori_loop(1, ne, one, 0)

    def spread_attn():
        for c in range(parts_c):
            spread(c, chunk_in.at[c], total.at[c], attn_out.at[x, :, pl.ds(c * part_w, part_w)])

    def spread_small():
        spread(parts_c, small_in, total_small, piece(small_out, x))

    def to_partner(src, dst, send, recv):
        pltpu.make_async_remote_copy(
            src_ref=src, dst_ref=dst, send_sem=send, recv_sem=recv, device_id={"pipe": other}, device_id_type=MESH).start()

    part = send_a.at[1, pl.ds(1, ne - 1)]
    pltpu.make_async_copy(part, part, sa_send.at[1, 1]).wait()
    deliver(hs.at[2], 1)
    g_s[...] = cot[...].astype(F32)

    def keep_grad(l, k, value):
        value = value.astype(BF16)
        for c in range(parts_c):
            chunk[l, c, k * per:(k + 1) * per] = value[:, c * part_w:(c + 1) * part_w].reshape(per, rows, part_w)

    def backward(i, _):
        l = 1 - i
        g = g_s[...]
        hot_e = chosen_of(named(l))
        ep = eprobs[l]
        picked = [jnp.sum(ep * hot_e[kk], -1, keepdims=True) for kk in range(2)]
        inv = picked[0] + picked[1]
        gates = [picked[kk] / inv for kk in range(2)]
        at = lanes_of((seq, LANES), 1)

        @pl.when(l == 0)
        def _():
            dy = jnp.concatenate([(gates[kk] * g).astype(BF16) for kk in range(2)], axis=0)
            send_a[1] = tn(comb[l], dy).astype(BF16).reshape(ne, 2 * CAP, width)
            exchange(1, l)

            @pl.when(p == 1)
            def _():
                merge_attn()
                merge_small()
            parts = split(arrived(1, l))
            for e in range(local):
                x_dy[e] = parts[e]

        @pl.when(l == 1)
        def _():
            await_all(send_g, recv_g, sg_send, sg_recv)
            weigh = jnp.sum(recv_g[...].astype(F32), -1, keepdims=True)
            part = recv_a.at[l, 1, pl.ds(1, ne - 1)]
            pltpu.make_async_copy(part, part, sa_recv.at[l, 1]).wait()
            wide = recv_a[l, 1].astype(F32) * weigh
            for e in range(local):
                x_dy[e] = wide[:, e * CAP:(e + 1) * CAP].reshape(ne * CAP, width).astype(BF16)

        def expert(e, _):
            dy_e = x_dy[e]
            dh = nt(dy_e, w_down[l, e])
            x_du[e] = (dh * u_s[l, e]).astype(BF16)
            return 0
        lax.fori_loop(0, local, expert, 0)
        for c in range(parts_c):
            cols = slice(c * part_w, (c + 1) * part_w)
            send_c[c] = join([nt(x_du[e], w_up[l, e, cols]) for e in range(local)])
            exchange_back(1, l, c)

        @pl.when((p == 1) & (l == 0))
        def _():
            spread_attn()
            spread_small()

        gg = jnp.zeros((seq, LANES), F32)
        for kk in range(2):
            part = None
            for c in range(parts_c):
                got = nn(comb[l, kk * seq:(kk + 1) * seq], recv_c[l, 0, c].reshape(slots, part_w))
                term = jnp.sum(g[:, c * part_w:(c + 1) * part_w] * got, -1, keepdims=True)
                part = term if part is None else part + term
            high = part.astype(BF16).astype(F32)
            gg = gg + jnp.where(at == kk, high, 0.0) + jnp.where(at == 2 + kk, part - high, 0.0)
        red_g[l, 0] = gg.astype(BF16)
        reduce_start(red_g.at[l], rd_send.at[l, 1], rd_recv.at[l, 1])

        def expert_grads(e, _):
            g_up[l, e] = tn(x_s[l, e], x_du[e]).astype(BF16)
            g_down[l, e] = tn(hid_s[l, e], x_dy[e]).astype(BF16)
            return 0
        lax.fori_loop(0, local, expert_grads, 0)

        both = comb[l, 0:seq] + comb[l, seq:2 * seq]
        dn2 = summed_back(1, l, lambda back: nn(both, back))

        @pl.when(p == l)
        def _():
            pltpu.make_async_copy(g_up.at[l], own_up, gr_loc.at[0]).start()
            pltpu.make_async_copy(g_down.at[l], own_down, gr_loc.at[1]).start()

        @pl.when(p != l)
        def _():
            to_partner(g_up.at[l], recv_up, gr_send.at[0], gr_recv.at[0])
            to_partner(g_down.at[l], recv_down, gr_send.at[1], gr_recv.at[1])

        h_mid = h_mid_s[l]
        scale = scale_of(h_mid)
        tail = reduce_end(red_g.at[l], rd_send.at[l, 1], rd_recv.at[l, 1])
        dn2 = dn2()
        gg = [jnp.sum(jnp.where((at == kk) | (at == 2 + kk), tail, 0.0), -1, keepdims=True) for kk in range(2)]
        centre = gg[0] * gates[0] + gg[1] * gates[1]
        dprob = hot_e[0] * ((gg[0] - centre) / inv) + hot_e[1] * ((gg[1] - centre) / inv)
        dlog = (ep * (dprob - jnp.sum(ep * dprob, -1, keepdims=True))).astype(BF16)
        high, low = router_of(l)
        dn2 = dn2 + nn(dlog, high) + nn(dlog, low)
        flat[...] = jnp.zeros_like(flat)
        flat[0:ne * local] = tn(dlog, n_two[l])
        flat[ne * local + 1:ne * local + 2] = jnp.sum(dn2 * h_mid * scale, 0, keepdims=True)
        dg = dn2 * gain_two[l]
        dmid = g + scale * dg - h_mid * (scale * scale * scale) * jnp.mean(h_mid * dg, -1, keepdims=True)
        da = dmid.astype(BF16)
        dmixed = nt(da, w_full[l, z]).astype(BF16)
        q, k, v = qkv[l, 0], qkv[l, 1], qkv[l, 2]
        dq = jnp.zeros((seq, hw), F32)
        dk = jnp.zeros((seq, hw), F32)
        dv = jnp.zeros((seq, hw), F32)
        causal = lanes_of((seq, seq), 0) >= lanes_of((seq, seq), 1)
        row_at = lanes_of((seq, seq), 0)
        top = lanes_of((8, LANES), 0)
        bias_g = jnp.zeros((8, LANES), F32)
        for h in range(heads):
            mask = head_mask(h)
            prob = probs_s[l, h]
            dm = dmixed * mask
            dp = nt(dm, v)
            dv = dv + tn(prob.astype(BF16), dm)
            ds = jnp.where(causal, prob * (dp - jnp.sum(prob * dp, -1, keepdims=True)), 0.0).astype(BF16)
            dq = dq + nn(ds, k * mask)
            dk = dk + tn(ds, q * mask)
            turned = ds.astype(F32)
            bit = 1
            while bit < seq:
                turned = jnp.where((row_at & bit) != 0, pltpu.roll(turned, seq - bit, 1), turned)
                bit *= 2
            bias_g = bias_g + jnp.where(top == h, jnp.sum(turned, 0, keepdims=True), 0.0)
        dqkv[0] = (dq * (hd ** -0.5)).astype(BF16)
        dqkv[1] = (dk * (hd ** -0.5)).astype(BF16)
        dqkv[2] = dv.astype(BF16)
        dn1 = nn(dqkv[0], w_qkv[l, 0]) + nn(dqkv[1], w_qkv[l, 1]) + nn(dqkv[2], w_qkv[l, 2])
        red_a[l, 0] = dn1.astype(BF16)
        reduce_start(red_a.at[l], rd_send.at[l, 0], rd_recv.at[l, 0])
        n1 = n_one[l]
        keep_grad(l, 3, tn(mixed_s[l], da))
        for c in range(3):
            keep_grad(l, c, tn(dqkv[c], n1))

        @pl.when(p != l)
        def _():
            to_partner(chunk.at[l], chunk_pair, pr_send.at[0], pr_recv.at[0])

        @pl.when((p == 0) & (l == 0))
        def _():
            merge_attn()

        bias_high = bias_g.astype(BF16)
        bias_low = (bias_g - bias_high.astype(F32)).astype(BF16)
        hot_b = hot[...].astype(BF16)
        flat[ne * local + 8:ne * local + 16, 0:hot.shape[1]] = nn(bias_high, hot_b) + nn(bias_low, hot_b)
        h_in = hs[l]
        scale_one = scale_of(h_in)
        dn1 = reduce_end(red_a.at[l], rd_send.at[l, 0], rd_recv.at[l, 0])
        flat[ne * local:ne * local + 1] = jnp.sum(dn1 * h_in * scale_one, 0, keepdims=True)
        for b in range(fold):
            small[l, b * SMALL:(b + 1) * SMALL] = flat[:, b * LANES:(b + 1) * LANES]

        @pl.when(p != l)
        def _():
            to_partner(small.at[l], small_pair, pr_send.at[1], pr_recv.at[1])

        dg = dn1 * gain_one[l]
        dh = dmid + scale_one * dg - h_in * (scale_one * scale_one * scale_one) * jnp.mean(h_in * dg, -1, keepdims=True)
        fin[...] = dh
        g_s[...] = dh.astype(BF16).astype(F32)
        return 0

    lax.fori_loop(0, 2, backward, 0)
    deliver(fin, 0)

    @pl.when(p == 0)
    def _():
        merge_small()
        spread_attn()
        spread_small()

    for k in range(len(weights)):
        lend(k).wait_send()
    for k, ref in enumerate((g_up, g_down)):
        for sem in (gr_loc, gr_send, gr_recv):
            pltpu.make_async_copy(ref.at[0], ref.at[0], sem.at[k]).wait()
    for sem in (sec_loc, sec_send, sec_recv):
        pltpu.make_async_copy(fin, fin, sem).wait()
    for k, pair in enumerate((chunk_pair, small_pair)):
        pltpu.make_async_copy(pair, pair, pr_send.at[k]).wait()
    for k in range(parts_c + 1):
        whole, arrived_at = (total.at[k], chunk_in.at[k]) if k < parts_c else (total_small, small_in)
        pltpu.make_async_copy(whole, whole, ag_loc.at[k]).wait()
        part = arrived_at.at[pl.ds(1, ne - 1)]
        pltpu.make_async_copy(part, part, ag_send.at[k]).wait()
        pltpu.make_async_copy(part, part, ag_recv.at[k]).wait()


def finish(
    local, heads, experts,
    sec, own_up, own_down, recv_up, recv_down, attn, small,
    sec_out, qkv_out, out_out, up_out, down_out, router_out, one_out, two_out, bias_out,
    own, got, whole, attn_v, attn_f, small_v, router_v, one_v, two_v, bias_v, sec_v, sem_own, sem_got, sem_out, sem_in, sem_small,
):
    pieces = [(k, e) for k in range(2) for e in range(local)]
    sources = ((own_up, recv_up), (own_down, recv_down))
    results = (up_out, down_out)

    def incoming(i):
        k, e = pieces[i]
        return (
            pltpu.make_async_copy(sources[k][0].at[e], own.at[i], sem_own.at[i]),
            pltpu.make_async_copy(sources[k][1].at[e], got.at[i], sem_got.at[i]),
        )

    def leaving(i):
        k, e = pieces[i]
        return pltpu.make_async_copy(whole.at[i], results[k].at[e], sem_out.at[i])

    last = [pltpu.make_async_copy(attn, attn_v, sem_in.at[0]), pltpu.make_async_copy(small, small_v, sem_in.at[1])]
    for i in range(len(pieces)):
        for copy in incoming(i):
            copy.start()
        if i == 0:
            for copy in last:
                copy.start()
    pass_in = pltpu.make_async_copy(sec, sec_v, sem_in.at[2])
    pass_out = pltpu.make_async_copy(sec_v, sec_out, sem_in.at[3])
    pass_in.start()
    step = 64
    for i in range(len(pieces)):
        for copy in incoming(i):
            copy.wait()

        def add(r, _, i=i):
            at = pl.ds(pl.multiple_of(r * step, step), step)
            whole[i, at] = own[i, at].astype(F32) + got[i, at].astype(F32)
            return 0
        lax.fori_loop(0, own.shape[1] // step, add, 0)
        leaving(i).start()
    pass_in.wait()
    pass_out.start()
    for copy in last:
        copy.wait()

    def widen(r, _):
        attn_f[r] = attn_v[r].astype(F32)
        return 0
    lax.fori_loop(0, attn_f.shape[0], widen, 0)
    cut = attn_f.shape[0] * 3 // 4
    out = [
        pltpu.make_async_copy(attn_f.at[pl.ds(0, cut)], qkv_out, sem_small.at[0]),
        pltpu.make_async_copy(attn_f.at[pl.ds(cut, attn_f.shape[0] - cut)], out_out, sem_small.at[1]),
    ]
    for b in range(router_v.shape[1] // LANES):
        cols = slice(b * LANES, (b + 1) * LANES)
        at = b * SMALL
        router_v[:, cols] = small_v[at:at + experts]
        one_v[:, cols] = small_v[at + experts:at + experts + 1]
        two_v[:, cols] = small_v[at + experts + 1:at + experts + 2]
    for h in range(heads):
        bias_v[h] = small_v[experts + 8 + h:experts + 9 + h, 0:bias_v.shape[2]]
    out += [
        pltpu.make_async_copy(src, dst, sem_small.at[2 + k])
        for k, (src, dst) in enumerate(((router_v, router_out), (one_v, one_out), (two_v, two_out), (bias_v, bias_out)))
    ]
    for copy in out:
        copy.start()
    for i in range(len(pieces)):
        leaving(i).wait()
    for copy in (*out, pass_out):
        copy.wait()


def body(
    block_input, cotangent, routes, offset_bucket, norm1_gain, qkv_weight, out_weight, bias_table, norm2_gain,
    router_weight, up_weight, down_weight,
):
    ne = lax.axis_size("expert")
    nz = lax.axis_size("tensor")
    micro, seq, width = block_input.shape
    heads, buckets = bias_table.shape[1:]
    local, _, ff = up_weight.shape[1:]
    hw = qkv_weight.shape[3]
    hd = hw // heads
    experts = router_weight.shape[2]
    rows = width // ne
    parts_c = PARTS
    part_w = width // parts_c
    fold = width // LANES
    per = hw // rows
    flat_rows = fold * SMALL // ne
    slots = ne * local * CAP

    any_space = pl.BlockSpec(memory_space=pl.ANY)
    hbm = pl.BlockSpec(memory_space=pltpu.HBM)
    vm = pltpu.VMEM
    dma = pltpu.SemaphoreType.DMA
    sds = jax.ShapeDtypeStruct
    part_w = width // PARTS
    flat = width // LANES * SMALL
    parts_in = (2, 2, PARTS, ne, 2 * CAP, part_w)
    half = (local, width, ff)
    cut = (PARTS, ne, rows, part_w)
    sec, own_up, own_down, recv_up, recv_down, attn, small = pl.pallas_call(
        functools.partial(kernel, (ne, nz, seq, width, local, heads, ff, hd)),
        out_shape=[
            sds((micro, seq, width), F32), sds(half, BF16), sds(half, BF16), sds(half, BF16), sds(half, BF16),
            sds((ne, rows, width), BF16), sds((flat, LANES), F32),
        ],
        in_specs=[hbm] * 12,
        out_specs=[any_space] * 7,
        scratch_shapes=[
            vm((seq, width), BF16), vm((seq, width), BF16), vm((1, seq), jnp.int32), vm((seq, buckets), F32),
            vm((2, 2, seq), jnp.int32), vm((2, 1, width), F32), vm((2, 1, width), F32), vm((2, heads, 1, buckets), F32),
            vm((2, experts, width), F32), vm((2, 3, hw, width), BF16),
            vm((2, nz, hw, width), BF16), vm((2, local, width, ff), BF16), vm((2, local, ff, width), BF16),
            vm((3, seq, width), F32), vm((2, seq, width), BF16), vm((2, 3, seq, hw), BF16),
            vm((2, heads, seq, seq), F32), vm((2, seq, hw), BF16), vm((2, seq, width), F32), vm((2, seq, width), BF16),
            vm((2, 2 * seq, slots), BF16), vm((2, seq, experts), F32), vm((2, local, ne * CAP, width), BF16),
            vm((2, local, ne * CAP, ff), F32),
            vm((local, ne * CAP, width), BF16), vm((local, ne * CAP, ff), BF16), vm((2, local, ne * CAP, ff), BF16),
            vm((seq, width), F32), vm((seq, width), F32), vm((3, seq, hw), BF16),
            vm((2, ne, 2 * CAP, width), BF16), vm((2, 2, ne, 2 * CAP, width), BF16), vm((ne, 2 * CAP, LANES), BF16),
            vm((ne, 2 * CAP, LANES), BF16), vm(parts_in[2:], BF16), vm(parts_in, BF16),
            vm((2, nz, seq, hw), BF16), vm((2, nz, seq, width), BF16), vm((2, 2, PARTS, nz, seq, part_w), BF16), vm((2, nz, seq, LANES), BF16),
            vm((2, *half), BF16), vm((2, *half), BF16), vm((2, *cut), BF16), vm(cut, BF16),
            vm(cut, BF16), vm((SMALL, width), F32), vm((2, flat, LANES), F32), vm((flat, LANES), F32),
            vm((ne, flat // ne, LANES), F32), vm((PARTS, rows, part_w), BF16), vm((flat // ne, LANES), F32),
            dma((4,)), dma((9, 2)), dma((9,)), dma, dma, dma((2,)), dma((2,)), dma((2, 2)), dma((2, 2)), dma, dma, dma((2, 2, PARTS)), dma((2, 2, PARTS)),
            dma((2, 2)), dma((2, 2)), dma((2, 2, PARTS)), dma((2, 2, PARTS)), dma((2,)), dma((2,)), dma((2,)),
            dma((PARTS + 1,)), dma((PARTS + 1,)), dma((2,)), dma((2,)), dma((PARTS + 1,)), dma((PARTS + 1,)), dma((PARTS + 1,)),
            dma, dma, dma,
        ],
        compiler_params=pltpu.CompilerParams(
            collective_id=0, has_side_effects=True, vmem_limit_bytes=VMEM_MB * 1024 * 1024),
        cost_estimate=pl.CostEstimate(flops=20_000_000_000, bytes_accessed=40_000_000, transcendentals=2_000_000),
    )(
        block_input, cotangent, routes[0].transpose(0, 2, 1), offset_bucket[None], norm1_gain, norm2_gain,
        bias_table.transpose(1, 0, 2), router_weight[0].T, qkv_weight[0].transpose(0, 2, 1), out_weight[0],
        up_weight[0], down_weight[0],
    )
    blocks = (2 * local, width, ff)
    sec, qkv_g, out_g, up_g, down_g, router_g, one_g, two_g, bias_g = pl.pallas_call(
        functools.partial(finish, local, heads, experts),
        out_shape=[
            sds((micro, seq, width), F32), sds((ne * 3 // 4, rows, width), F32), sds((ne // 4, rows, width), F32),
            sds(half, F32), sds(half, F32), sds((experts, width), F32), sds((1, width), F32), sds((1, width), F32),
            sds((heads, 1, buckets), F32),
        ],
        in_specs=[hbm] * 7,
        out_specs=[hbm] * 9,
        scratch_shapes=[
            vm(blocks, BF16), vm(blocks, BF16), vm(blocks, F32), vm((ne, rows, width), BF16), vm((ne, rows, width), F32),
            vm((flat, LANES), F32), vm((experts, width), F32), vm((1, width), F32), vm((1, width), F32),
            vm((heads, 1, buckets), F32), vm((micro, seq, width), F32),
            dma((2 * local,)), dma((2 * local,)), dma((2 * local,)), dma((4,)), dma((6,)),
        ],
        compiler_params=pltpu.CompilerParams(vmem_limit_bytes=60 * 1024 * 1024),
        cost_estimate=pl.CostEstimate(flops=3_000_000, bytes_accessed=25_000_000, transcendentals=0),
    )(sec, own_up, own_down, recv_up, recv_down, attn, small)
    return (
        sec[None], one_g, qkv_g.reshape(1, 3, hw, width).transpose(0, 1, 3, 2), out_g.reshape(1, hw, width),
        bias_g.transpose(1, 0, 2), two_g, router_g.T[None], up_g[None], down_g[None],
    )


def solution(mesh):
    in_specs = (
        P(None, "expert", None), P(None, "expert", None), P("pipe", None, "expert", None), P(), P("pipe", None),
        P("pipe", None, None, "tensor"), P("pipe", "tensor", None), P("pipe", "tensor", None), P("pipe", None),
        P("pipe", None, None), P("pipe", "expert", None, "tensor"), P("pipe", "expert", "tensor", None),
    )
    out_specs = (
        P("pipe", None, "expert", None), P("pipe", None), P("pipe", None, None, "tensor"), P("pipe", "tensor", None),
        P("pipe", "tensor", None), P("pipe", None), P("pipe", None, None), P("pipe", "expert", None, "tensor"),
        P("pipe", "expert", "tensor", None),
    )
    return jax.shard_map(body, mesh=mesh, in_specs=in_specs, out_specs=out_specs, check_vma=False)
```

```python
import functools

import jax
import jax.numpy as jnp
from jax import lax
from jax.experimental import pallas as pl
from jax.experimental.pallas import tpu as pltpu
from jax.sharding import PartitionSpec as P

EPS = 1e-06
MASKED = -1e30
MESH = pl.DeviceIdType.MESH
F32 = jnp.float32
BF16 = jnp.bfloat16
LANES = 128
CAP = 8
PARTS = 3
SMALL = 64
VMEM_MB = 60
TANH_A = 0.7978845608
TANH_B = 0.044715


def dot(a, b, left, right):
    return lax.dot_general(a, b, (((left,), (right,)), ((), ())), preferred_element_type=F32)


def nn(a, b):
    return dot(a, b, 1, 0)


def nt(a, b):
    return dot(a, b, 1, 1)


def tn(a, b):
    return dot(a, b, 0, 0)


def lanes_of(shape, dim):
    return lax.broadcasted_iota(jnp.int32, shape, dim)


def kernel(
    dims,
    x_in, cot_in, routes_in, bucket_in, one_in, two_in, bias_in, router_in, qkv_in, out_in, up_in, down_in,
    sec_out, own_up, own_down, attn_out, small_out,
    xin, cot, bucket, hot, routes, gain_one, gain_two, bias_w, router, w_qkv, w_full, w_up, w_down,
    hs, n_one, qkv, probs_s, mixed_s, h_mid_s, n_two, comb, eprobs, x_s, u_s, x_dy, x_du, hid_s, g_s, fin, dqkv,
    send_a, recv_a, send_g, recv_g, send_c, recv_c, mix, red_a, red_c, red_g, g_up, g_down, recv_up, recv_down, chunk, chunk_pair, chunk_in, flat, small, small_pair,
    small_in, total, total_small,
    sem_in, sem_w, sem_ws, wo_send, wo_recv, mx_send, mx_recv, sa_send, sa_recv, sg_send, sg_recv, sc_send, sc_recv, rd_send, rd_recv, rc_send, rc_recv, gr_send, gr_recv, gr_loc,
    ck_send, ck_recv, pr_send, pr_recv, ag_send, ag_recv, ag_loc, sec_send, sec_recv, sec_loc,
):
    ne, nz, seq, width, local, heads, ff, hd = dims
    p = lax.axis_index("pipe")
    x = lax.axis_index("expert")
    z = lax.axis_index("tensor")
    other = 1 - p
    slots = ne * 2 * CAP
    hw = heads * hd
    rows = width // ne
    parts_c = PARTS
    part_w = width // parts_c
    fold = width // LANES
    per = hw // rows
    flat_rows = fold * SMALL // ne

    barrier = pltpu.get_barrier_semaphore()

    def hello_e(r, _):
        pl.semaphore_signal(barrier, inc=1, device_id={"expert": lax.rem(x + r, ne)}, device_id_type=MESH)
        return 0

    def hello_z(r, _):
        pl.semaphore_signal(barrier, inc=1, device_id={"tensor": lax.rem(z + r, nz)}, device_id_type=MESH)
        return 0

    lax.fori_loop(1, ne, hello_e, 0)
    lax.fori_loop(1, nz, hello_z, 0)
    pl.semaphore_signal(barrier, inc=1, device_id={"pipe": other}, device_id_type=MESH)

    ins = [
        pltpu.make_async_copy(x_in.at[p], xin, sem_in.at[0]),
        pltpu.make_async_copy(cot_in.at[p], cot, sem_in.at[1]),
        pltpu.make_async_copy(bucket_in, bucket, sem_in.at[2]),
    ]
    for copy in ins:
        copy.start()
    weights = [
        (one_in, gain_one), (qkv_in, w_qkv), (bias_in, bias_w), (w_full, w_full), (routes_in, routes), (router_in, router),
        (two_in, gain_two), (up_in, w_up), (down_in, w_down),
    ]
    def to_partner(src, dst, send, recv):
        pltpu.make_async_remote_copy(
            src_ref=src, dst_ref=dst, send_sem=send, recv_sem=recv, device_id={"pipe": other}, device_id_type=MESH).start()

    def load(k):
        src, dst = weights[k]
        pltpu.make_async_copy(src.at[p] if k == 4 else src, dst.at[p], sem_w.at[k, p]).start()

    def lend(k):
        src, dst = weights[k]
        return pltpu.make_async_remote_copy(
            src_ref=src.at[other] if k == 4 else src.at[p] if k == 3 else src, dst_ref=dst.at[p], send_sem=sem_ws.at[k], recv_sem=sem_w.at[k, p],
            device_id={"pipe": other}, device_id_type=MESH)

    def gather_start():
        pltpu.make_async_copy(out_in, w_full.at[p, z], sem_in.at[3]).start()

        def one(r, _):
            pltpu.make_async_remote_copy(
                src_ref=out_in, dst_ref=w_full.at[p, z], send_sem=wo_send, recv_sem=wo_recv.at[r],
                device_id={"tensor": lax.rem(z + r, nz)}, device_id_type=MESH).start()
            return 0
        lax.fori_loop(1, nz, one, 0)
        to_partner(out_in, w_full.at[p, z], sem_ws.at[3], sem_w.at[3, p])

    def gather_end():
        pltpu.make_async_copy(out_in, w_full.at[p, z], sem_in.at[3]).wait()
        part = w_full.at[p, pl.ds(1, nz - 1)]
        pltpu.make_async_copy(part, part, wo_send).wait()
        for r in range(1, nz):
            got = w_full.at[p, lax.rem(z + nz - r, nz)]
            pltpu.make_async_copy(got, got, wo_recv.at[r]).wait()
            to_partner(got, got, sem_ws.at[3], sem_w.at[3, p])

    load(4)

    @pl.when(p == 0)
    def _():
        for k in (0, 1, 2, 5, 6):
            load(k)
    pl.semaphore_wait(barrier, ne - 1 + nz - 1 + 1)
    lend(4).start()

    @pl.when(p == 0)
    def _():
        gather_start()
        for k in (0, 1, 2, 5, 6, 7, 8):
            lend(k).start()
        for k in (7, 8):
            load(k)

    def await_weight(k, l):
        dst = weights[k][1]
        pltpu.make_async_copy(dst.at[l], dst.at[l], sem_w.at[k, l]).wait()

    def send_all(src, dst, send, recv, forth):
        def one(i, _):
            r = ne - i
            pltpu.make_async_remote_copy(
                src_ref=src.at[r], dst_ref=dst.at[r], send_sem=send, recv_sem=recv,
                device_id={"expert": lax.rem(x + r if forth else x + ne - r, ne)}, device_id_type=MESH).start()
            return 0
        lax.fori_loop(1, ne, one, 0)
        dst[0] = src[0]

    def await_all(src, dst, send, recv):
        part = src.at[pl.ds(1, ne - 1)]
        pltpu.make_async_copy(part, part, send).wait()
        part = dst.at[pl.ds(1, ne - 1)]
        pltpu.make_async_copy(part, part, recv).wait()

    def exchange(kind, l):
        send_all(send_a.at[kind], recv_a.at[l, kind], sa_send.at[l, kind], sa_recv.at[l, kind], True)

    def arrived(kind, l):
        await_all(send_a.at[kind], recv_a.at[l, kind], sa_send.at[l, kind], sa_recv.at[l, kind])
        return recv_a[l, kind]

    def exchange_back(kind, l, c):
        send_all(send_c.at[c], recv_c.at[l, kind, c], sc_send.at[l, kind, c], sc_recv.at[l, kind, c], False)

    def arrived_back(kind, l, c):
        await_all(send_c.at[c], recv_c.at[l, kind, c], sc_send.at[l, kind, c], sc_recv.at[l, kind, c])
        return recv_c[l, kind, c].reshape(slots, part_w)

    def reduce_start(buf, send, recv):
        for r in sorted(range(1, nz), key=lambda r: -min(r, nz - r)):
            pltpu.make_async_remote_copy(
                src_ref=buf.at[0], dst_ref=buf.at[r], send_sem=send, recv_sem=recv,
                device_id={"tensor": lax.rem(z + r, nz)}, device_id_type=MESH).start()

    def reduce_end(buf, send, recv):
        part = buf.at[pl.ds(1, nz - 1)]
        pltpu.make_async_copy(part, part, send).wait()
        pltpu.make_async_copy(part, part, recv).wait()
        acc = None
        for a in range(nz):
            term = buf[lax.rem(z + nz - a, nz)].astype(F32)
            acc = term if acc is None else acc + term
        return acc

    def summed_back(kind, l, weigh):
        for c in range(parts_c):
            red_c[l, kind, c, 0] = weigh(arrived_back(kind, l, c)).astype(BF16)
            reduce_start(red_c.at[l, kind, c], rc_send.at[l, kind, c], rc_recv.at[l, kind, c])
        return lambda: jnp.concatenate(
            [reduce_end(red_c.at[l, kind, c], rc_send.at[l, kind, c], rc_recv.at[l, kind, c]) for c in range(parts_c)], axis=1)

    def split(blocks):
        wide = blocks.astype(F32)
        return [wide[:, e * CAP:(e + 1) * CAP].reshape(ne * CAP, width).astype(BF16) for e in range(local)]

    def join(parts):
        return jnp.concatenate([part.reshape(ne, CAP, part_w) for part in parts], axis=1).astype(BF16)

    def head_mask(h):
        at = lanes_of((1, hw), 1)
        return ((at >= h * hd) & (at < (h + 1) * hd)).astype(BF16)

    def scale_of(h):
        return lax.rsqrt(jnp.mean(h * h, -1, keepdims=True) + EPS)

    def column(row):
        eye = lanes_of((seq, seq), 0) == lanes_of((seq, seq), 1)
        return jnp.sum(jnp.where(eye, row.astype(F32), 0.0), -1, keepdims=True)

    def chosen_of(ids):
        at = lanes_of((seq, ne * local), 1)
        return [(at == e).astype(F32) for e in ids]

    def named(l):
        return [column(routes[l, k:k + 1]).astype(jnp.int32) for k in range(2)]

    def router_of(l):
        r = router[l]
        high = r.astype(BF16)
        return high, (r - high.astype(F32)).astype(BF16)

    def place(l):
        ids = named(l)
        hot_e = chosen_of(ids)
        row_at, col_at = lanes_of((seq, seq), 0), lanes_of((seq, seq), 1)
        earlier = (row_at > col_at).astype(BF16)
        count = nn(earlier, (hot_e[0] + hot_e[1]).astype(BF16))
        for kk in range(2):
            before = count if kk == 0 else count + hot_e[0]
            c = jnp.sum(before * hot_e[kk], -1, keepdims=True).astype(jnp.int32)
            e = ids[kk]
            at = (((e >> 1) - x + ne) & (ne - 1)) * (2 * CAP) + (e & 1) * CAP + c
            comb[l, kk * seq:(kk + 1) * seq] = (lanes_of((seq, slots), 1) == at).astype(F32).astype(BF16)

    def forward(l, _):
        h_in = hs[l]
        await_weight(0, l)
        n1 = (h_in * scale_of(h_in) * gain_one[l]).astype(BF16)
        n_one[l] = n1
        await_weight(1, l)
        for c in range(3):
            qkv[l, c] = nt(n1, w_qkv[l, c]).astype(BF16)
        q, k, v = qkv[l, 0], qkv[l, 1], qkv[l, 2]
        await_weight(2, l)
        causal = lanes_of((seq, seq), 0) >= lanes_of((seq, seq), 1)
        mixed = jnp.zeros((seq, hw), F32)
        for h in range(heads):
            mask = head_mask(h)
            rel = lax.dot_general(
                jnp.broadcast_to(bias_w[l, h], (8, hot.shape[1])), hot[...], (((1,), (1,)), ((), ())),
                precision=lax.Precision.HIGHEST, preferred_element_type=F32)
            bias = pltpu.roll(jnp.broadcast_to(rel[0:1], (seq, seq)), 0, 1, stride=1, stride_axis=0)
            s = nt(q * mask, k) * (hd ** -0.5) + bias
            s = jnp.where(causal, s, MASKED)
            e = jnp.exp(s - jnp.max(s, -1, keepdims=True))
            prob = e / jnp.sum(e, -1, keepdims=True)
            probs_s[l, h] = prob
            mixed = mixed + nn(prob.astype(BF16), v * mask)
        mixed = mixed.astype(BF16)
        mixed_s[l] = mixed
        mix[l, 0] = mixed
        reduce_start(mix.at[l], mx_send.at[l], mx_recv.at[l])

        @pl.when(l == 0)
        def _():
            @pl.when(p == 1)
            def _():
                gather_start()
                for k in (0, 1, 2, 5, 6, 7, 8):
                    lend(k).start()
                    load(k)
            for layer in range(2):
                await_weight(4, layer)
                place(layer)
            send_a[1] = tn(comb[1, 0:seq] + comb[1, seq:2 * seq], cot[...]).astype(BF16).reshape(ne, 2 * CAP, width)
            exchange(1, 1)

        hot_e = chosen_of(named(l))
        both = comb[l, 0:seq] + comb[l, seq:2 * seq]
        await_weight(5, l)
        await_weight(6, l)

        @pl.when((p == 0) & (l == 0))
        def _():
            gather_end()

        @pl.when(l != p)
        def _():
            await_weight(3, l)

        part = mix.at[l, pl.ds(1, nz - 1)]
        pltpu.make_async_copy(part, part, mx_send.at[l]).wait()
        pltpu.make_async_copy(part, part, mx_recv.at[l]).wait()
        attn = None
        for a in range(nz):
            term = nn(mix[l, lax.rem(z + nz - a, nz)], w_full[l, a])
            attn = term if attn is None else attn + term
        h_mid = h_in + attn
        h_mid_s[l] = h_mid
        n2 = (h_mid * scale_of(h_mid) * gain_two[l]).astype(BF16)
        n_two[l] = n2
        send_a[0] = tn(both, n2).astype(BF16).reshape(ne, 2 * CAP, width)
        exchange(0, l)
        high, low = router_of(l)
        logits = nt(n2, high) + nt(n2, low)
        e = jnp.exp(logits - jnp.max(logits, -1, keepdims=True))
        ep = e / jnp.sum(e, -1, keepdims=True)
        eprobs[l] = ep
        picked = [jnp.sum(ep * hot_e[kk], -1, keepdims=True) for kk in range(2)]
        inv = picked[0] + picked[1]
        gates = [picked[kk] / inv for kk in range(2)]

        @pl.when(l == 1)
        def _():
            at = lanes_of((seq, LANES), 1)
            sent = []
            for kk in range(2):
                top = gates[kk].astype(BF16).astype(F32)
                sent.append(jnp.where(at == 0, top, jnp.where(at == 1, gates[kk] - top, 0.0)).astype(BF16))
            send_g[...] = tn(comb[l], jnp.concatenate(sent, axis=0)).astype(BF16).reshape(ne, 2 * CAP, LANES)
            send_all(send_g, recv_g, sg_send, sg_recv, True)

        await_weight(7, l)
        await_weight(8, l)
        parts = split(arrived(0, l))
        for e in range(local):
            x_s[l, e] = parts[e]

        def expert(e, _):
            u = nn(x_s[l, e], w_up[l, e])
            u_s[l, e] = u
            t = jnp.tanh(TANH_A * (u + TANH_B * u * u * u))
            hid_s[l, e] = (0.5 * u * (1.0 + t)).astype(BF16)
            return 0
        lax.fori_loop(0, local, expert, 0)
        for c in range(parts_c):
            cols = slice(c * part_w, (c + 1) * part_w)
            send_c[c] = join([nn(hid_s[l, e], w_down[l, e, :, cols]) for e in range(local)])
            exchange_back(0, l, c)

        @pl.when((p == 1) & (l == 0))
        def _():
            gather_end()

        def slopes(e, _):
            u = u_s[l, e]
            t = jnp.tanh(TANH_A * (u + TANH_B * u * u * u))
            u_s[l, e] = 0.5 * (1.0 + t) + (0.5 * TANH_A) * u * (1.0 - t * t) * (1.0 + (3.0 * TANH_B) * u * u)
            return 0
        lax.fori_loop(0, local, slopes, 0)
        out = summed_back(0, l, lambda back: gates[0] * nn(comb[l, 0:seq], back) + gates[1] * nn(comb[l, seq:2 * seq], back))
        out = h_mid + out()
        hs[l + 1] = jnp.where(l == 0, out.astype(BF16).astype(F32), out)
        return 0

    for copy in ins:
        copy.wait()
    hs[0] = xin[...].astype(F32)
    turn_at, turn_of = lanes_of((seq, seq), 0), lanes_of((seq, seq), 1)
    turned_bucket = jnp.where((turn_at + turn_of == 0) | (turn_at + turn_of == seq), bucket[...].astype(F32), 0.0)
    turned_bucket = jnp.sum(turned_bucket, -1, keepdims=True).astype(jnp.int32)
    hot[...] = (turned_bucket == lanes_of(hot.shape, 1)).astype(F32)
    lax.fori_loop(0, 2, forward, 0)

    def deliver(src, owner):
        @pl.when(p == owner)
        def _():
            pltpu.make_async_copy(src, sec_out.at[p], sec_loc).start()

        @pl.when(p != owner)
        def _():
            pltpu.make_async_remote_copy(
                src_ref=src, dst_ref=sec_out.at[p], send_sem=sec_send, recv_sem=sec_recv,
                device_id={"pipe": other}, device_id_type=MESH).start()

    def piece(ref, j):
        return ref.at[pl.ds(pl.multiple_of(j * flat_rows, 8), flat_rows)]

    def sum_experts():
        step = 64
        for k, (mine, theirs, dst) in enumerate(((g_up, recv_up, own_up), (g_down, recv_down, own_down))):
            pltpu.make_async_copy(theirs, theirs, gr_recv.at[k]).wait()
            for e in range(local):
                def add(r, _, mine=mine, theirs=theirs, e=e):
                    at = pl.ds(pl.multiple_of(r * step, step), step)
                    mine[p, e, at] = (mine[p, e, at].astype(F32) + theirs[e, at].astype(F32)).astype(BF16)
                    return 0
                lax.fori_loop(0, theirs.shape[1] // step, add, 0)
            pltpu.make_async_copy(mine.at[p], dst, gr_loc.at[k]).start()

    def merge_attn():
        pltpu.make_async_copy(chunk_pair, chunk_pair, pr_recv.at[0]).wait()
        for c in range(parts_c):
            chunk_pair[c] = (chunk[p, c].astype(F32) + chunk_pair[c].astype(F32)).astype(BF16)

            def scatter(i, _, c=c):
                r = ne - i
                to = lax.rem(x + r, ne)
                pltpu.make_async_remote_copy(
                    src_ref=chunk_pair.at[c, to], dst_ref=chunk_in.at[c, r], send_sem=ck_send.at[c], recv_sem=ck_recv.at[c],
                    device_id={"expert": to}, device_id_type=MESH).start()
                return 0
            lax.fori_loop(1, ne, scatter, 0)
            chunk_in[c, 0] = chunk_pair[c, x]

    def merge_small():
        pltpu.make_async_copy(small_pair, small_pair, pr_recv.at[1]).wait()
        small_pair[...] = small[p] + small_pair[...]

        def scatter(i, _):
            r = ne - i
            to = lax.rem(x + r, ne)
            pltpu.make_async_remote_copy(
                src_ref=piece(small_pair, to), dst_ref=small_in.at[r], send_sem=ck_send.at[parts_c], recv_sem=ck_recv.at[parts_c],
                device_id={"expert": to}, device_id_type=MESH).start()
            return 0
        lax.fori_loop(1, ne, scatter, 0)
        small_in[0] = small_pair[pl.ds(pl.multiple_of(x * flat_rows, 8), flat_rows)]

    def spread(k, arrived_at, whole, dst):
        part = arrived_at.at[pl.ds(1, ne - 1)]
        pltpu.make_async_copy(part, part, ck_send.at[k]).wait()
        pltpu.make_async_copy(part, part, ck_recv.at[k]).wait()
        acc = arrived_at[0].astype(F32)
        for r in range(1, ne):
            acc = acc + arrived_at[r].astype(F32)
        whole[...] = acc.astype(whole.dtype)
        pltpu.make_async_copy(whole, dst, ag_loc.at[k]).start()

        def one(r, _):
            pltpu.make_async_remote_copy(
                src_ref=whole, dst_ref=dst, send_sem=ag_send.at[k], recv_sem=ag_recv.at[k],
                device_id={"expert": lax.rem(x + ne - r, ne)}, device_id_type=MESH).start()
            return 0
        lax.fori_loop(1, ne, one, 0)

    def spread_attn():
        for c in range(parts_c):
            spread(c, chunk_in.at[c], total.at[c], attn_out.at[x, :, pl.ds(c * part_w, part_w)])

    def spread_small():
        spread(parts_c, small_in, total_small, piece(small_out, x))

    part = send_a.at[1, pl.ds(1, ne - 1)]
    pltpu.make_async_copy(part, part, sa_send.at[1, 1]).wait()
    deliver(hs.at[2], 1)
    g_s[...] = cot[...].astype(F32)

    def keep_grad(l, k, value):
        value = value.astype(BF16)
        for c in range(parts_c):
            chunk[l, c, k * per:(k + 1) * per] = value[:, c * part_w:(c + 1) * part_w].reshape(per, rows, part_w)

        @pl.when(p != l)
        def _():
            at = pl.ds(k * per, per)
            to_partner(chunk.at[l, :, at], chunk_pair.at[:, at], pr_send.at[0], pr_recv.at[0])

    def backward(i, _):
        l = 1 - i
        g = g_s[...]
        hot_e = chosen_of(named(l))
        ep = eprobs[l]
        picked = [jnp.sum(ep * hot_e[kk], -1, keepdims=True) for kk in range(2)]
        inv = picked[0] + picked[1]
        gates = [picked[kk] / inv for kk in range(2)]
        at = lanes_of((seq, LANES), 1)

        @pl.when(l == 0)
        def _():
            dy = jnp.concatenate([(gates[kk] * g).astype(BF16) for kk in range(2)], axis=0)
            send_a[1] = tn(comb[l], dy).astype(BF16).reshape(ne, 2 * CAP, width)
            exchange(1, l)

            @pl.when(p == 1)
            def _():
                merge_attn()
                merge_small()
            parts = split(arrived(1, l))
            for e in range(local):
                x_dy[e] = parts[e]

        @pl.when(l == 1)
        def _():
            await_all(send_g, recv_g, sg_send, sg_recv)
            weigh = jnp.sum(recv_g[...].astype(F32), -1, keepdims=True)
            part = recv_a.at[l, 1, pl.ds(1, ne - 1)]
            pltpu.make_async_copy(part, part, sa_recv.at[l, 1]).wait()
            wide = recv_a[l, 1].astype(F32) * weigh
            for e in range(local):
                x_dy[e] = wide[:, e * CAP:(e + 1) * CAP].reshape(ne * CAP, width).astype(BF16)

        def expert(e, _):
            dy_e = x_dy[e]
            dh = nt(dy_e, w_down[l, e])
            x_du[e] = (dh * u_s[l, e]).astype(BF16)
            return 0
        lax.fori_loop(0, local, expert, 0)
        for c in range(parts_c):
            cols = slice(c * part_w, (c + 1) * part_w)
            send_c[c] = join([nt(x_du[e], w_up[l, e, cols]) for e in range(local)])
            exchange_back(1, l, c)

        @pl.when((p == 1) & (l == 0))
        def _():
            spread_attn()
            spread_small()
            sum_experts()

        gg = jnp.zeros((seq, LANES), F32)
        for kk in range(2):
            part = None
            for c in range(parts_c):
                got = nn(comb[l, kk * seq:(kk + 1) * seq], recv_c[l, 0, c].reshape(slots, part_w))
                term = jnp.sum(g[:, c * part_w:(c + 1) * part_w] * got, -1, keepdims=True)
                part = term if part is None else part + term
            high = part.astype(BF16).astype(F32)
            gg = gg + jnp.where(at == kk, high, 0.0) + jnp.where(at == 2 + kk, part - high, 0.0)
        red_g[l, 0] = gg.astype(BF16)
        reduce_start(red_g.at[l], rd_send.at[l, 1], rd_recv.at[l, 1])

        def expert_grads(e, _):
            g_up[l, e] = tn(x_s[l, e], x_du[e]).astype(BF16)
            g_down[l, e] = tn(hid_s[l, e], x_dy[e]).astype(BF16)
            return 0
        lax.fori_loop(0, local, expert_grads, 0)

        both = comb[l, 0:seq] + comb[l, seq:2 * seq]
        dn2 = summed_back(1, l, lambda back: nn(both, back))

        @pl.when(p != l)
        def _():
            to_partner(g_up.at[l], recv_up, gr_send.at[0], gr_recv.at[0])
            to_partner(g_down.at[l], recv_down, gr_send.at[1], gr_recv.at[1])

        h_mid = h_mid_s[l]
        scale = scale_of(h_mid)
        tail = reduce_end(red_g.at[l], rd_send.at[l, 1], rd_recv.at[l, 1])
        dn2 = dn2()
        gg = [jnp.sum(jnp.where((at == kk) | (at == 2 + kk), tail, 0.0), -1, keepdims=True) for kk in range(2)]
        centre = gg[0] * gates[0] + gg[1] * gates[1]
        dprob = hot_e[0] * ((gg[0] - centre) / inv) + hot_e[1] * ((gg[1] - centre) / inv)
        dlog = (ep * (dprob - jnp.sum(ep * dprob, -1, keepdims=True))).astype(BF16)
        high, low = router_of(l)
        dn2 = dn2 + nn(dlog, high) + nn(dlog, low)
        flat[...] = jnp.zeros_like(flat)
        flat[0:ne * local] = tn(dlog, n_two[l])
        flat[ne * local + 1:ne * local + 2] = jnp.sum(dn2 * h_mid * scale, 0, keepdims=True)
        dg = dn2 * gain_two[l]
        dmid = g + scale * dg - h_mid * (scale * scale * scale) * jnp.mean(h_mid * dg, -1, keepdims=True)
        da = dmid.astype(BF16)
        dmixed = nt(da, w_full[l, z]).astype(BF16)
        q, k, v = qkv[l, 0], qkv[l, 1], qkv[l, 2]
        dq = jnp.zeros((seq, hw), F32)
        dk = jnp.zeros((seq, hw), F32)
        dv = jnp.zeros((seq, hw), F32)
        causal = lanes_of((seq, seq), 0) >= lanes_of((seq, seq), 1)
        row_at = lanes_of((seq, seq), 0)
        top = lanes_of((8, LANES), 0)
        bias_g = jnp.zeros((8, LANES), F32)
        for h in range(heads):
            mask = head_mask(h)
            prob = probs_s[l, h]
            dm = dmixed * mask
            dp = nt(dm, v)
            dv = dv + tn(prob.astype(BF16), dm)
            ds = jnp.where(causal, prob * (dp - jnp.sum(prob * dp, -1, keepdims=True)), 0.0).astype(BF16)
            dq = dq + nn(ds, k * mask)
            dk = dk + tn(ds, q * mask)
            turned = ds.astype(F32)
            bit = 1
            while bit < seq:
                turned = jnp.where((row_at & bit) != 0, pltpu.roll(turned, seq - bit, 1), turned)
                bit *= 2
            bias_g = bias_g + jnp.where(top == h, jnp.sum(turned, 0, keepdims=True), 0.0)
        dqkv[0] = (dq * (hd ** -0.5)).astype(BF16)
        dqkv[1] = (dk * (hd ** -0.5)).astype(BF16)
        dqkv[2] = dv.astype(BF16)
        dn1 = nn(dqkv[0], w_qkv[l, 0]) + nn(dqkv[1], w_qkv[l, 1]) + nn(dqkv[2], w_qkv[l, 2])
        red_a[l, 0] = dn1.astype(BF16)
        reduce_start(red_a.at[l], rd_send.at[l, 0], rd_recv.at[l, 0])
        n1 = n_one[l]
        keep_grad(l, 3, tn(mixed_s[l], da))
        for c in range(3):
            keep_grad(l, c, tn(dqkv[c], n1))

        @pl.when((p == 0) & (l == 0))
        def _():
            merge_attn()
            sum_experts()

        bias_high = bias_g.astype(BF16)
        bias_low = (bias_g - bias_high.astype(F32)).astype(BF16)
        hot_b = hot[...].astype(BF16)
        flat[ne * local + 8:ne * local + 16, 0:hot.shape[1]] = nn(bias_high, hot_b) + nn(bias_low, hot_b)
        h_in = hs[l]
        scale_one = scale_of(h_in)
        dn1 = reduce_end(red_a.at[l], rd_send.at[l, 0], rd_recv.at[l, 0])
        flat[ne * local:ne * local + 1] = jnp.sum(dn1 * h_in * scale_one, 0, keepdims=True)
        for b in range(fold):
            small[l, b * SMALL:(b + 1) * SMALL] = flat[:, b * LANES:(b + 1) * LANES]

        @pl.when(p != l)
        def _():
            to_partner(small.at[l], small_pair, pr_send.at[1], pr_recv.at[1])

        dg = dn1 * gain_one[l]
        dh = dmid + scale_one * dg - h_in * (scale_one * scale_one * scale_one) * jnp.mean(h_in * dg, -1, keepdims=True)
        fin[...] = dh
        g_s[...] = dh.astype(BF16).astype(F32)
        return 0

    lax.fori_loop(0, 2, backward, 0)
    deliver(fin, 0)

    @pl.when(p == 0)
    def _():
        merge_small()
        spread_attn()
        spread_small()

    for k in range(len(weights)):
        lend(k).wait_send()
    for k, ref in enumerate((g_up, g_down)):
        for sem in (gr_loc, gr_send):
            pltpu.make_async_copy(ref.at[0], ref.at[0], sem.at[k]).wait()
    for sem in (sec_loc, sec_send, sec_recv):
        pltpu.make_async_copy(fin, fin, sem).wait()
    for k, pair in enumerate((chunk_pair, small_pair)):
        pltpu.make_async_copy(pair, pair, pr_send.at[k]).wait()
    for k in range(parts_c + 1):
        whole, arrived_at = (total.at[k], chunk_in.at[k]) if k < parts_c else (total_small, small_in)
        pltpu.make_async_copy(whole, whole, ag_loc.at[k]).wait()
        part = arrived_at.at[pl.ds(1, ne - 1)]
        pltpu.make_async_copy(part, part, ag_send.at[k]).wait()
        pltpu.make_async_copy(part, part, ag_recv.at[k]).wait()


def finish(
    local, heads, experts,
    sec, own_up, own_down, attn, small,
    sec_out, qkv_out, out_out, up_out, down_out, router_out, one_out, two_out, bias_out,
    own, whole, attn_v, attn_f, small_v, router_v, one_v, two_v, bias_v, sec_v, sem_own, sem_out, sem_in, sem_small,
):
    pieces = [(k, e) for k in range(2) for e in range(local)]
    sources = (own_up, own_down)
    results = (up_out, down_out)

    def incoming(i):
        k, e = pieces[i]
        return pltpu.make_async_copy(sources[k].at[e], own.at[i], sem_own.at[i])

    def leaving(i):
        k, e = pieces[i]
        return pltpu.make_async_copy(whole.at[i], results[k].at[e], sem_out.at[i])

    last = [pltpu.make_async_copy(attn, attn_v, sem_in.at[0]), pltpu.make_async_copy(small, small_v, sem_in.at[1])]
    for i in range(len(pieces)):
        incoming(i).start()
        if i == 0:
            for copy in last:
                copy.start()
    pass_in = pltpu.make_async_copy(sec, sec_v, sem_in.at[2])
    pass_out = pltpu.make_async_copy(sec_v, sec_out, sem_in.at[3])
    pass_in.start()
    step = 64
    for i in range(len(pieces)):
        incoming(i).wait()

        def convert(r, _, i=i):
            at = pl.ds(pl.multiple_of(r * step, step), step)
            whole[i, at] = own[i, at].astype(F32)
            return 0
        lax.fori_loop(0, own.shape[1] // step, convert, 0)
        leaving(i).start()
    pass_in.wait()
    pass_out.start()
    for copy in last:
        copy.wait()

    def widen(r, _):
        attn_f[r] = attn_v[r].astype(F32)
        return 0
    lax.fori_loop(0, attn_f.shape[0], widen, 0)
    cut = attn_f.shape[0] * 3 // 4
    out = [
        pltpu.make_async_copy(attn_f.at[pl.ds(0, cut)], qkv_out, sem_small.at[0]),
        pltpu.make_async_copy(attn_f.at[pl.ds(cut, attn_f.shape[0] - cut)], out_out, sem_small.at[1]),
    ]
    for b in range(router_v.shape[1] // LANES):
        cols = slice(b * LANES, (b + 1) * LANES)
        at = b * SMALL
        router_v[:, cols] = small_v[at:at + experts]
        one_v[:, cols] = small_v[at + experts:at + experts + 1]
        two_v[:, cols] = small_v[at + experts + 1:at + experts + 2]
    for h in range(heads):
        bias_v[h] = small_v[experts + 8 + h:experts + 9 + h, 0:bias_v.shape[2]]
    out += [
        pltpu.make_async_copy(src, dst, sem_small.at[2 + k])
        for k, (src, dst) in enumerate(((router_v, router_out), (one_v, one_out), (two_v, two_out), (bias_v, bias_out)))
    ]
    for copy in out:
        copy.start()
    for i in range(len(pieces)):
        leaving(i).wait()
    for copy in (*out, pass_out):
        copy.wait()


def body(
    block_input, cotangent, routes, offset_bucket, norm1_gain, qkv_weight, out_weight, bias_table, norm2_gain,
    router_weight, up_weight, down_weight,
):
    ne = lax.axis_size("expert")
    nz = lax.axis_size("tensor")
    micro, seq, width = block_input.shape
    heads, buckets = bias_table.shape[1:]
    local, _, ff = up_weight.shape[1:]
    hw = qkv_weight.shape[3]
    hd = hw // heads
    experts = router_weight.shape[2]
    rows = width // ne
    parts_c = PARTS
    part_w = width // parts_c
    fold = width // LANES
    per = hw // rows
    flat_rows = fold * SMALL // ne
    slots = ne * local * CAP

    any_space = pl.BlockSpec(memory_space=pl.ANY)
    hbm = pl.BlockSpec(memory_space=pltpu.HBM)
    vm = pltpu.VMEM
    dma = pltpu.SemaphoreType.DMA
    sds = jax.ShapeDtypeStruct
    part_w = width // PARTS
    flat = width // LANES * SMALL
    parts_in = (2, 2, PARTS, ne, 2 * CAP, part_w)
    half = (local, width, ff)
    cut = (PARTS, ne, rows, part_w)
    sec, own_up, own_down, attn, small = pl.pallas_call(
        functools.partial(kernel, (ne, nz, seq, width, local, heads, ff, hd)),
        out_shape=[
            sds((micro, seq, width), F32), sds(half, BF16), sds(half, BF16),
            sds((ne, rows, width), BF16), sds((flat, LANES), F32),
        ],
        in_specs=[hbm] * 12,
        out_specs=[any_space] * 5,
        scratch_shapes=[
            vm((seq, width), BF16), vm((seq, width), BF16), vm((1, seq), jnp.int32), vm((seq, buckets), F32),
            vm((2, 2, seq), jnp.int32), vm((2, 1, width), F32), vm((2, 1, width), F32), vm((2, heads, 1, buckets), F32),
            vm((2, experts, width), F32), vm((2, 3, hw, width), BF16),
            vm((2, nz, hw, width), BF16), vm((2, local, width, ff), BF16), vm((2, local, ff, width), BF16),
            vm((3, seq, width), F32), vm((2, seq, width), BF16), vm((2, 3, seq, hw), BF16),
            vm((2, heads, seq, seq), F32), vm((2, seq, hw), BF16), vm((2, seq, width), F32), vm((2, seq, width), BF16),
            vm((2, 2 * seq, slots), BF16), vm((2, seq, experts), F32), vm((2, local, ne * CAP, width), BF16),
            vm((2, local, ne * CAP, ff), F32),
            vm((local, ne * CAP, width), BF16), vm((local, ne * CAP, ff), BF16), vm((2, local, ne * CAP, ff), BF16),
            vm((seq, width), F32), vm((seq, width), F32), vm((3, seq, hw), BF16),
            vm((2, ne, 2 * CAP, width), BF16), vm((2, 2, ne, 2 * CAP, width), BF16), vm((ne, 2 * CAP, LANES), BF16),
            vm((ne, 2 * CAP, LANES), BF16), vm(parts_in[2:], BF16), vm(parts_in, BF16),
            vm((2, nz, seq, hw), BF16), vm((2, nz, seq, width), BF16), vm((2, 2, PARTS, nz, seq, part_w), BF16), vm((2, nz, seq, LANES), BF16),
            vm((2, *half), BF16), vm((2, *half), BF16), vm(half, BF16), vm(half, BF16), vm((2, *cut), BF16), vm(cut, BF16),
            vm(cut, BF16), vm((SMALL, width), F32), vm((2, flat, LANES), F32), vm((flat, LANES), F32),
            vm((ne, flat // ne, LANES), F32), vm((PARTS, rows, part_w), BF16), vm((flat // ne, LANES), F32),
            dma((4,)), dma((9, 2)), dma((9,)), dma, dma((4,)), dma((2,)), dma((2,)), dma((2, 2)), dma((2, 2)), dma, dma, dma((2, 2, PARTS)), dma((2, 2, PARTS)),
            dma((2, 2)), dma((2, 2)), dma((2, 2, PARTS)), dma((2, 2, PARTS)), dma((2,)), dma((2,)), dma((2,)),
            dma((PARTS + 1,)), dma((PARTS + 1,)), dma((2,)), dma((2,)), dma((PARTS + 1,)), dma((PARTS + 1,)), dma((PARTS + 1,)),
            dma, dma, dma,
        ],
        compiler_params=pltpu.CompilerParams(
            collective_id=0, has_side_effects=True, vmem_limit_bytes=VMEM_MB * 1024 * 1024),
        cost_estimate=pl.CostEstimate(flops=20_000_000_000, bytes_accessed=40_000_000, transcendentals=2_000_000),
    )(
        block_input, cotangent, routes[0].transpose(0, 2, 1), offset_bucket[None], norm1_gain, norm2_gain,
        bias_table.transpose(1, 0, 2), router_weight[0].T, qkv_weight[0].transpose(0, 2, 1), out_weight[0],
        up_weight[0], down_weight[0],
    )
    blocks = (2 * local, width, ff)
    sec, qkv_g, out_g, up_g, down_g, router_g, one_g, two_g, bias_g = pl.pallas_call(
        functools.partial(finish, local, heads, experts),
        out_shape=[
            sds((micro, seq, width), F32), sds((ne * 3 // 4, rows, width), F32), sds((ne // 4, rows, width), F32),
            sds(half, F32), sds(half, F32), sds((experts, width), F32), sds((1, width), F32), sds((1, width), F32),
            sds((heads, 1, buckets), F32),
        ],
        in_specs=[hbm] * 5,
        out_specs=[hbm] * 9,
        scratch_shapes=[
            vm(blocks, BF16), vm(blocks, F32), vm((ne, rows, width), BF16), vm((ne, rows, width), F32),
            vm((flat, LANES), F32), vm((experts, width), F32), vm((1, width), F32), vm((1, width), F32),
            vm((heads, 1, buckets), F32), vm((micro, seq, width), F32),
            dma((2 * local,)), dma((2 * local,)), dma((4,)), dma((6,)),
        ],
        compiler_params=pltpu.CompilerParams(vmem_limit_bytes=60 * 1024 * 1024),
        cost_estimate=pl.CostEstimate(flops=3_000_000, bytes_accessed=25_000_000, transcendentals=0),
    )(sec, own_up, own_down, attn, small)
    return (
        sec[None], one_g, qkv_g.reshape(1, 3, hw, width).transpose(0, 1, 3, 2), out_g.reshape(1, hw, width),
        bias_g.transpose(1, 0, 2), two_g, router_g.T[None], up_g[None], down_g[None],
    )


def solution(mesh):
    in_specs = (
        P(None, "expert", None), P(None, "expert", None), P("pipe", None, "expert", None), P(), P("pipe", None),
        P("pipe", None, None, "tensor"), P("pipe", "tensor", None), P("pipe", "tensor", None), P("pipe", None),
        P("pipe", None, None), P("pipe", "expert", None, "tensor"), P("pipe", "expert", "tensor", None),
    )
    out_specs = (
        P("pipe", None, "expert", None), P("pipe", None), P("pipe", None, None, "tensor"), P("pipe", "tensor", None),
        P("pipe", "tensor", None), P("pipe", None), P("pipe", None, None), P("pipe", "expert", None, "tensor"),
        P("pipe", "expert", "tensor", None),
    )
    return jax.shard_map(body, mesh=mesh, in_specs=in_specs, out_specs=out_specs, check_vma=False)
```

```python
import functools

import jax
import jax.numpy as jnp
from jax import lax
from jax.experimental import pallas as pl
from jax.experimental.pallas import tpu as pltpu
from jax.sharding import PartitionSpec as P

EPS = 1e-06
MASKED = -1e30
MESH = pl.DeviceIdType.MESH
F32 = jnp.float32
BF16 = jnp.bfloat16
LANES = 128
CAP = 8
PARTS = 6
CUTS = 6
SMALL = 64
VMEM_MB = 60
TANH_A = 0.7978845608
TANH_B = 0.044715


def dot(a, b, left, right):
    return lax.dot_general(a, b, (((left,), (right,)), ((), ())), preferred_element_type=F32)


def nn(a, b):
    return dot(a, b, 1, 0)


def nt(a, b):
    return dot(a, b, 1, 1)


def tn(a, b):
    return dot(a, b, 0, 0)


def lanes_of(shape, dim):
    return lax.broadcasted_iota(jnp.int32, shape, dim)


def kernel(
    dims,
    x_in, cot_in, routes_in, bucket_in, one_in, two_in, bias_in, router_in, qkv_in, out_in, up_in, down_in,
    sec_out, own_up, own_down, attn_out, small_out,
    xin, cot, bucket, hot, routes, gain_one, gain_two, bias_w, router, w_qkv, w_full, w_up, w_down,
    hs, n_one, qkv, probs_s, mixed_s, h_mid_s, n_two, comb, eprobs, x_s, u_s, x_dy, x_du, hid_s, g_s, fin, dqkv,
    send_a, recv_a, send_g, recv_g, send_c, recv_c, mix, red_a, red_c, red_g, g_up, g_down, recv_up, recv_down, chunk, chunk_pair, chunk_in, flat, small, small_pair,
    small_in, total, total_small,
    sem_in, sem_w, sem_ws, wo_send, wo_recv, mx_send, mx_recv, sa_send, sa_recv, sg_send, sg_recv, sc_send, sc_recv, rd_send, rd_recv, rc_send, rc_recv, gr_send, gr_recv, gr_loc,
    ck_send, ck_recv, pr_send, pr_recv, ag_send, ag_recv, ag_loc, sec_send, sec_recv, sec_loc,
):
    ne, nz, seq, width, local, heads, ff, hd = dims
    p = lax.axis_index("pipe")
    x = lax.axis_index("expert")
    z = lax.axis_index("tensor")
    other = 1 - p
    slots = ne * 2 * CAP
    hw = heads * hd
    rows = width // ne
    parts_c = PARTS
    part_w = width // parts_c
    cut_w = width // CUTS
    fold = width // LANES
    per = hw // rows
    flat_rows = fold * SMALL // ne

    barrier = pltpu.get_barrier_semaphore()

    def hello_e(r, _):
        pl.semaphore_signal(barrier, inc=1, device_id={"expert": lax.rem(x + r, ne)}, device_id_type=MESH)
        return 0

    def hello_z(r, _):
        pl.semaphore_signal(barrier, inc=1, device_id={"tensor": lax.rem(z + r, nz)}, device_id_type=MESH)
        return 0

    lax.fori_loop(1, ne, hello_e, 0)
    lax.fori_loop(1, nz, hello_z, 0)
    pl.semaphore_signal(barrier, inc=1, device_id={"pipe": other}, device_id_type=MESH)

    ins = [
        pltpu.make_async_copy(x_in.at[p], xin, sem_in.at[0]),
        pltpu.make_async_copy(cot_in.at[p], cot, sem_in.at[1]),
        pltpu.make_async_copy(bucket_in, bucket, sem_in.at[2]),
    ]
    for copy in ins:
        copy.start()
    weights = [
        (one_in, gain_one), (qkv_in, w_qkv), (bias_in, bias_w), (w_full, w_full), (routes_in, routes), (router_in, router),
        (two_in, gain_two), (up_in, w_up), (down_in, w_down),
    ]
    def to_partner(src, dst, send, recv):
        pltpu.make_async_remote_copy(
            src_ref=src, dst_ref=dst, send_sem=send, recv_sem=recv, device_id={"pipe": other}, device_id_type=MESH).start()

    def load(k):
        src, dst = weights[k]
        pltpu.make_async_copy(src.at[p] if k == 4 else src, dst.at[p], sem_w.at[k, p]).start()

    def lend(k):
        src, dst = weights[k]
        return pltpu.make_async_remote_copy(
            src_ref=src.at[other] if k == 4 else src.at[p] if k == 3 else src, dst_ref=dst.at[p], send_sem=sem_ws.at[k], recv_sem=sem_w.at[k, p],
            device_id={"pipe": other}, device_id_type=MESH)

    def gather_start():
        pltpu.make_async_copy(out_in, w_full.at[p, z], sem_in.at[3]).start()

        def one(r, _):
            pltpu.make_async_remote_copy(
                src_ref=out_in, dst_ref=w_full.at[p, z], send_sem=wo_send, recv_sem=wo_recv.at[r],
                device_id={"tensor": lax.rem(z + r, nz)}, device_id_type=MESH).start()
            return 0
        lax.fori_loop(1, nz, one, 0)
        to_partner(out_in, w_full.at[p, z], sem_ws.at[3], sem_w.at[3, p])

    def gather_end():
        pltpu.make_async_copy(out_in, w_full.at[p, z], sem_in.at[3]).wait()
        part = w_full.at[p, pl.ds(1, nz - 1)]
        pltpu.make_async_copy(part, part, wo_send).wait()
        for r in range(1, nz):
            got = w_full.at[p, lax.rem(z + nz - r, nz)]
            pltpu.make_async_copy(got, got, wo_recv.at[r]).wait()
            to_partner(got, got, sem_ws.at[3], sem_w.at[3, p])

    load(4)

    @pl.when(p == 0)
    def _():
        for k in (0, 1, 2, 5, 6):
            load(k)
    pl.semaphore_wait(barrier, ne - 1 + nz - 1 + 1)
    lend(4).start()

    @pl.when(p == 0)
    def _():
        gather_start()
        for k in (0, 1, 2, 5, 6, 7, 8):
            lend(k).start()
        for k in (7, 8):
            load(k)

    def await_weight(k, l):
        dst = weights[k][1]
        pltpu.make_async_copy(dst.at[l], dst.at[l], sem_w.at[k, l]).wait()

    def send_all(src, dst, send, recv, forth):
        def one(i, _):
            r = ne - i
            pltpu.make_async_remote_copy(
                src_ref=src.at[r], dst_ref=dst.at[r], send_sem=send, recv_sem=recv,
                device_id={"expert": lax.rem(x + r if forth else x + ne - r, ne)}, device_id_type=MESH).start()
            return 0
        lax.fori_loop(1, ne, one, 0)
        dst[0] = src[0]

    def await_all(src, dst, send, recv):
        part = src.at[pl.ds(1, ne - 1)]
        pltpu.make_async_copy(part, part, send).wait()
        part = dst.at[pl.ds(1, ne - 1)]
        pltpu.make_async_copy(part, part, recv).wait()

    def exchange(kind, l):
        send_all(send_a.at[kind], recv_a.at[l, kind], sa_send.at[l, kind], sa_recv.at[l, kind], True)

    def arrived(kind, l):
        await_all(send_a.at[kind], recv_a.at[l, kind], sa_send.at[l, kind], sa_recv.at[l, kind])
        return recv_a[l, kind]

    def exchange_back(kind, l, c):
        send_all(send_c.at[c], recv_c.at[l, kind, c], sc_send.at[l, kind, c], sc_recv.at[l, kind, c], False)

    def arrived_back(kind, l, c):
        await_all(send_c.at[c], recv_c.at[l, kind, c], sc_send.at[l, kind, c], sc_recv.at[l, kind, c])
        return recv_c[l, kind, c].reshape(slots, part_w)

    def reduce_start(buf, send, recv):
        for r in sorted(range(1, nz), key=lambda r: -min(r, nz - r)):
            pltpu.make_async_remote_copy(
                src_ref=buf.at[0], dst_ref=buf.at[r], send_sem=send, recv_sem=recv,
                device_id={"tensor": lax.rem(z + r, nz)}, device_id_type=MESH).start()

    def reduce_end(buf, send, recv):
        part = buf.at[pl.ds(1, nz - 1)]
        pltpu.make_async_copy(part, part, send).wait()
        pltpu.make_async_copy(part, part, recv).wait()
        acc = None
        for a in range(nz):
            term = buf[lax.rem(z + nz - a, nz)].astype(F32)
            acc = term if acc is None else acc + term
        return acc

    def summed_back(kind, l, weigh):
        for c in range(parts_c):
            red_c[l, kind, c, 0] = weigh(arrived_back(kind, l, c)).astype(BF16)
            reduce_start(red_c.at[l, kind, c], rc_send.at[l, kind, c], rc_recv.at[l, kind, c])
        return lambda: jnp.concatenate(
            [reduce_end(red_c.at[l, kind, c], rc_send.at[l, kind, c], rc_recv.at[l, kind, c]) for c in range(parts_c)], axis=1)

    def split(blocks):
        wide = blocks.astype(F32)
        return [wide[:, e * CAP:(e + 1) * CAP].reshape(ne * CAP, width).astype(BF16) for e in range(local)]

    def join(parts):
        return jnp.concatenate([part.reshape(ne, CAP, part_w) for part in parts], axis=1).astype(BF16)

    def head_mask(h):
        at = lanes_of((1, hw), 1)
        return ((at >= h * hd) & (at < (h + 1) * hd)).astype(BF16)

    def scale_of(h):
        return lax.rsqrt(jnp.mean(h * h, -1, keepdims=True) + EPS)

    def column(row):
        eye = lanes_of((seq, seq), 0) == lanes_of((seq, seq), 1)
        return jnp.sum(jnp.where(eye, row.astype(F32), 0.0), -1, keepdims=True)

    def chosen_of(ids):
        at = lanes_of((seq, ne * local), 1)
        return [(at == e).astype(F32) for e in ids]

    def named(l):
        return [column(routes[l, k:k + 1]).astype(jnp.int32) for k in range(2)]

    def router_of(l):
        r = router[l]
        high = r.astype(BF16)
        return high, (r - high.astype(F32)).astype(BF16)

    def place(l):
        ids = named(l)
        hot_e = chosen_of(ids)
        row_at, col_at = lanes_of((seq, seq), 0), lanes_of((seq, seq), 1)
        earlier = (row_at > col_at).astype(BF16)
        count = nn(earlier, (hot_e[0] + hot_e[1]).astype(BF16))
        for kk in range(2):
            before = count if kk == 0 else count + hot_e[0]
            c = jnp.sum(before * hot_e[kk], -1, keepdims=True).astype(jnp.int32)
            e = ids[kk]
            at = (((e >> 1) - x + ne) & (ne - 1)) * (2 * CAP) + (e & 1) * CAP + c
            comb[l, kk * seq:(kk + 1) * seq] = (lanes_of((seq, slots), 1) == at).astype(F32).astype(BF16)

    def forward(l, _):
        h_in = hs[l]
        await_weight(0, l)
        n1 = (h_in * scale_of(h_in) * gain_one[l]).astype(BF16)
        n_one[l] = n1
        await_weight(1, l)
        for c in range(3):
            qkv[l, c] = nt(n1, w_qkv[l, c]).astype(BF16)
        q, k, v = qkv[l, 0], qkv[l, 1], qkv[l, 2]
        await_weight(2, l)
        causal = lanes_of((seq, seq), 0) >= lanes_of((seq, seq), 1)
        mixed = jnp.zeros((seq, hw), F32)
        for h in range(heads):
            mask = head_mask(h)
            rel = lax.dot_general(
                jnp.broadcast_to(bias_w[l, h], (8, hot.shape[1])), hot[...], (((1,), (1,)), ((), ())),
                precision=lax.Precision.HIGHEST, preferred_element_type=F32)
            bias = pltpu.roll(jnp.broadcast_to(rel[0:1], (seq, seq)), 0, 1, stride=1, stride_axis=0)
            s = nt(q * mask, k) * (hd ** -0.5) + bias
            s = jnp.where(causal, s, MASKED)
            e = jnp.exp(s - jnp.max(s, -1, keepdims=True))
            prob = e / jnp.sum(e, -1, keepdims=True)
            probs_s[l, h] = prob
            mixed = mixed + nn(prob.astype(BF16), v * mask)
        mixed = mixed.astype(BF16)
        mixed_s[l] = mixed
        mix[l, 0] = mixed
        reduce_start(mix.at[l], mx_send.at[l], mx_recv.at[l])

        @pl.when(l == 0)
        def _():
            @pl.when(p == 1)
            def _():
                gather_start()
                for k in (0, 1, 2, 5, 6, 7, 8):
                    lend(k).start()
                    load(k)
            for layer in range(2):
                await_weight(4, layer)
                place(layer)
            send_a[1] = tn(comb[1, 0:seq] + comb[1, seq:2 * seq], cot[...]).astype(BF16).reshape(ne, 2 * CAP, width)
            exchange(1, 1)

        hot_e = chosen_of(named(l))
        both = comb[l, 0:seq] + comb[l, seq:2 * seq]
        await_weight(5, l)
        await_weight(6, l)

        @pl.when((p == 0) & (l == 0))
        def _():
            gather_end()

        @pl.when(l != p)
        def _():
            await_weight(3, l)

        part = mix.at[l, pl.ds(1, nz - 1)]
        pltpu.make_async_copy(part, part, mx_send.at[l]).wait()
        pltpu.make_async_copy(part, part, mx_recv.at[l]).wait()
        attn = None
        for a in range(nz):
            term = nn(mix[l, lax.rem(z + nz - a, nz)], w_full[l, a])
            attn = term if attn is None else attn + term
        h_mid = h_in + attn
        h_mid_s[l] = h_mid
        n2 = (h_mid * scale_of(h_mid) * gain_two[l]).astype(BF16)
        n_two[l] = n2
        send_a[0] = tn(both, n2).astype(BF16).reshape(ne, 2 * CAP, width)
        exchange(0, l)
        high, low = router_of(l)
        logits = nt(n2, high) + nt(n2, low)
        e = jnp.exp(logits - jnp.max(logits, -1, keepdims=True))
        ep = e / jnp.sum(e, -1, keepdims=True)
        eprobs[l] = ep
        picked = [jnp.sum(ep * hot_e[kk], -1, keepdims=True) for kk in range(2)]
        inv = picked[0] + picked[1]
        gates = [picked[kk] / inv for kk in range(2)]

        @pl.when(l == 1)
        def _():
            at = lanes_of((seq, LANES), 1)
            sent = []
            for kk in range(2):
                top = gates[kk].astype(BF16).astype(F32)
                sent.append(jnp.where(at == 0, top, jnp.where(at == 1, gates[kk] - top, 0.0)).astype(BF16))
            send_g[...] = tn(comb[l], jnp.concatenate(sent, axis=0)).astype(BF16).reshape(ne, 2 * CAP, LANES)
            send_all(send_g, recv_g, sg_send, sg_recv, True)

        await_weight(7, l)
        await_weight(8, l)
        parts = split(arrived(0, l))
        for e in range(local):
            x_s[l, e] = parts[e]

        def expert(e, _):
            u = nn(x_s[l, e], w_up[l, e])
            u_s[l, e] = u
            t = jnp.tanh(TANH_A * (u + TANH_B * u * u * u))
            hid_s[l, e] = (0.5 * u * (1.0 + t)).astype(BF16)
            return 0
        lax.fori_loop(0, local, expert, 0)
        for c in range(parts_c):
            cols = slice(c * part_w, (c + 1) * part_w)
            send_c[c] = join([nn(hid_s[l, e], w_down[l, e, :, cols]) for e in range(local)])
            exchange_back(0, l, c)

        @pl.when((p == 1) & (l == 0))
        def _():
            gather_end()

        def slopes(e, _):
            u = u_s[l, e]
            t = jnp.tanh(TANH_A * (u + TANH_B * u * u * u))
            u_s[l, e] = 0.5 * (1.0 + t) + (0.5 * TANH_A) * u * (1.0 - t * t) * (1.0 + (3.0 * TANH_B) * u * u)
            return 0
        lax.fori_loop(0, local, slopes, 0)
        out = summed_back(0, l, lambda back: gates[0] * nn(comb[l, 0:seq], back) + gates[1] * nn(comb[l, seq:2 * seq], back))
        out = h_mid + out()
        hs[l + 1] = jnp.where(l == 0, out.astype(BF16).astype(F32), out)
        return 0

    for copy in ins:
        copy.wait()
    hs[0] = xin[...].astype(F32)
    turn_at, turn_of = lanes_of((seq, seq), 0), lanes_of((seq, seq), 1)
    turned_bucket = jnp.where((turn_at + turn_of == 0) | (turn_at + turn_of == seq), bucket[...].astype(F32), 0.0)
    turned_bucket = jnp.sum(turned_bucket, -1, keepdims=True).astype(jnp.int32)
    hot[...] = (turned_bucket == lanes_of(hot.shape, 1)).astype(F32)
    lax.fori_loop(0, 2, forward, 0)

    def deliver(src, owner):
        @pl.when(p == owner)
        def _():
            pltpu.make_async_copy(src, sec_out.at[p], sec_loc).start()

        @pl.when(p != owner)
        def _():
            pltpu.make_async_remote_copy(
                src_ref=src, dst_ref=sec_out.at[p], send_sem=sec_send, recv_sem=sec_recv,
                device_id={"pipe": other}, device_id_type=MESH).start()

    def piece(ref, j):
        return ref.at[pl.ds(pl.multiple_of(j * flat_rows, 8), flat_rows)]

    def sum_experts():
        step = 64
        for k, (mine, theirs, dst) in enumerate(((g_up, recv_up, own_up), (g_down, recv_down, own_down))):
            pltpu.make_async_copy(theirs, theirs, gr_recv.at[k]).wait()
            for e in range(local):
                def add(r, _, mine=mine, theirs=theirs, e=e):
                    at = pl.ds(pl.multiple_of(r * step, step), step)
                    mine[p, e, at] = (mine[p, e, at].astype(F32) + theirs[e, at].astype(F32)).astype(BF16)
                    return 0
                lax.fori_loop(0, theirs.shape[1] // step, add, 0)
            pltpu.make_async_copy(mine.at[p], dst, gr_loc.at[k]).start()

    def merge_attn():
        pltpu.make_async_copy(chunk_pair, chunk_pair, pr_recv.at[0]).wait()
        for c in range(CUTS):
            chunk_pair[c] = (chunk[p, c].astype(F32) + chunk_pair[c].astype(F32)).astype(BF16)

            def scatter(i, _, c=c):
                r = ne - i
                to = lax.rem(x + r, ne)
                pltpu.make_async_remote_copy(
                    src_ref=chunk_pair.at[c, to], dst_ref=chunk_in.at[c, r], send_sem=ck_send.at[c], recv_sem=ck_recv.at[c],
                    device_id={"expert": to}, device_id_type=MESH).start()
                return 0
            lax.fori_loop(1, ne, scatter, 0)
            chunk_in[c, 0] = chunk_pair[c, x]

    def merge_small():
        pltpu.make_async_copy(small_pair, small_pair, pr_recv.at[1]).wait()
        small_pair[...] = small[p] + small_pair[...]

        def scatter(i, _):
            r = ne - i
            to = lax.rem(x + r, ne)
            pltpu.make_async_remote_copy(
                src_ref=piece(small_pair, to), dst_ref=small_in.at[r], send_sem=ck_send.at[CUTS], recv_sem=ck_recv.at[CUTS],
                device_id={"expert": to}, device_id_type=MESH).start()
            return 0
        lax.fori_loop(1, ne, scatter, 0)
        small_in[0] = small_pair[pl.ds(pl.multiple_of(x * flat_rows, 8), flat_rows)]

    def spread(k, arrived_at, whole, dst):
        part = arrived_at.at[pl.ds(1, ne - 1)]
        pltpu.make_async_copy(part, part, ck_send.at[k]).wait()
        pltpu.make_async_copy(part, part, ck_recv.at[k]).wait()
        acc = arrived_at[0].astype(F32)
        for r in range(1, ne):
            acc = acc + arrived_at[r].astype(F32)
        whole[...] = acc.astype(whole.dtype)
        pltpu.make_async_copy(whole, dst, ag_loc.at[k]).start()

        def one(r, _):
            pltpu.make_async_remote_copy(
                src_ref=whole, dst_ref=dst, send_sem=ag_send.at[k], recv_sem=ag_recv.at[k],
                device_id={"expert": lax.rem(x + ne - r, ne)}, device_id_type=MESH).start()
            return 0
        lax.fori_loop(1, ne, one, 0)

    def spread_attn():
        for c in range(CUTS):
            spread(c, chunk_in.at[c], total.at[c], attn_out.at[x, :, pl.ds(c * cut_w, cut_w)])

    def spread_small():
        spread(CUTS, small_in, total_small, piece(small_out, x))

    part = send_a.at[1, pl.ds(1, ne - 1)]
    pltpu.make_async_copy(part, part, sa_send.at[1, 1]).wait()
    deliver(hs.at[2], 1)
    g_s[...] = cot[...].astype(F32)

    def keep_grad(l, k, value):
        value = value.astype(BF16)
        for c in range(CUTS):
            chunk[l, c, k * per:(k + 1) * per] = value[:, c * cut_w:(c + 1) * cut_w].reshape(per, rows, cut_w)

        @pl.when(p != l)
        def _():
            at = pl.ds(k * per, per)
            to_partner(chunk.at[l, :, at], chunk_pair.at[:, at], pr_send.at[0], pr_recv.at[0])

    def backward(i, _):
        l = 1 - i
        g = g_s[...]
        hot_e = chosen_of(named(l))
        ep = eprobs[l]
        picked = [jnp.sum(ep * hot_e[kk], -1, keepdims=True) for kk in range(2)]
        inv = picked[0] + picked[1]
        gates = [picked[kk] / inv for kk in range(2)]
        at = lanes_of((seq, LANES), 1)

        @pl.when(l == 0)
        def _():
            dy = jnp.concatenate([(gates[kk] * g).astype(BF16) for kk in range(2)], axis=0)
            send_a[1] = tn(comb[l], dy).astype(BF16).reshape(ne, 2 * CAP, width)
            exchange(1, l)

            @pl.when(p == 1)
            def _():
                merge_attn()
                merge_small()
            parts = split(arrived(1, l))
            for e in range(local):
                x_dy[e] = parts[e]

        @pl.when(l == 1)
        def _():
            await_all(send_g, recv_g, sg_send, sg_recv)
            weigh = jnp.sum(recv_g[...].astype(F32), -1, keepdims=True)
            part = recv_a.at[l, 1, pl.ds(1, ne - 1)]
            pltpu.make_async_copy(part, part, sa_recv.at[l, 1]).wait()
            wide = recv_a[l, 1].astype(F32) * weigh
            for e in range(local):
                x_dy[e] = wide[:, e * CAP:(e + 1) * CAP].reshape(ne * CAP, width).astype(BF16)

        def expert(e, _):
            dy_e = x_dy[e]
            dh = nt(dy_e, w_down[l, e])
            x_du[e] = (dh * u_s[l, e]).astype(BF16)
            return 0
        lax.fori_loop(0, local, expert, 0)
        for c in range(parts_c):
            cols = slice(c * part_w, (c + 1) * part_w)
            send_c[c] = join([nt(x_du[e], w_up[l, e, cols]) for e in range(local)])
            exchange_back(1, l, c)

        @pl.when((p == 1) & (l == 0))
        def _():
            spread_attn()
            spread_small()
            sum_experts()

        gg = jnp.zeros((seq, LANES), F32)
        for kk in range(2):
            part = None
            for c in range(parts_c):
                got = nn(comb[l, kk * seq:(kk + 1) * seq], recv_c[l, 0, c].reshape(slots, part_w))
                term = jnp.sum(g[:, c * part_w:(c + 1) * part_w] * got, -1, keepdims=True)
                part = term if part is None else part + term
            high = part.astype(BF16).astype(F32)
            gg = gg + jnp.where(at == kk, high, 0.0) + jnp.where(at == 2 + kk, part - high, 0.0)
        red_g[l, 0] = gg.astype(BF16)
        reduce_start(red_g.at[l], rd_send.at[l, 1], rd_recv.at[l, 1])

        def expert_grads(e, _):
            g_up[l, e] = tn(x_s[l, e], x_du[e]).astype(BF16)
            g_down[l, e] = tn(hid_s[l, e], x_dy[e]).astype(BF16)
            return 0
        lax.fori_loop(0, local, expert_grads, 0)

        both = comb[l, 0:seq] + comb[l, seq:2 * seq]
        dn2 = summed_back(1, l, lambda back: nn(both, back))

        @pl.when(p != l)
        def _():
            to_partner(g_up.at[l], recv_up, gr_send.at[0], gr_recv.at[0])
            to_partner(g_down.at[l], recv_down, gr_send.at[1], gr_recv.at[1])

        h_mid = h_mid_s[l]
        scale = scale_of(h_mid)
        tail = reduce_end(red_g.at[l], rd_send.at[l, 1], rd_recv.at[l, 1])
        dn2 = dn2()
        gg = [jnp.sum(jnp.where((at == kk) | (at == 2 + kk), tail, 0.0), -1, keepdims=True) for kk in range(2)]
        centre = gg[0] * gates[0] + gg[1] * gates[1]
        dprob = hot_e[0] * ((gg[0] - centre) / inv) + hot_e[1] * ((gg[1] - centre) / inv)
        dlog = (ep * (dprob - jnp.sum(ep * dprob, -1, keepdims=True))).astype(BF16)
        high, low = router_of(l)
        dn2 = dn2 + nn(dlog, high) + nn(dlog, low)
        flat[...] = jnp.zeros_like(flat)
        flat[0:ne * local] = tn(dlog, n_two[l])
        flat[ne * local + 1:ne * local + 2] = jnp.sum(dn2 * h_mid * scale, 0, keepdims=True)
        dg = dn2 * gain_two[l]
        dmid = g + scale * dg - h_mid * (scale * scale * scale) * jnp.mean(h_mid * dg, -1, keepdims=True)
        da = dmid.astype(BF16)
        dmixed = nt(da, w_full[l, z]).astype(BF16)
        q, k, v = qkv[l, 0], qkv[l, 1], qkv[l, 2]
        dq = jnp.zeros((seq, hw), F32)
        dk = jnp.zeros((seq, hw), F32)
        dv = jnp.zeros((seq, hw), F32)
        causal = lanes_of((seq, seq), 0) >= lanes_of((seq, seq), 1)
        row_at = lanes_of((seq, seq), 0)
        top = lanes_of((8, LANES), 0)
        bias_g = jnp.zeros((8, LANES), F32)
        for h in range(heads):
            mask = head_mask(h)
            prob = probs_s[l, h]
            dm = dmixed * mask
            dp = nt(dm, v)
            dv = dv + tn(prob.astype(BF16), dm)
            ds = jnp.where(causal, prob * (dp - jnp.sum(prob * dp, -1, keepdims=True)), 0.0).astype(BF16)
            dq = dq + nn(ds, k * mask)
            dk = dk + tn(ds, q * mask)
            turned = ds.astype(F32)
            bit = 1
            while bit < seq:
                turned = jnp.where((row_at & bit) != 0, pltpu.roll(turned, seq - bit, 1), turned)
                bit *= 2
            bias_g = bias_g + jnp.where(top == h, jnp.sum(turned, 0, keepdims=True), 0.0)
        dqkv[0] = (dq * (hd ** -0.5)).astype(BF16)
        dqkv[1] = (dk * (hd ** -0.5)).astype(BF16)
        dqkv[2] = dv.astype(BF16)
        dn1 = nn(dqkv[0], w_qkv[l, 0]) + nn(dqkv[1], w_qkv[l, 1]) + nn(dqkv[2], w_qkv[l, 2])
        red_a[l, 0] = dn1.astype(BF16)
        reduce_start(red_a.at[l], rd_send.at[l, 0], rd_recv.at[l, 0])
        n1 = n_one[l]
        keep_grad(l, 3, tn(mixed_s[l], da))
        for c in range(3):
            keep_grad(l, c, tn(dqkv[c], n1))

        @pl.when((p == 0) & (l == 0))
        def _():
            merge_attn()
            sum_experts()

        bias_high = bias_g.astype(BF16)
        bias_low = (bias_g - bias_high.astype(F32)).astype(BF16)
        hot_b = hot[...].astype(BF16)
        flat[ne * local + 8:ne * local + 16, 0:hot.shape[1]] = nn(bias_high, hot_b) + nn(bias_low, hot_b)
        h_in = hs[l]
        scale_one = scale_of(h_in)
        dn1 = reduce_end(red_a.at[l], rd_send.at[l, 0], rd_recv.at[l, 0])
        flat[ne * local:ne * local + 1] = jnp.sum(dn1 * h_in * scale_one, 0, keepdims=True)
        for b in range(fold):
            small[l, b * SMALL:(b + 1) * SMALL] = flat[:, b * LANES:(b + 1) * LANES]

        @pl.when(p != l)
        def _():
            to_partner(small.at[l], small_pair, pr_send.at[1], pr_recv.at[1])

        dg = dn1 * gain_one[l]
        dh = dmid + scale_one * dg - h_in * (scale_one * scale_one * scale_one) * jnp.mean(h_in * dg, -1, keepdims=True)
        fin[...] = dh
        g_s[...] = dh.astype(BF16).astype(F32)
        return 0

    lax.fori_loop(0, 2, backward, 0)
    deliver(fin, 0)

    @pl.when(p == 0)
    def _():
        merge_small()
        spread_attn()
        spread_small()

    for k in range(len(weights)):
        lend(k).wait_send()
    for k, ref in enumerate((g_up, g_down)):
        for sem in (gr_loc, gr_send):
            pltpu.make_async_copy(ref.at[0], ref.at[0], sem.at[k]).wait()
    for sem in (sec_loc, sec_send, sec_recv):
        pltpu.make_async_copy(fin, fin, sem).wait()
    for k, pair in enumerate((chunk_pair, small_pair)):
        pltpu.make_async_copy(pair, pair, pr_send.at[k]).wait()
    for k in range(CUTS + 1):
        whole, arrived_at = (total.at[k], chunk_in.at[k]) if k < CUTS else (total_small, small_in)
        pltpu.make_async_copy(whole, whole, ag_loc.at[k]).wait()
        part = arrived_at.at[pl.ds(1, ne - 1)]
        pltpu.make_async_copy(part, part, ag_send.at[k]).wait()
        pltpu.make_async_copy(part, part, ag_recv.at[k]).wait()


def finish(
    local, heads, experts,
    sec, own_up, own_down, attn, small,
    sec_out, qkv_out, out_out, up_out, down_out, router_out, one_out, two_out, bias_out,
    own, whole, attn_v, attn_f, small_v, router_v, one_v, two_v, bias_v, sec_v, sem_own, sem_out, sem_in, sem_small,
):
    pieces = [(k, e) for k in range(2) for e in range(local)]
    sources = (own_up, own_down)
    results = (up_out, down_out)

    def incoming(i):
        k, e = pieces[i]
        return pltpu.make_async_copy(sources[k].at[e], own.at[i], sem_own.at[i])

    def leaving(i):
        k, e = pieces[i]
        return pltpu.make_async_copy(whole.at[i], results[k].at[e], sem_out.at[i])

    last = [pltpu.make_async_copy(attn, attn_v, sem_in.at[0]), pltpu.make_async_copy(small, small_v, sem_in.at[1])]
    for i in range(len(pieces)):
        incoming(i).start()
        if i == 0:
            for copy in last:
                copy.start()
    pass_in = pltpu.make_async_copy(sec, sec_v, sem_in.at[2])
    pass_out = pltpu.make_async_copy(sec_v, sec_out, sem_in.at[3])
    pass_in.start()
    step = 64
    for i in range(len(pieces)):
        incoming(i).wait()

        def convert(r, _, i=i):
            at = pl.ds(pl.multiple_of(r * step, step), step)
            whole[i, at] = own[i, at].astype(F32)
            return 0
        lax.fori_loop(0, own.shape[1] // step, convert, 0)
        leaving(i).start()
    pass_in.wait()
    pass_out.start()
    for copy in last:
        copy.wait()

    def widen(r, _):
        attn_f[r] = attn_v[r].astype(F32)
        return 0
    lax.fori_loop(0, attn_f.shape[0], widen, 0)
    cut = attn_f.shape[0] * 3 // 4
    out = [
        pltpu.make_async_copy(attn_f.at[pl.ds(0, cut)], qkv_out, sem_small.at[0]),
        pltpu.make_async_copy(attn_f.at[pl.ds(cut, attn_f.shape[0] - cut)], out_out, sem_small.at[1]),
    ]
    for b in range(router_v.shape[1] // LANES):
        cols = slice(b * LANES, (b + 1) * LANES)
        at = b * SMALL
        router_v[:, cols] = small_v[at:at + experts]
        one_v[:, cols] = small_v[at + experts:at + experts + 1]
        two_v[:, cols] = small_v[at + experts + 1:at + experts + 2]
    for h in range(heads):
        bias_v[h] = small_v[experts + 8 + h:experts + 9 + h, 0:bias_v.shape[2]]
    out += [
        pltpu.make_async_copy(src, dst, sem_small.at[2 + k])
        for k, (src, dst) in enumerate(((router_v, router_out), (one_v, one_out), (two_v, two_out), (bias_v, bias_out)))
    ]
    for copy in out:
        copy.start()
    for i in range(len(pieces)):
        leaving(i).wait()
    for copy in (*out, pass_out):
        copy.wait()


def body(
    block_input, cotangent, routes, offset_bucket, norm1_gain, qkv_weight, out_weight, bias_table, norm2_gain,
    router_weight, up_weight, down_weight,
):
    ne = lax.axis_size("expert")
    nz = lax.axis_size("tensor")
    micro, seq, width = block_input.shape
    heads, buckets = bias_table.shape[1:]
    local, _, ff = up_weight.shape[1:]
    hw = qkv_weight.shape[3]
    hd = hw // heads
    experts = router_weight.shape[2]
    rows = width // ne
    parts_c = PARTS
    part_w = width // parts_c
    cut_w = width // CUTS
    fold = width // LANES
    per = hw // rows
    flat_rows = fold * SMALL // ne
    slots = ne * local * CAP

    any_space = pl.BlockSpec(memory_space=pl.ANY)
    hbm = pl.BlockSpec(memory_space=pltpu.HBM)
    vm = pltpu.VMEM
    dma = pltpu.SemaphoreType.DMA
    sds = jax.ShapeDtypeStruct
    part_w = width // PARTS
    flat = width // LANES * SMALL
    parts_in = (2, 2, PARTS, ne, 2 * CAP, part_w)
    half = (local, width, ff)
    cut = (CUTS, ne, rows, width // CUTS)
    sec, own_up, own_down, attn, small = pl.pallas_call(
        functools.partial(kernel, (ne, nz, seq, width, local, heads, ff, hd)),
        out_shape=[
            sds((micro, seq, width), F32), sds(half, BF16), sds(half, BF16),
            sds((ne, rows, width), BF16), sds((flat, LANES), F32),
        ],
        in_specs=[hbm] * 12,
        out_specs=[any_space] * 5,
        scratch_shapes=[
            vm((seq, width), BF16), vm((seq, width), BF16), vm((1, seq), jnp.int32), vm((seq, buckets), F32),
            vm((2, 2, seq), jnp.int32), vm((2, 1, width), F32), vm((2, 1, width), F32), vm((2, heads, 1, buckets), F32),
            vm((2, experts, width), F32), vm((2, 3, hw, width), BF16),
            vm((2, nz, hw, width), BF16), vm((2, local, width, ff), BF16), vm((2, local, ff, width), BF16),
            vm((3, seq, width), F32), vm((2, seq, width), BF16), vm((2, 3, seq, hw), BF16),
            vm((2, heads, seq, seq), F32), vm((2, seq, hw), BF16), vm((2, seq, width), F32), vm((2, seq, width), BF16),
            vm((2, 2 * seq, slots), BF16), vm((2, seq, experts), F32), vm((2, local, ne * CAP, width), BF16),
            vm((2, local, ne * CAP, ff), F32),
            vm((local, ne * CAP, width), BF16), vm((local, ne * CAP, ff), BF16), vm((2, local, ne * CAP, ff), BF16),
            vm((seq, width), F32), vm((seq, width), F32), vm((3, seq, hw), BF16),
            vm((2, ne, 2 * CAP, width), BF16), vm((2, 2, ne, 2 * CAP, width), BF16), vm((ne, 2 * CAP, LANES), BF16),
            vm((ne, 2 * CAP, LANES), BF16), vm(parts_in[2:], BF16), vm(parts_in, BF16),
            vm((2, nz, seq, hw), BF16), vm((2, nz, seq, width), BF16), vm((2, 2, PARTS, nz, seq, part_w), BF16), vm((2, nz, seq, LANES), BF16),
            vm((2, *half), BF16), vm((2, *half), BF16), vm(half, BF16), vm(half, BF16), vm((2, *cut), BF16), vm(cut, BF16),
            vm(cut, BF16), vm((SMALL, width), F32), vm((2, flat, LANES), F32), vm((flat, LANES), F32),
            vm((ne, flat // ne, LANES), F32), vm((CUTS, rows, width // CUTS), BF16), vm((flat // ne, LANES), F32),
            dma((4,)), dma((9, 2)), dma((9,)), dma, dma((4,)), dma((2,)), dma((2,)), dma((2, 2)), dma((2, 2)), dma, dma, dma((2, 2, PARTS)), dma((2, 2, PARTS)),
            dma((2, 2)), dma((2, 2)), dma((2, 2, PARTS)), dma((2, 2, PARTS)), dma((2,)), dma((2,)), dma((2,)),
            dma((CUTS + 1,)), dma((CUTS + 1,)), dma((2,)), dma((2,)), dma((CUTS + 1,)), dma((CUTS + 1,)), dma((CUTS + 1,)),
            dma, dma, dma,
        ],
        compiler_params=pltpu.CompilerParams(
            collective_id=0, has_side_effects=True, vmem_limit_bytes=VMEM_MB * 1024 * 1024),
        cost_estimate=pl.CostEstimate(flops=20_000_000_000, bytes_accessed=40_000_000, transcendentals=2_000_000),
    )(
        block_input, cotangent, routes[0].transpose(0, 2, 1), offset_bucket[None], norm1_gain, norm2_gain,
        bias_table.transpose(1, 0, 2), router_weight[0].T, qkv_weight[0].transpose(0, 2, 1), out_weight[0],
        up_weight[0], down_weight[0],
    )
    blocks = (2 * local, width, ff)
    sec, qkv_g, out_g, up_g, down_g, router_g, one_g, two_g, bias_g = pl.pallas_call(
        functools.partial(finish, local, heads, experts),
        out_shape=[
            sds((micro, seq, width), F32), sds((ne * 3 // 4, rows, width), F32), sds((ne // 4, rows, width), F32),
            sds(half, F32), sds(half, F32), sds((experts, width), F32), sds((1, width), F32), sds((1, width), F32),
            sds((heads, 1, buckets), F32),
        ],
        in_specs=[hbm] * 5,
        out_specs=[hbm] * 9,
        scratch_shapes=[
            vm(blocks, BF16), vm(blocks, F32), vm((ne, rows, width), BF16), vm((ne, rows, width), F32),
            vm((flat, LANES), F32), vm((experts, width), F32), vm((1, width), F32), vm((1, width), F32),
            vm((heads, 1, buckets), F32), vm((micro, seq, width), F32),
            dma((2 * local,)), dma((2 * local,)), dma((4,)), dma((6,)),
        ],
        compiler_params=pltpu.CompilerParams(vmem_limit_bytes=60 * 1024 * 1024),
        cost_estimate=pl.CostEstimate(flops=3_000_000, bytes_accessed=25_000_000, transcendentals=0),
    )(sec, own_up, own_down, attn, small)
    return (
        sec[None], one_g, qkv_g.reshape(1, 3, hw, width).transpose(0, 1, 3, 2), out_g.reshape(1, hw, width),
        bias_g.transpose(1, 0, 2), two_g, router_g.T[None], up_g[None], down_g[None],
    )


def solution(mesh):
    in_specs = (
        P(None, "expert", None), P(None, "expert", None), P("pipe", None, "expert", None), P(), P("pipe", None),
        P("pipe", None, None, "tensor"), P("pipe", "tensor", None), P("pipe", "tensor", None), P("pipe", None),
        P("pipe", None, None), P("pipe", "expert", None, "tensor"), P("pipe", "expert", "tensor", None),
    )
    out_specs = (
        P("pipe", None, "expert", None), P("pipe", None), P("pipe", None, None, "tensor"), P("pipe", "tensor", None),
        P("pipe", "tensor", None), P("pipe", None), P("pipe", None, None), P("pipe", "expert", None, "tensor"),
        P("pipe", "expert", "tensor", None),
    )
    return jax.shard_map(body, mesh=mesh, in_specs=in_specs, out_specs=out_specs, check_vma=False)
```

```python
import functools

import jax
import jax.numpy as jnp
from jax import lax
from jax.experimental import pallas as pl
from jax.experimental.pallas import tpu as pltpu
from jax.sharding import PartitionSpec as P

EPS = 1e-06
MASKED = -1e30
MESH = pl.DeviceIdType.MESH
F32 = jnp.float32
BF16 = jnp.bfloat16
LANES = 128
CAP = 8
PARTS = 6
CUTS = 6
SMALL = 64
VMEM_MB = 60
TANH_A = 0.7978845608
TANH_B = 0.044715


def dot(a, b, left, right):
    return lax.dot_general(a, b, (((left,), (right,)), ((), ())), preferred_element_type=F32)


def nn(a, b):
    return dot(a, b, 1, 0)


def nt(a, b):
    return dot(a, b, 1, 1)


def tn(a, b):
    return dot(a, b, 0, 0)


def lanes_of(shape, dim):
    return lax.broadcasted_iota(jnp.int32, shape, dim)


def kernel(
    dims,
    x_in, cot_in, routes_in, bucket_in, one_in, two_in, bias_in, router_in, qkv_in, out_in, up_in, down_in,
    sec_out, own_up, own_down, attn_out, small_out,
    xin, cot, bucket, hot, routes, gain_one, gain_two, bias_w, router, w_qkv, w_full, w_up, w_down,
    hs, n_one, qkv, probs_s, mixed_s, h_mid_s, n_two, comb, eprobs, x_s, u_s, x_dy, x_du, hid_s, g_s, fin, dqkv,
    send_a, recv_a, send_g, recv_g, send_c, recv_c, mix, red_a, red_c, red_g, g_up, g_down, recv_up, recv_down, chunk, chunk_pair, chunk_in, flat, small, small_pair,
    small_in, total, total_small,
    sem_in, sem_w, sem_ws, wo_send, wo_recv, mx_send, mx_recv, sa_send, sa_recv, sg_send, sg_recv, sc_send, sc_recv, rd_send, rd_recv, rc_send, rc_recv, gr_send, gr_recv, gr_loc,
    ck_send, ck_recv, pr_send, pr_recv, ag_send, ag_recv, ag_loc, sec_send, sec_recv, sec_loc,
):
    ne, nz, seq, width, local, heads, ff, hd = dims
    p = lax.axis_index("pipe")
    x = lax.axis_index("expert")
    z = lax.axis_index("tensor")
    other = 1 - p
    slots = ne * 2 * CAP
    hw = heads * hd
    rows = width // ne
    parts_c = PARTS
    part_w = width // parts_c
    cut_w = width // CUTS
    fold = width // LANES
    per = hw // rows
    flat_rows = fold * SMALL // ne

    barrier = pltpu.get_barrier_semaphore()

    def hello_e(r, _):
        pl.semaphore_signal(barrier, inc=1, device_id={"expert": lax.rem(x + r, ne)}, device_id_type=MESH)
        return 0

    def hello_z(r, _):
        pl.semaphore_signal(barrier, inc=1, device_id={"tensor": lax.rem(z + r, nz)}, device_id_type=MESH)
        return 0

    lax.fori_loop(1, ne, hello_e, 0)
    lax.fori_loop(1, nz, hello_z, 0)
    pl.semaphore_signal(barrier, inc=1, device_id={"pipe": other}, device_id_type=MESH)

    ins = [
        pltpu.make_async_copy(x_in.at[p], xin, sem_in.at[0]),
        pltpu.make_async_copy(cot_in.at[p], cot, sem_in.at[1]),
        pltpu.make_async_copy(bucket_in, bucket, sem_in.at[2]),
    ]
    for copy in ins:
        copy.start()
    weights = [
        (one_in, gain_one), (qkv_in, w_qkv), (bias_in, bias_w), (w_full, w_full), (routes_in, routes), (router_in, router),
        (two_in, gain_two), (up_in, w_up), (down_in, w_down),
    ]
    def to_partner(src, dst, send, recv):
        pltpu.make_async_remote_copy(
            src_ref=src, dst_ref=dst, send_sem=send, recv_sem=recv, device_id={"pipe": other}, device_id_type=MESH).start()

    def load(k):
        src, dst = weights[k]
        pltpu.make_async_copy(src.at[p] if k == 4 else src, dst.at[p], sem_w.at[k, p]).start()

    def lend(k):
        src, dst = weights[k]
        return pltpu.make_async_remote_copy(
            src_ref=src.at[other] if k == 4 else src.at[p] if k == 3 else src, dst_ref=dst.at[p], send_sem=sem_ws.at[k], recv_sem=sem_w.at[k, p],
            device_id={"pipe": other}, device_id_type=MESH)

    def gather_start():
        pltpu.make_async_copy(out_in, w_full.at[p, z], sem_in.at[3]).start()

        def one(r, _):
            pltpu.make_async_remote_copy(
                src_ref=out_in, dst_ref=w_full.at[p, z], send_sem=wo_send, recv_sem=wo_recv.at[r],
                device_id={"tensor": lax.rem(z + r, nz)}, device_id_type=MESH).start()
            return 0
        lax.fori_loop(1, nz, one, 0)
        to_partner(out_in, w_full.at[p, z], sem_ws.at[3], sem_w.at[3, p])

    def gather_end():
        pltpu.make_async_copy(out_in, w_full.at[p, z], sem_in.at[3]).wait()
        part = w_full.at[p, pl.ds(1, nz - 1)]
        pltpu.make_async_copy(part, part, wo_send).wait()
        for r in range(1, nz):
            got = w_full.at[p, lax.rem(z + nz - r, nz)]
            pltpu.make_async_copy(got, got, wo_recv.at[r]).wait()
            to_partner(got, got, sem_ws.at[3], sem_w.at[3, p])

    load(4)

    @pl.when(p == 0)
    def _():
        for k in (0, 1, 2, 5, 6):
            load(k)
    pl.semaphore_wait(barrier, ne - 1 + nz - 1 + 1)
    lend(4).start()

    @pl.when(p == 0)
    def _():
        for k in (0, 1):
            lend(k).start()
        gather_start()
        for k in (2, 5, 6, 7, 8):
            lend(k).start()
        for k in (7, 8):
            load(k)

    def await_weight(k, l):
        dst = weights[k][1]
        pltpu.make_async_copy(dst.at[l], dst.at[l], sem_w.at[k, l]).wait()

    def send_all(src, dst, send, recv, forth):
        def one(i, _):
            r = ne - i
            pltpu.make_async_remote_copy(
                src_ref=src.at[r], dst_ref=dst.at[r], send_sem=send, recv_sem=recv,
                device_id={"expert": lax.rem(x + r if forth else x + ne - r, ne)}, device_id_type=MESH).start()
            return 0
        lax.fori_loop(1, ne, one, 0)
        dst[0] = src[0]

    def await_all(src, dst, send, recv):
        part = src.at[pl.ds(1, ne - 1)]
        pltpu.make_async_copy(part, part, send).wait()
        part = dst.at[pl.ds(1, ne - 1)]
        pltpu.make_async_copy(part, part, recv).wait()

    def exchange(kind, l):
        send_all(send_a.at[kind], recv_a.at[l, kind], sa_send.at[l, kind], sa_recv.at[l, kind], True)

    def arrived(kind, l):
        await_all(send_a.at[kind], recv_a.at[l, kind], sa_send.at[l, kind], sa_recv.at[l, kind])
        return recv_a[l, kind]

    def exchange_back(kind, l, c):
        send_all(send_c.at[c], recv_c.at[l, kind, c], sc_send.at[l, kind, c], sc_recv.at[l, kind, c], False)

    def arrived_back(kind, l, c):
        await_all(send_c.at[c], recv_c.at[l, kind, c], sc_send.at[l, kind, c], sc_recv.at[l, kind, c])
        return recv_c[l, kind, c].reshape(slots, part_w)

    def reduce_start(buf, send, recv):
        for r in sorted(range(1, nz), key=lambda r: -min(r, nz - r)):
            pltpu.make_async_remote_copy(
                src_ref=buf.at[0], dst_ref=buf.at[r], send_sem=send, recv_sem=recv,
                device_id={"tensor": lax.rem(z + r, nz)}, device_id_type=MESH).start()

    def reduce_end(buf, send, recv):
        part = buf.at[pl.ds(1, nz - 1)]
        pltpu.make_async_copy(part, part, send).wait()
        pltpu.make_async_copy(part, part, recv).wait()
        acc = None
        for a in range(nz):
            term = buf[lax.rem(z + nz - a, nz)].astype(F32)
            acc = term if acc is None else acc + term
        return acc

    def summed_back(kind, l, weigh):
        for c in range(parts_c):
            red_c[l, kind, c, 0] = weigh(arrived_back(kind, l, c)).astype(BF16)
            reduce_start(red_c.at[l, kind, c], rc_send.at[l, kind, c], rc_recv.at[l, kind, c])
        return lambda: jnp.concatenate(
            [reduce_end(red_c.at[l, kind, c], rc_send.at[l, kind, c], rc_recv.at[l, kind, c]) for c in range(parts_c)], axis=1)

    def split(blocks):
        wide = blocks.astype(F32)
        return [wide[:, e * CAP:(e + 1) * CAP].reshape(ne * CAP, width).astype(BF16) for e in range(local)]

    def join(parts):
        return jnp.concatenate([part.reshape(ne, CAP, part_w) for part in parts], axis=1).astype(BF16)

    def head_mask(h):
        at = lanes_of((1, hw), 1)
        return ((at >= h * hd) & (at < (h + 1) * hd)).astype(BF16)

    def scale_of(h):
        return lax.rsqrt(jnp.mean(h * h, -1, keepdims=True) + EPS)

    def column(row):
        eye = lanes_of((seq, seq), 0) == lanes_of((seq, seq), 1)
        return jnp.sum(jnp.where(eye, row.astype(F32), 0.0), -1, keepdims=True)

    def chosen_of(ids):
        at = lanes_of((seq, ne * local), 1)
        return [(at == e).astype(F32) for e in ids]

    def named(l):
        return [column(routes[l, k:k + 1]).astype(jnp.int32) for k in range(2)]

    def router_of(l):
        r = router[l]
        high = r.astype(BF16)
        return high, (r - high.astype(F32)).astype(BF16)

    def place(l):
        ids = named(l)
        hot_e = chosen_of(ids)
        row_at, col_at = lanes_of((seq, seq), 0), lanes_of((seq, seq), 1)
        earlier = (row_at > col_at).astype(BF16)
        count = nn(earlier, (hot_e[0] + hot_e[1]).astype(BF16))
        for kk in range(2):
            before = count if kk == 0 else count + hot_e[0]
            c = jnp.sum(before * hot_e[kk], -1, keepdims=True).astype(jnp.int32)
            e = ids[kk]
            at = (((e >> 1) - x + ne) & (ne - 1)) * (2 * CAP) + (e & 1) * CAP + c
            comb[l, kk * seq:(kk + 1) * seq] = (lanes_of((seq, slots), 1) == at).astype(F32).astype(BF16)

    def forward(l, _):
        h_in = hs[l]
        await_weight(0, l)
        n1 = (h_in * scale_of(h_in) * gain_one[l]).astype(BF16)
        n_one[l] = n1
        await_weight(1, l)
        for c in range(3):
            qkv[l, c] = nt(n1, w_qkv[l, c]).astype(BF16)
        q, k, v = qkv[l, 0], qkv[l, 1], qkv[l, 2]
        await_weight(2, l)
        causal = lanes_of((seq, seq), 0) >= lanes_of((seq, seq), 1)
        mixed = jnp.zeros((seq, hw), F32)
        for h in range(heads):
            mask = head_mask(h)
            rel = lax.dot_general(
                jnp.broadcast_to(bias_w[l, h], (8, hot.shape[1])), hot[...], (((1,), (1,)), ((), ())),
                precision=lax.Precision.HIGHEST, preferred_element_type=F32)
            bias = pltpu.roll(jnp.broadcast_to(rel[0:1], (seq, seq)), 0, 1, stride=1, stride_axis=0)
            s = nt(q * mask, k) * (hd ** -0.5) + bias
            s = jnp.where(causal, s, MASKED)
            e = jnp.exp(s - jnp.max(s, -1, keepdims=True))
            prob = e / jnp.sum(e, -1, keepdims=True)
            probs_s[l, h] = prob
            mixed = mixed + nn(prob.astype(BF16), v * mask)
        mixed = mixed.astype(BF16)
        mixed_s[l] = mixed
        mix[l, 0] = mixed
        reduce_start(mix.at[l], mx_send.at[l], mx_recv.at[l])

        @pl.when(l == 0)
        def _():
            @pl.when(p == 1)
            def _():
                gather_start()
                for k in (0, 1, 2, 5, 6, 7, 8):
                    lend(k).start()
                    load(k)
            for layer in range(2):
                await_weight(4, layer)
                place(layer)
            send_a[1] = tn(comb[1, 0:seq] + comb[1, seq:2 * seq], cot[...]).astype(BF16).reshape(ne, 2 * CAP, width)
            exchange(1, 1)

        hot_e = chosen_of(named(l))
        both = comb[l, 0:seq] + comb[l, seq:2 * seq]
        await_weight(5, l)
        await_weight(6, l)

        @pl.when((p == 0) & (l == 0))
        def _():
            gather_end()

        @pl.when(l != p)
        def _():
            await_weight(3, l)

        part = mix.at[l, pl.ds(1, nz - 1)]
        pltpu.make_async_copy(part, part, mx_send.at[l]).wait()
        pltpu.make_async_copy(part, part, mx_recv.at[l]).wait()
        attn = None
        for a in range(nz):
            term = nn(mix[l, lax.rem(z + nz - a, nz)], w_full[l, a])
            attn = term if attn is None else attn + term
        h_mid = h_in + attn
        h_mid_s[l] = h_mid
        n2 = (h_mid * scale_of(h_mid) * gain_two[l]).astype(BF16)
        n_two[l] = n2
        send_a[0] = tn(both, n2).astype(BF16).reshape(ne, 2 * CAP, width)
        exchange(0, l)
        high, low = router_of(l)
        logits = nt(n2, high) + nt(n2, low)
        e = jnp.exp(logits - jnp.max(logits, -1, keepdims=True))
        ep = e / jnp.sum(e, -1, keepdims=True)
        eprobs[l] = ep
        picked = [jnp.sum(ep * hot_e[kk], -1, keepdims=True) for kk in range(2)]
        inv = picked[0] + picked[1]
        gates = [picked[kk] / inv for kk in range(2)]

        @pl.when(l == 1)
        def _():
            at = lanes_of((seq, LANES), 1)
            sent = []
            for kk in range(2):
                top = gates[kk].astype(BF16).astype(F32)
                sent.append(jnp.where(at == 0, top, jnp.where(at == 1, gates[kk] - top, 0.0)).astype(BF16))
            send_g[...] = tn(comb[l], jnp.concatenate(sent, axis=0)).astype(BF16).reshape(ne, 2 * CAP, LANES)
            send_all(send_g, recv_g, sg_send, sg_recv, True)

        await_weight(7, l)
        await_weight(8, l)
        parts = split(arrived(0, l))
        for e in range(local):
            x_s[l, e] = parts[e]

        def expert(e, _):
            u = nn(x_s[l, e], w_up[l, e])
            u_s[l, e] = u
            t = jnp.tanh(TANH_A * (u + TANH_B * u * u * u))
            hid_s[l, e] = (0.5 * u * (1.0 + t)).astype(BF16)
            return 0
        lax.fori_loop(0, local, expert, 0)
        for c in range(parts_c):
            cols = slice(c * part_w, (c + 1) * part_w)
            send_c[c] = join([nn(hid_s[l, e], w_down[l, e, :, cols]) for e in range(local)])
            exchange_back(0, l, c)

        @pl.when((p == 1) & (l == 0))
        def _():
            gather_end()

        def slopes(e, _):
            u = u_s[l, e]
            t = jnp.tanh(TANH_A * (u + TANH_B * u * u * u))
            u_s[l, e] = 0.5 * (1.0 + t) + (0.5 * TANH_A) * u * (1.0 - t * t) * (1.0 + (3.0 * TANH_B) * u * u)
            return 0
        lax.fori_loop(0, local, slopes, 0)
        out = summed_back(0, l, lambda back: gates[0] * nn(comb[l, 0:seq], back) + gates[1] * nn(comb[l, seq:2 * seq], back))
        out = h_mid + out()
        hs[l + 1] = jnp.where(l == 0, out.astype(BF16).astype(F32), out)
        return 0

    for copy in ins:
        copy.wait()
    hs[0] = xin[...].astype(F32)
    turn_at, turn_of = lanes_of((seq, seq), 0), lanes_of((seq, seq), 1)
    turned_bucket = jnp.where((turn_at + turn_of == 0) | (turn_at + turn_of == seq), bucket[...].astype(F32), 0.0)
    turned_bucket = jnp.sum(turned_bucket, -1, keepdims=True).astype(jnp.int32)
    hot[...] = (turned_bucket == lanes_of(hot.shape, 1)).astype(F32)
    lax.fori_loop(0, 2, forward, 0)

    def deliver(src, owner):
        @pl.when(p == owner)
        def _():
            pltpu.make_async_copy(src, sec_out.at[p], sec_loc).start()

        @pl.when(p != owner)
        def _():
            pltpu.make_async_remote_copy(
                src_ref=src, dst_ref=sec_out.at[p], send_sem=sec_send, recv_sem=sec_recv,
                device_id={"pipe": other}, device_id_type=MESH).start()

    def piece(ref, j):
        return ref.at[pl.ds(pl.multiple_of(j * flat_rows, 8), flat_rows)]

    def sum_experts():
        step = 64
        for k, (mine, theirs, dst) in enumerate(((g_up, recv_up, own_up), (g_down, recv_down, own_down))):
            pltpu.make_async_copy(theirs, theirs, gr_recv.at[k]).wait()
            for e in range(local):
                def add(r, _, mine=mine, theirs=theirs, e=e):
                    at = pl.ds(pl.multiple_of(r * step, step), step)
                    mine[p, e, at] = (mine[p, e, at].astype(F32) + theirs[e, at].astype(F32)).astype(BF16)
                    return 0
                lax.fori_loop(0, theirs.shape[1] // step, add, 0)
            pltpu.make_async_copy(mine.at[p], dst, gr_loc.at[k]).start()

    def merge_attn():
        pltpu.make_async_copy(chunk_pair, chunk_pair, pr_recv.at[0]).wait()
        for c in range(CUTS):
            chunk_pair[c] = (chunk[p, c].astype(F32) + chunk_pair[c].astype(F32)).astype(BF16)

            def scatter(i, _, c=c):
                r = ne - i
                to = lax.rem(x + r, ne)
                pltpu.make_async_remote_copy(
                    src_ref=chunk_pair.at[c, to], dst_ref=chunk_in.at[c, r], send_sem=ck_send.at[c], recv_sem=ck_recv.at[c],
                    device_id={"expert": to}, device_id_type=MESH).start()
                return 0
            lax.fori_loop(1, ne, scatter, 0)
            chunk_in[c, 0] = chunk_pair[c, x]

    def merge_small():
        pltpu.make_async_copy(small_pair, small_pair, pr_recv.at[1]).wait()
        small_pair[...] = small[p] + small_pair[...]

        def scatter(i, _):
            r = ne - i
            to = lax.rem(x + r, ne)
            pltpu.make_async_remote_copy(
                src_ref=piece(small_pair, to), dst_ref=small_in.at[r], send_sem=ck_send.at[CUTS], recv_sem=ck_recv.at[CUTS],
                device_id={"expert": to}, device_id_type=MESH).start()
            return 0
        lax.fori_loop(1, ne, scatter, 0)
        small_in[0] = small_pair[pl.ds(pl.multiple_of(x * flat_rows, 8), flat_rows)]

    def spread(k, arrived_at, whole, dst):
        part = arrived_at.at[pl.ds(1, ne - 1)]
        pltpu.make_async_copy(part, part, ck_send.at[k]).wait()
        pltpu.make_async_copy(part, part, ck_recv.at[k]).wait()
        acc = arrived_at[0].astype(F32)
        for r in range(1, ne):
            acc = acc + arrived_at[r].astype(F32)
        whole[...] = acc.astype(whole.dtype)
        pltpu.make_async_copy(whole, dst, ag_loc.at[k]).start()

        def one(r, _):
            pltpu.make_async_remote_copy(
                src_ref=whole, dst_ref=dst, send_sem=ag_send.at[k], recv_sem=ag_recv.at[k],
                device_id={"expert": lax.rem(x + ne - r, ne)}, device_id_type=MESH).start()
            return 0
        lax.fori_loop(1, ne, one, 0)

    def spread_attn():
        for c in range(CUTS):
            spread(c, chunk_in.at[c], total.at[c], attn_out.at[x, :, pl.ds(c * cut_w, cut_w)])

    def spread_small():
        spread(CUTS, small_in, total_small, piece(small_out, x))

    part = send_a.at[1, pl.ds(1, ne - 1)]
    pltpu.make_async_copy(part, part, sa_send.at[1, 1]).wait()
    deliver(hs.at[2], 1)
    g_s[...] = cot[...].astype(F32)

    def keep_grad(l, k, value):
        value = value.astype(BF16)
        for c in range(CUTS):
            chunk[l, c, k * per:(k + 1) * per] = value[:, c * cut_w:(c + 1) * cut_w].reshape(per, rows, cut_w)

        @pl.when(p != l)
        def _():
            at = pl.ds(k * per, per)
            to_partner(chunk.at[l, :, at], chunk_pair.at[:, at], pr_send.at[0], pr_recv.at[0])

    def backward(i, _):
        l = 1 - i
        g = g_s[...]
        hot_e = chosen_of(named(l))
        ep = eprobs[l]
        picked = [jnp.sum(ep * hot_e[kk], -1, keepdims=True) for kk in range(2)]
        inv = picked[0] + picked[1]
        gates = [picked[kk] / inv for kk in range(2)]
        at = lanes_of((seq, LANES), 1)

        @pl.when(l == 0)
        def _():
            dy = jnp.concatenate([(gates[kk] * g).astype(BF16) for kk in range(2)], axis=0)
            send_a[1] = tn(comb[l], dy).astype(BF16).reshape(ne, 2 * CAP, width)
            exchange(1, l)

            @pl.when(p == 1)
            def _():
                merge_attn()
                merge_small()
            parts = split(arrived(1, l))
            for e in range(local):
                x_dy[e] = parts[e]

        @pl.when(l == 1)
        def _():
            await_all(send_g, recv_g, sg_send, sg_recv)
            weigh = jnp.sum(recv_g[...].astype(F32), -1, keepdims=True)
            part = recv_a.at[l, 1, pl.ds(1, ne - 1)]
            pltpu.make_async_copy(part, part, sa_recv.at[l, 1]).wait()
            wide = recv_a[l, 1].astype(F32) * weigh
            for e in range(local):
                x_dy[e] = wide[:, e * CAP:(e + 1) * CAP].reshape(ne * CAP, width).astype(BF16)

        def expert(e, _):
            dy_e = x_dy[e]
            dh = nt(dy_e, w_down[l, e])
            x_du[e] = (dh * u_s[l, e]).astype(BF16)
            return 0
        lax.fori_loop(0, local, expert, 0)
        for c in range(parts_c):
            cols = slice(c * part_w, (c + 1) * part_w)
            send_c[c] = join([nt(x_du[e], w_up[l, e, cols]) for e in range(local)])
            exchange_back(1, l, c)

        @pl.when((p == 1) & (l == 0))
        def _():
            spread_attn()
            spread_small()
            sum_experts()

        gg = jnp.zeros((seq, LANES), F32)
        for kk in range(2):
            part = None
            for c in range(parts_c):
                got = nn(comb[l, kk * seq:(kk + 1) * seq], recv_c[l, 0, c].reshape(slots, part_w))
                term = jnp.sum(g[:, c * part_w:(c + 1) * part_w] * got, -1, keepdims=True)
                part = term if part is None else part + term
            high = part.astype(BF16).astype(F32)
            gg = gg + jnp.where(at == kk, high, 0.0) + jnp.where(at == 2 + kk, part - high, 0.0)
        red_g[l, 0] = gg.astype(BF16)
        reduce_start(red_g.at[l], rd_send.at[l, 1], rd_recv.at[l, 1])

        def expert_grads(e, _):
            g_up[l, e] = tn(x_s[l, e], x_du[e]).astype(BF16)
            g_down[l, e] = tn(hid_s[l, e], x_dy[e]).astype(BF16)
            return 0
        lax.fori_loop(0, local, expert_grads, 0)

        both = comb[l, 0:seq] + comb[l, seq:2 * seq]
        dn2 = summed_back(1, l, lambda back: nn(both, back))

        @pl.when(p != l)
        def _():
            to_partner(g_up.at[l], recv_up, gr_send.at[0], gr_recv.at[0])
            to_partner(g_down.at[l], recv_down, gr_send.at[1], gr_recv.at[1])

        h_mid = h_mid_s[l]
        scale = scale_of(h_mid)
        tail = reduce_end(red_g.at[l], rd_send.at[l, 1], rd_recv.at[l, 1])
        dn2 = dn2()
        gg = [jnp.sum(jnp.where((at == kk) | (at == 2 + kk), tail, 0.0), -1, keepdims=True) for kk in range(2)]
        centre = gg[0] * gates[0] + gg[1] * gates[1]
        dprob = hot_e[0] * ((gg[0] - centre) / inv) + hot_e[1] * ((gg[1] - centre) / inv)
        dlog = (ep * (dprob - jnp.sum(ep * dprob, -1, keepdims=True))).astype(BF16)
        high, low = router_of(l)
        dn2 = dn2 + nn(dlog, high) + nn(dlog, low)
        flat[...] = jnp.zeros_like(flat)
        flat[0:ne * local] = tn(dlog, n_two[l])
        flat[ne * local + 1:ne * local + 2] = jnp.sum(dn2 * h_mid * scale, 0, keepdims=True)
        dg = dn2 * gain_two[l]
        dmid = g + scale * dg - h_mid * (scale * scale * scale) * jnp.mean(h_mid * dg, -1, keepdims=True)
        da = dmid.astype(BF16)
        dmixed = nt(da, w_full[l, z]).astype(BF16)
        q, k, v = qkv[l, 0], qkv[l, 1], qkv[l, 2]
        dq = jnp.zeros((seq, hw), F32)
        dk = jnp.zeros((seq, hw), F32)
        dv = jnp.zeros((seq, hw), F32)
        causal = lanes_of((seq, seq), 0) >= lanes_of((seq, seq), 1)
        row_at = lanes_of((seq, seq), 0)
        for h in range(heads):
            mask = head_mask(h)
            prob = probs_s[l, h]
            dm = dmixed * mask
            dp = nt(dm, v)
            dv = dv + tn(prob.astype(BF16), dm)
            ds = jnp.where(causal, prob * (dp - jnp.sum(prob * dp, -1, keepdims=True)), 0.0).astype(BF16)
            dq = dq + nn(ds, k * mask)
            dk = dk + tn(ds, q * mask)
            probs_s[l, h] = ds.astype(F32)
        dqkv[0] = (dq * (hd ** -0.5)).astype(BF16)
        dqkv[1] = (dk * (hd ** -0.5)).astype(BF16)
        dqkv[2] = dv.astype(BF16)
        dn1 = nn(dqkv[0], w_qkv[l, 0]) + nn(dqkv[1], w_qkv[l, 1]) + nn(dqkv[2], w_qkv[l, 2])
        red_a[l, 0] = dn1.astype(BF16)
        reduce_start(red_a.at[l], rd_send.at[l, 0], rd_recv.at[l, 0])
        n1 = n_one[l]
        keep_grad(l, 3, tn(mixed_s[l], da))
        for c in range(3):
            keep_grad(l, c, tn(dqkv[c], n1))

        @pl.when((p == 0) & (l == 0))
        def _():
            merge_attn()
            sum_experts()

        top = lanes_of((8, LANES), 0)
        bias_g = jnp.zeros((8, LANES), F32)
        for h in range(heads):
            turned = probs_s[l, h]
            bit = 1
            while bit < seq:
                turned = jnp.where((row_at & bit) != 0, pltpu.roll(turned, seq - bit, 1), turned)
                bit *= 2
            bias_g = bias_g + jnp.where(top == h, jnp.sum(turned, 0, keepdims=True), 0.0)
        bias_high = bias_g.astype(BF16)
        bias_low = (bias_g - bias_high.astype(F32)).astype(BF16)
        hot_b = hot[...].astype(BF16)
        flat[ne * local + 8:ne * local + 16, 0:hot.shape[1]] = nn(bias_high, hot_b) + nn(bias_low, hot_b)
        h_in = hs[l]
        scale_one = scale_of(h_in)
        dn1 = reduce_end(red_a.at[l], rd_send.at[l, 0], rd_recv.at[l, 0])
        flat[ne * local:ne * local + 1] = jnp.sum(dn1 * h_in * scale_one, 0, keepdims=True)
        for b in range(fold):
            small[l, b * SMALL:(b + 1) * SMALL] = flat[:, b * LANES:(b + 1) * LANES]

        @pl.when(p != l)
        def _():
            to_partner(small.at[l], small_pair, pr_send.at[1], pr_recv.at[1])

        dg = dn1 * gain_one[l]
        dh = dmid + scale_one * dg - h_in * (scale_one * scale_one * scale_one) * jnp.mean(h_in * dg, -1, keepdims=True)
        fin[...] = dh
        g_s[...] = dh.astype(BF16).astype(F32)
        return 0

    lax.fori_loop(0, 2, backward, 0)
    deliver(fin, 0)

    @pl.when(p == 0)
    def _():
        merge_small()
        spread_attn()
        spread_small()

    for k in range(len(weights)):
        lend(k).wait_send()
    for k, ref in enumerate((g_up, g_down)):
        for sem in (gr_loc, gr_send):
            pltpu.make_async_copy(ref.at[0], ref.at[0], sem.at[k]).wait()
    for sem in (sec_loc, sec_send, sec_recv):
        pltpu.make_async_copy(fin, fin, sem).wait()
    for k, pair in enumerate((chunk_pair, small_pair)):
        pltpu.make_async_copy(pair, pair, pr_send.at[k]).wait()
    for k in range(CUTS + 1):
        whole, arrived_at = (total.at[k], chunk_in.at[k]) if k < CUTS else (total_small, small_in)
        pltpu.make_async_copy(whole, whole, ag_loc.at[k]).wait()
        part = arrived_at.at[pl.ds(1, ne - 1)]
        pltpu.make_async_copy(part, part, ag_send.at[k]).wait()
        pltpu.make_async_copy(part, part, ag_recv.at[k]).wait()


def finish(
    local, heads, experts,
    sec, own_up, own_down, attn, small,
    sec_out, qkv_out, out_out, up_out, down_out, router_out, one_out, two_out, bias_out,
    own, whole, attn_v, attn_f, small_v, router_v, one_v, two_v, bias_v, sec_v, sem_own, sem_out, sem_in, sem_small,
):
    pieces = [(k, e) for k in range(2) for e in range(local)]
    sources = (own_up, own_down)
    results = (up_out, down_out)

    def incoming(i):
        k, e = pieces[i]
        return pltpu.make_async_copy(sources[k].at[e], own.at[i], sem_own.at[i])

    def leaving(i):
        k, e = pieces[i]
        return pltpu.make_async_copy(whole.at[i], results[k].at[e], sem_out.at[i])

    last = [pltpu.make_async_copy(attn, attn_v, sem_in.at[0]), pltpu.make_async_copy(small, small_v, sem_in.at[1])]
    for i in range(len(pieces)):
        incoming(i).start()
        if i == 0:
            for copy in last:
                copy.start()
    pass_in = pltpu.make_async_copy(sec, sec_v, sem_in.at[2])
    pass_out = pltpu.make_async_copy(sec_v, sec_out, sem_in.at[3])
    pass_in.start()
    step = 64
    for i in range(len(pieces)):
        incoming(i).wait()

        def convert(r, _, i=i):
            at = pl.ds(pl.multiple_of(r * step, step), step)
            whole[i, at] = own[i, at].astype(F32)
            return 0
        lax.fori_loop(0, own.shape[1] // step, convert, 0)
        leaving(i).start()
    pass_in.wait()
    pass_out.start()
    for copy in last:
        copy.wait()

    def widen(r, _):
        attn_f[r] = attn_v[r].astype(F32)
        return 0
    lax.fori_loop(0, attn_f.shape[0], widen, 0)
    cut = attn_f.shape[0] * 3 // 4
    out = [
        pltpu.make_async_copy(attn_f.at[pl.ds(0, cut)], qkv_out, sem_small.at[0]),
        pltpu.make_async_copy(attn_f.at[pl.ds(cut, attn_f.shape[0] - cut)], out_out, sem_small.at[1]),
    ]
    for b in range(router_v.shape[1] // LANES):
        cols = slice(b * LANES, (b + 1) * LANES)
        at = b * SMALL
        router_v[:, cols] = small_v[at:at + experts]
        one_v[:, cols] = small_v[at + experts:at + experts + 1]
        two_v[:, cols] = small_v[at + experts + 1:at + experts + 2]
    for h in range(heads):
        bias_v[h] = small_v[experts + 8 + h:experts + 9 + h, 0:bias_v.shape[2]]
    out += [
        pltpu.make_async_copy(src, dst, sem_small.at[2 + k])
        for k, (src, dst) in enumerate(((router_v, router_out), (one_v, one_out), (two_v, two_out), (bias_v, bias_out)))
    ]
    for copy in out:
        copy.start()
    for i in range(len(pieces)):
        leaving(i).wait()
    for copy in (*out, pass_out):
        copy.wait()


def body(
    block_input, cotangent, routes, offset_bucket, norm1_gain, qkv_weight, out_weight, bias_table, norm2_gain,
    router_weight, up_weight, down_weight,
):
    ne = lax.axis_size("expert")
    nz = lax.axis_size("tensor")
    micro, seq, width = block_input.shape
    heads, buckets = bias_table.shape[1:]
    local, _, ff = up_weight.shape[1:]
    hw = qkv_weight.shape[3]
    hd = hw // heads
    experts = router_weight.shape[2]
    rows = width // ne
    parts_c = PARTS
    part_w = width // parts_c
    cut_w = width // CUTS
    fold = width // LANES
    per = hw // rows
    flat_rows = fold * SMALL // ne
    slots = ne * local * CAP

    any_space = pl.BlockSpec(memory_space=pl.ANY)
    hbm = pl.BlockSpec(memory_space=pltpu.HBM)
    vm = pltpu.VMEM
    dma = pltpu.SemaphoreType.DMA
    sds = jax.ShapeDtypeStruct
    part_w = width // PARTS
    flat = width // LANES * SMALL
    parts_in = (2, 2, PARTS, ne, 2 * CAP, part_w)
    half = (local, width, ff)
    cut = (CUTS, ne, rows, width // CUTS)
    sec, own_up, own_down, attn, small = pl.pallas_call(
        functools.partial(kernel, (ne, nz, seq, width, local, heads, ff, hd)),
        out_shape=[
            sds((micro, seq, width), F32), sds(half, BF16), sds(half, BF16),
            sds((ne, rows, width), BF16), sds((flat, LANES), F32),
        ],
        in_specs=[hbm] * 12,
        out_specs=[any_space] * 5,
        scratch_shapes=[
            vm((seq, width), BF16), vm((seq, width), BF16), vm((1, seq), jnp.int32), vm((seq, buckets), F32),
            vm((2, 2, seq), jnp.int32), vm((2, 1, width), F32), vm((2, 1, width), F32), vm((2, heads, 1, buckets), F32),
            vm((2, experts, width), F32), vm((2, 3, hw, width), BF16),
            vm((2, nz, hw, width), BF16), vm((2, local, width, ff), BF16), vm((2, local, ff, width), BF16),
            vm((3, seq, width), F32), vm((2, seq, width), BF16), vm((2, 3, seq, hw), BF16),
            vm((2, heads, seq, seq), F32), vm((2, seq, hw), BF16), vm((2, seq, width), F32), vm((2, seq, width), BF16),
            vm((2, 2 * seq, slots), BF16), vm((2, seq, experts), F32), vm((2, local, ne * CAP, width), BF16),
            vm((2, local, ne * CAP, ff), F32),
            vm((local, ne * CAP, width), BF16), vm((local, ne * CAP, ff), BF16), vm((2, local, ne * CAP, ff), BF16),
            vm((seq, width), F32), vm((seq, width), F32), vm((3, seq, hw), BF16),
            vm((2, ne, 2 * CAP, width), BF16), vm((2, 2, ne, 2 * CAP, width), BF16), vm((ne, 2 * CAP, LANES), BF16),
            vm((ne, 2 * CAP, LANES), BF16), vm(parts_in[2:], BF16), vm(parts_in, BF16),
            vm((2, nz, seq, hw), BF16), vm((2, nz, seq, width), BF16), vm((2, 2, PARTS, nz, seq, part_w), BF16), vm((2, nz, seq, LANES), BF16),
            vm((2, *half), BF16), vm((2, *half), BF16), vm(half, BF16), vm(half, BF16), vm((2, *cut), BF16), vm(cut, BF16),
            vm(cut, BF16), vm((SMALL, width), F32), vm((2, flat, LANES), F32), vm((flat, LANES), F32),
            vm((ne, flat // ne, LANES), F32), vm((CUTS, rows, width // CUTS), BF16), vm((flat // ne, LANES), F32),
            dma((4,)), dma((9, 2)), dma((9,)), dma, dma((4,)), dma((2,)), dma((2,)), dma((2, 2)), dma((2, 2)), dma, dma, dma((2, 2, PARTS)), dma((2, 2, PARTS)),
            dma((2, 2)), dma((2, 2)), dma((2, 2, PARTS)), dma((2, 2, PARTS)), dma((2,)), dma((2,)), dma((2,)),
            dma((CUTS + 1,)), dma((CUTS + 1,)), dma((2,)), dma((2,)), dma((CUTS + 1,)), dma((CUTS + 1,)), dma((CUTS + 1,)),
            dma, dma, dma,
        ],
        compiler_params=pltpu.CompilerParams(
            collective_id=0, has_side_effects=True, vmem_limit_bytes=VMEM_MB * 1024 * 1024),
        cost_estimate=pl.CostEstimate(flops=20_000_000_000, bytes_accessed=40_000_000, transcendentals=2_000_000),
    )(
        block_input, cotangent, routes[0].transpose(0, 2, 1), offset_bucket[None], norm1_gain, norm2_gain,
        bias_table.transpose(1, 0, 2), router_weight[0].T, qkv_weight[0].transpose(0, 2, 1), out_weight[0],
        up_weight[0], down_weight[0],
    )
    blocks = (2 * local, width, ff)
    sec, qkv_g, out_g, up_g, down_g, router_g, one_g, two_g, bias_g = pl.pallas_call(
        functools.partial(finish, local, heads, experts),
        out_shape=[
            sds((micro, seq, width), F32), sds((ne * 3 // 4, rows, width), F32), sds((ne // 4, rows, width), F32),
            sds(half, F32), sds(half, F32), sds((experts, width), F32), sds((1, width), F32), sds((1, width), F32),
            sds((heads, 1, buckets), F32),
        ],
        in_specs=[hbm] * 5,
        out_specs=[hbm] * 9,
        scratch_shapes=[
            vm(blocks, BF16), vm(blocks, F32), vm((ne, rows, width), BF16), vm((ne, rows, width), F32),
            vm((flat, LANES), F32), vm((experts, width), F32), vm((1, width), F32), vm((1, width), F32),
            vm((heads, 1, buckets), F32), vm((micro, seq, width), F32),
            dma((2 * local,)), dma((2 * local,)), dma((4,)), dma((6,)),
        ],
        compiler_params=pltpu.CompilerParams(vmem_limit_bytes=60 * 1024 * 1024),
        cost_estimate=pl.CostEstimate(flops=3_000_000, bytes_accessed=25_000_000, transcendentals=0),
    )(sec, own_up, own_down, attn, small)
    return (
        sec[None], one_g, qkv_g.reshape(1, 3, hw, width).transpose(0, 1, 3, 2), out_g.reshape(1, hw, width),
        bias_g.transpose(1, 0, 2), two_g, router_g.T[None], up_g[None], down_g[None],
    )


def solution(mesh):
    in_specs = (
        P(None, "expert", None), P(None, "expert", None), P("pipe", None, "expert", None), P(), P("pipe", None),
        P("pipe", None, None, "tensor"), P("pipe", "tensor", None), P("pipe", "tensor", None), P("pipe", None),
        P("pipe", None, None), P("pipe", "expert", None, "tensor"), P("pipe", "expert", "tensor", None),
    )
    out_specs = (
        P("pipe", None, "expert", None), P("pipe", None), P("pipe", None, None, "tensor"), P("pipe", "tensor", None),
        P("pipe", "tensor", None), P("pipe", None), P("pipe", None, None), P("pipe", "expert", None, "tensor"),
        P("pipe", "expert", "tensor", None),
    )
    return jax.shard_map(body, mesh=mesh, in_specs=in_specs, out_specs=out_specs, check_vma=False)
```
